128 devices in a mesh: blk: 8 (over x, z_lo), grp: 16 (over z_hi, y, core).
Axes of the slice: x: 4, y: 4, z: 4 (z_hi: 2, z_lo: 2; z = z_hi * 2 + z_lo), core: 2. Of those that a mesh axis runs over, the one named last changes fastest.
Arguments:
- queries: bfloat16 [65536, 4096], P(('blk', 'grp')), may hold values from -8 to 8
- passages: bfloat16 [16384, 4096], P(('blk', 'grp')), may hold values from -0.75 to 0.75
- positive_ids: int32 [65536], P(('blk', 'grp')), may hold values from 0 to 1023
- hard_ids: int32 [65536, 1], P(('blk', 'grp')), may hold values from 0 to 2047, as said below
Outputs:
- loss: float32 [], replicated
- loss_slope_by_question: bfloat16 [65536, 4096], P(('blk', 'grp'))
- grad_passages: bfloat16 [16384, 4096], P(('blk', 'grp'))
The draws below stay inside these ranges and needn't reach their ends.
Inputs may be any that keep to these rules, and one draw needn't show every extreme that they name: `hard_ids`: of the 512 entries of one device, at most 64 name passages of any one grp index (rows g * 128 to g * 128 + 127 of the pool); in every batch shard one grp index receives exactly 64 from each device of the shard.
All inputs are finite; a program needn't handle non-finite values.
Results may differ from the reference program's by a relative error of at most 0.017.
Values may be sent and summed in bfloat16 or wider, within the bound.
A program may use at most 192 MiB of HBM per device.

```python
import math
import jax
import jax.numpy as jnp
from jax import lax

D = 4096
Q_DEV = 512
P_DEV = 128
HARD = 1
BLOCKS = 8
GROUPS = 16
LOOP = 1024
POOL = 2048
CAP = 64
Q_TOTAL = 65536
P_TOTAL = 16384


def shared_passages(key):
    values = jax.random.truncated_normal(key, -6.0, 6.0, (P_TOTAL, D), jnp.float32)
    return values / math.sqrt(D)


def positive_table(key):
    key = jax.random.fold_in(key, 31)
    return jax.random.randint(key, (Q_TOTAL,), 0, LOOP).astype(jnp.int32)


def hard_table(key):
    key = jax.random.fold_in(key, 21)
    seat_total_number = Q_DEV * HARD
    seat_count = GROUPS * CAP
    device_count = Q_TOTAL // Q_DEV

    def one_device(device):
        shard_key = jax.random.fold_in(key, 100000 + device // GROUPS)
        favored = jax.random.randint(jax.random.fold_in(shard_key, 1), (), 0, GROUPS)
        owner_bias = jax.random.randint(jax.random.fold_in(shard_key, 2), (GROUPS,), 0, 4)
        device_key = jax.random.fold_in(key, device)
        noise_key, order_key, local_key = jax.random.split(device_key, 3)
        seat_owner = jnp.arange(seat_count, dtype=jnp.int32) // CAP
        noise = jax.random.randint(noise_key, (seat_count,), 0, 4096)
        score = noise + owner_bias[seat_owner] * 2048 + jnp.where(seat_owner == favored, 16384, 0)
        keyed = score * seat_count + jnp.arange(seat_count, dtype=jnp.int32)
        ignored, chosen = lax.top_k(keyed, seat_total_number)
        chosen = jax.random.permutation(order_key, chosen)
        local_rows = jax.random.randint(local_key, (seat_total_number,), 0, P_DEV)
        ident = chosen // CAP * P_DEV + local_rows
        return ident.astype(jnp.int32).reshape(Q_DEV, HARD)
    return jax.vmap(one_device)(jnp.arange(device_count, dtype=jnp.int32)).reshape(Q_TOTAL, HARD)


def draw_passages(key, part):
    shared = shared_passages(key)
    return shared.astype(jnp.bfloat16)


def draw_positive_ids(key, part):
    positive = positive_table(key)
    return positive


def draw_hard_ids(key, part):
    hard = hard_table(key)
    return hard


def draw_queries(key, part):
    shared = shared_passages(key)
    positive = positive_table(key)
    hard = hard_table(key)
    key = jax.random.fold_in(key, 12)
    first_key = jax.random.fold_in(key, 0)
    third_key = jax.random.fold_in(key, 2)
    fourth_key = jax.random.fold_in(key, 3)
    device_count = Q_TOTAL // Q_DEV
    owner = jnp.arange(Q_TOTAL, dtype=jnp.int32) // Q_DEV
    fraction = (owner.astype(jnp.float32) / float(max(device_count - 1, 1)))[:, None, None]
    loop_row = (positive // P_DEV * GROUPS + owner % GROUPS) * P_DEV + positive % P_DEV
    pool_row = (owner // GROUPS)[:, None] * POOL + hard
    pull_positive = jax.random.uniform(third_key, (Q_TOTAL, 1), jnp.float32, 0.25, 0.4)
    jitter = jax.random.uniform(fourth_key, (Q_TOTAL, HARD, 1), jnp.float32, 0.85, 1.15)
    pull_hard = (0.1 + 0.5 * fraction) * jitter
    toward = pull_positive * jnp.take(shared, loop_row, axis=0) + jnp.sum(pull_hard * jnp.take(shared, pool_row, axis=0), 1)
    values = jax.random.truncated_normal(first_key, -6.0, 6.0, (Q_TOTAL, D), jnp.float32) / math.sqrt(D) + toward
    values = jnp.clip(values, -8.0, 8.0)
    return values.astype(jnp.bfloat16)


def setup_inputs(seed: int = 0) -> dict:
    seeds = jax.random.split(jax.random.key(seed), 5)
    return {
        "queries": draw_queries(jax.random.fold_in(seeds[4], 71), 0),
        "passages": draw_passages(jax.random.fold_in(seeds[4], 71), 0),
        "positive_ids": draw_positive_ids(jax.random.fold_in(seeds[4], 71), 0),
        "hard_ids": draw_hard_ids(jax.random.fold_in(seeds[4], 71), 0),
    }


logit_scaling_coefficient = 20.0


def pick_rows(table, index_rows):
    return table[index_rows]


def increment_entries(summed_total_so_far, index_rows, values):
    return summed_total_so_far.at[index_rows.reshape(-1)].add(values.reshape(-1, D).astype(jnp.float32))


def reference(queries, passages, positive_ids, hard_ids):
    query_grid = queries.reshape(BLOCKS, GROUPS, Q_DEV, D).transpose(1, 0, 2, 3)
    passage_grid = passages.reshape(BLOCKS, GROUPS, P_DEV, D)
    pool_table = passage_grid.reshape(BLOCKS, POOL, D)
    loop_table = passage_grid.transpose(1, 0, 2, 3).reshape(GROUPS, LOOP, D)
    positive_grid = positive_ids.reshape(BLOCKS, GROUPS, Q_DEV).transpose(1, 0, 2)
    hard_grid = hard_ids.reshape(BLOCKS, GROUPS, Q_DEV, HARD).transpose(1, 0, 2, 3)

    def scan_step(summed_total_so_far, inputs):
        query_block, loop_block, positive_block, tough_candidate_tile = inputs
        asker_embedding_store = query_block.astype(jnp.float32)
        minibatch_document_table = loop_block.astype(jnp.float32)
        hard_rows = jax.vmap(pick_rows)(pool_table, tough_candidate_tile)
        difficult_distractor_table = hard_rows.astype(jnp.float32)
        affinity_scores_raw = logit_scaling_coefficient * jnp.einsum("aet,ot->aeo", asker_embedding_store, minibatch_document_table)
        difficult_distractor_scores_raw = logit_scaling_coefficient * jnp.einsum("yli,ylpi->ylp", asker_embedding_store, difficult_distractor_table)
        top_score = jnp.maximum(jnp.max(affinity_scores_raw, -1), jnp.max(difficult_distractor_scores_raw, -1))
        total = jnp.sum(jnp.exp(affinity_scores_raw - top_score[..., None]), -1) + jnp.sum(jnp.exp(difficult_distractor_scores_raw - top_score[..., None]), -1)
        log_total = top_score + jnp.log(total)
        positive_mask = positive_block[..., None] == jnp.arange(LOOP, dtype=jnp.int32)
        positive_logit = jnp.sum(jnp.where(positive_mask, affinity_scores_raw, jnp.float32(0.0)), -1)
        loss_sum = jnp.sum(log_total - positive_logit)
        minibatch_normalized_probability = (jnp.exp(affinity_scores_raw - log_total[..., None]) - positive_mask.astype(jnp.float32)).astype(jnp.bfloat16)
        tough_candidate_likelihood = jnp.exp(difficult_distractor_scores_raw - log_total[..., None]).astype(jnp.bfloat16)
        minibatch_normalized_probability = lax.optimization_barrier(minibatch_normalized_probability).astype(jnp.float32)
        tough_candidate_likelihood = lax.optimization_barrier(tough_candidate_likelihood).astype(jnp.float32)
        question_slope_lines = logit_scaling_coefficient * (jnp.einsum("ryj,jz->ryz", minibatch_normalized_probability, minibatch_document_table) + jnp.einsum("ztn,ztnr->ztr", tough_candidate_likelihood, difficult_distractor_table))
        cumulative_question_slope = (logit_scaling_coefficient * jnp.einsum("lrc,lrw->lcw", minibatch_normalized_probability, asker_embedding_store)).astype(jnp.bfloat16)
        cumulative_question_slope = lax.optimization_barrier(cumulative_question_slope).astype(jnp.float32)
        loop_grad = jnp.sum(cumulative_question_slope, 0)
        location_offsets = (logit_scaling_coefficient * tough_candidate_likelihood[..., None] * asker_embedding_store[:, :, None, :]).astype(jnp.bfloat16)
        location_offsets = lax.optimization_barrier(location_offsets)
        summed_total_so_far = jax.vmap(increment_entries)(summed_total_so_far, tough_candidate_tile, location_offsets)
        return summed_total_so_far, (question_slope_lines.astype(jnp.bfloat16), loop_grad, loss_sum)

    initial = jnp.zeros((BLOCKS, POOL, D), jnp.float32)
    hard_total, (query_grads, loop_grads, loss_sums) = lax.scan(scan_step, initial, (query_grid, loop_table, positive_grid, hard_grid))
    loss_slope_by_question = query_grads.transpose(1, 0, 2, 3).reshape(Q_TOTAL, D)
    loop_sum = loop_grads.reshape(GROUPS, BLOCKS, P_DEV, D).transpose(1, 0, 2, 3)
    grad_passages = (loop_sum + hard_total.reshape(BLOCKS, GROUPS, P_DEV, D)).astype(jnp.bfloat16).reshape(P_TOTAL, D)
    loss = jnp.sum(loss_sums) / Q_TOTAL
    return loss, loss_slope_by_question, grad_passages
```

```python
import functools

import jax
import jax.numpy as jnp
from jax import lax
from jax.experimental import pallas as pl
from jax.experimental.pallas import tpu as pltpu
from jax.sharding import PartitionSpec as P

logit_scaling_coefficient = 20.0
MESH = pl.DeviceIdType.MESH
BF16 = jnp.bfloat16
F32 = jnp.float32
COPIES = 80
NT = (((1,), (1,)), ((), ()))


def rows(start, size, multiple=64):
    return pl.ds(pl.multiple_of(start, multiple), size)


def kernel(
    q_hbm, p_hbm, pos_ref, hid_ref,
    loss_ref, dq_hbm, dp_hbm, other_hbm,
    lbuf, pbuf, qbuf, s, wt, wall, wht, xs, ys, xrf, xrs, yrf, yrs, zrh, zrl,
    ids, hs, hin, w2, top, lsum, lsend, lrecv, otile, dqt,
    ssem, rsem, csem,
):
    q_dev, width = q_hbm.shape
    p_dev = p_hbm.shape[0]
    half = p_dev // 2
    scale = logit_scaling_coefficient

    b = lax.axis_index("blk")
    g = lax.axis_index("grp")
    x, zl = lax.div(b, 2), lax.rem(b, 2)
    zh, y, core = lax.div(g, 8), lax.div(lax.rem(g, 8), 2), lax.rem(g, 2)
    pb = x * 2 + 1 - zl
    px = [lax.rem(x + k, 4) for k in range(4)]
    py = [lax.rem(y + k, 4) for k in range(4)]
    xp = (px[1] * 2 + zl, g)
    xm = (px[3] * 2 + zl, g)
    yp = (b, zh * 8 + py[1] * 2 + core)
    ym = (b, zh * 8 + py[3] * 2 + core)
    p1 = (pb, g)
    p2 = (pb, lax.rem(g + 8, 16))
    sib = (b, zh * 8 + y * 2 + 1 - core)

    number = {}
    started = {}

    def describe(name, src, dst, peer):
        k = number.setdefault(name, len(number))
        return pltpu.make_async_remote_copy(
            src_ref=src, dst_ref=dst, send_sem=ssem.at[k], recv_sem=rsem.at[k],
            device_id=peer, device_id_type=MESH,
        )

    def send(name, src, dst, peer):
        copy = describe(name, src, dst, peer)
        copy.start()
        started[name] = copy

    def sent(name):
        started.pop(name).wait_send()

    def arrived(name, dst):
        describe(name, dst, dst, sib).wait_recv()

    barrier = pltpu.get_barrier_semaphore()
    for peer in (xp, xm, yp, ym, p1, p2, sib):
        pl.semaphore_signal(barrier, inc=1, device_id=peer, device_id_type=MESH)
    pl.semaphore_wait(barrier, 7)

    def lrow(xx, zz, h=0, n=p_dev):
        return lbuf.at[rows((xx * 2 + zz) * p_dev + h * half, n)]

    def prow(yy, zz, h=0, n=p_dev):
        return pbuf.at[rows((yy * 2 + zz) * p_dev + h * half, n)]

    def orow(yy, zz):
        return other_hbm.at[rows((yy * 2 + zz) * p_dev, p_dev)]

    own = [p_hbm.at[pl.ds(h * half, half)] for h in range(2)]

    for h in range(2):
        send(f"z{h}", own[h], lrow(x, zl, h, half), p1)
    for h in range(2):
        send(f"x+o{h}", own[h], lrow(x, zl, h, half), xp)
        send(f"x-o{1 - h}", own[1 - h], lrow(x, zl, 1 - h, half), xm)
        send(f"y+o{h}", own[h], prow(y, zh, h, half), yp)
        send(f"y-o{1 - h}", own[1 - h], prow(y, zh, 1 - h, half), ym)
    local = [
        pltpu.make_async_copy(q_hbm, qbuf.at[pl.ds(0, q_dev)], csem.at[0]),
        pltpu.make_async_copy(p_hbm, lrow(x, zl), csem.at[1]),
        pltpu.make_async_copy(p_hbm, prow(y, zh), csem.at[2]),
    ]
    for copy in local:
        copy.start()
    ids[0] = jnp.broadcast_to(hid_ref[...], ids.shape[1:])
    send("ids", ids.at[0], ids.at[1], sib)
    send("q", q_hbm, qbuf.at[pl.ds(q_dev, q_dev)], sib)
    send("oo", p_hbm, orow(y, zh), sib)

    hs[...] = jnp.zeros(hs.shape, F32)
    top[...] = jnp.full(top.shape, -jnp.inf, F32)

    def score_loop(xx, zz):
        c = xx * 2 + zz

        @pl.loop(0, q_dev // 256)
        def _(n):
            cols = rows(n * 256, 256, 256)
            acc = scale * lax.dot_general(
                lbuf[rows(c * p_dev, p_dev), :], qbuf[cols, :], NT, preferred_element_type=F32
            )
            s[:, rows(c * q_dev + n * 256, 256, 256)] = acc
            top[:, cols] = jnp.maximum(top[:, cols], jnp.max(acc, axis=0, keepdims=True))

    def pool_base(yy, zz, cc):
        return (zz * 8 + yy * 2 + cc) * p_dev

    def score_pool(yy, zz):
        slot = yy * 2 + zz
        base = pool_base(yy, zz, core)
        for k in range(2):

            @pl.loop(0, q_dev // 256)
            def _(n):
                cols = rows(n * 256, 256, 256)
                acc = lax.dot_general(
                    pbuf[rows(slot * p_dev, p_dev), :],
                    qbuf[rows(k * q_dev + n * 256, 256, 256), :],
                    NT,
                    preferred_element_type=F32,
                )
                row = lax.broadcasted_iota(jnp.int32, acc.shape, 0) + base
                named = jnp.where(row == ids[k, 0:1, cols], scale * acc, 0.0)
                hs[k, :, cols] += jnp.sum(named, axis=0, keepdims=True)

    oz, oh = 1 - zl, 1 - zh

    for copy in local:
        copy.wait()
    score_loop(x, zl)

    arrived("x+o0", lrow(px[3], zl, 0, half))
    send("x+f", lrow(px[3], zl, 0, half), lrow(px[3], zl, 0, half), xp)
    arrived("x-o1", lrow(px[1], zl, 1, half))
    send("x-f", lrow(px[1], zl, 1, half), lrow(px[1], zl, 1, half), xm)
    arrived("y+o0", prow(py[3], zh, 0, half))
    send("y+f", prow(py[3], zh, 0, half), prow(py[3], zh, 0, half), yp)
    arrived("y-o1", prow(py[1], zh, 1, half))
    send("y-f", prow(py[1], zh, 1, half), prow(py[1], zh, 1, half), ym)
    arrived("z0", lrow(x, oz, 0, half))
    send("h0", lrow(x, oz, 0, half), prow(y, zh, 0, half), p2)
    send("x+p0", lrow(x, oz, 0, half), lrow(x, oz, 0, half), xp)
    arrived("ids", ids.at[1])
    arrived("q", qbuf.at[pl.ds(q_dev, q_dev)])
    score_pool(y, zh)

    arrived("z1", lrow(x, oz, 1, half))
    send("h1", lrow(x, oz, 1, half), prow(y, zh, 1, half), p2)
    send("x-p1", lrow(x, oz, 1, half), lrow(x, oz, 1, half), xm)
    send("x+p1", lrow(x, oz, 1, half), lrow(x, oz, 1, half), xp)
    send("x-p0", lrow(x, oz, 0, half), lrow(x, oz, 0, half), xm)
    arrived("h0", prow(y, oh, 0, half))
    send("y+p0", prow(y, oh, 0, half), prow(y, oh, 0, half), yp)
    score_loop(x, oz)
    arrived("x+o1", lrow(px[3], zl, 1, half))
    score_loop(px[3], zl)
    arrived("x-o0", lrow(px[1], zl, 0, half))
    score_loop(px[1], zl)
    arrived("y+o1", prow(py[3], zh, 1, half))
    send("o3", prow(py[3], zh), orow(py[3], zh), sib)
    score_pool(py[3], zh)
    arrived("y-o0", prow(py[1], zh, 0, half))
    send("o1", prow(py[1], zh), orow(py[1], zh), sib)
    arrived("h1", prow(y, oh, 1, half))
    send("y-p1", prow(y, oh, 1, half), prow(y, oh, 1, half), ym)
    send("y+p1", prow(y, oh, 1, half), prow(y, oh, 1, half), yp)
    send("y-p0", prow(y, oh, 0, half), prow(y, oh, 0, half), ym)
    send("op", prow(y, oh), orow(y, oh), sib)
    score_pool(py[1], zh)
    arrived("x+f", lrow(px[2], zl, 0, half))
    arrived("x-f", lrow(px[2], zl, 1, half))
    score_loop(px[2], zl)
    arrived("y+f", prow(py[2], zh, 0, half))
    arrived("y-f", prow(py[2], zh, 1, half))
    send("o2", prow(py[2], zh), orow(py[2], zh), sib)
    arrived("x+p0", lrow(px[3], oz, 0, half))
    send("x+g", lrow(px[3], oz, 0, half), lrow(px[3], oz, 0, half), xp)
    arrived("x-p1", lrow(px[1], oz, 1, half))
    send("x-g", lrow(px[1], oz, 1, half), lrow(px[1], oz, 1, half), xm)
    arrived("y+p0", prow(py[3], oh, 0, half))
    send("y+g", prow(py[3], oh, 0, half), prow(py[3], oh, 0, half), yp)
    arrived("y-p1", prow(py[1], oh, 1, half))
    send("y-g", prow(py[1], oh, 1, half), prow(py[1], oh, 1, half), ym)
    score_pool(y, oh)
    score_pool(py[2], zh)
    arrived("x+p1", lrow(px[3], oz, 1, half))
    score_loop(px[3], oz)
    arrived("x-p0", lrow(px[1], oz, 0, half))
    score_loop(px[1], oz)
    arrived("y+p1", prow(py[3], oh, 1, half))
    score_pool(py[3], oh)
    arrived("y-p0", prow(py[1], oh, 0, half))
    score_pool(py[1], oh)
    arrived("y+g", prow(py[2], oh, 0, half))
    arrived("y-g", prow(py[2], oh, 1, half))
    score_pool(py[2], oh)
    send("hs", hs.at[1], hin, sib)
    arrived("x+g", lrow(px[2], oz, 0, half))
    arrived("x-g", lrow(px[2], oz, 1, half))
    score_loop(px[2], oz)

    arrived("hs", hin)
    hard = hs[0] + hin[...]
    hard = hard[0:1]
    peak = jnp.maximum(top[0:1], hard)
    total = jnp.exp(hard - peak)
    positive = jnp.zeros_like(peak)
    blocks = s.shape[1] // q_dev
    for c in range(blocks):
        part = s[:, c * q_dev:(c + 1) * q_dev]
        total += jnp.sum(jnp.exp(part - peak), axis=0, keepdims=True)
        row = lax.broadcasted_iota(jnp.int32, part.shape, 0) + c * p_dev
        positive += jnp.sum(jnp.where(row == pos_ref[...], part, 0.0), axis=0, keepdims=True)
    log_total = peak + jnp.log(total)
    w_hard = jnp.exp(hard - log_total).astype(BF16).astype(F32)
    w2[0] = jnp.broadcast_to(w_hard, w2.shape[1:])
    send("w", w2.at[0], w2.at[1], sib)
    for c in range(blocks):
        part = s[:, c * q_dev:(c + 1) * q_dev]
        row = lax.broadcasted_iota(jnp.int32, part.shape, 0) + c * p_dev
        hit = jnp.where(row == pos_ref[...], 1.0, 0.0)
        wt[c * p_dev:(c + 1) * p_dev, :] = (jnp.exp(part - log_total) - hit).astype(BF16)
    lsum[...] = jnp.broadcast_to(
        jnp.sum(log_total - positive, axis=1, keepdims=True), lsum.shape
    )

    x_pair = [
        (lax.rem(b + 2 + 4 * lax.rem(x, 2), 8), g),
        ((3 - x) * 2 + zl, g),
    ]
    y_pair = [
        (b, zh * 8 + lax.rem(y + 1 + 2 * lax.rem(y, 2), 4) * 2 + core),
        (b, zh * 8 + (3 - y) * 2 + core),
    ]
    loss_peers = [x_pair[0], y_pair[0], x_pair[1], y_pair[1], p1, p2, sib]

    def loss_start(k):
        lsend[k] = lsum[...]
        send(f"l{k}", lsend.at[k], lrecv.at[k], loss_peers[k])

    def loss_finish(k):
        arrived(f"l{k}", lrecv.at[k])
        lsum[...] = lsend[k] + lrecv[k]

    step = 512

    def loop_part(start, count, store):
        @pl.loop(0, width // step)
        def _(t):
            cols = rows(t * step, step, step)
            store(cols, scale * jnp.dot(
                wt[rows(start, count), :], qbuf[pl.ds(0, q_dev), cols],
                preferred_element_type=F32,
            ))

    def pool_weights(yy, zz, at):
        base = pool_base(yy, zz, core)
        for k in range(2):
            row = lax.broadcasted_iota(jnp.int32, (p_dev, q_dev), 0) + base
            wht[at:at + p_dev, k * q_dev:(k + 1) * q_dev] = jnp.where(
                row == ids[k, 0:1, :], w2[k, 0:1, :], 0.0
            ).astype(BF16)

    def pool_part(count, store):
        @pl.loop(0, width // step)
        def _(t):
            cols = rows(t * step, step, step)
            store(cols, scale * jnp.dot(
                wht[pl.ds(0, count), :], qbuf[:, cols], preferred_element_type=F32
            ))

    def into(ref, k):
        def store(cols, value):
            ref[k, :, cols] = value.astype(BF16)
        return store

    def x_part(k):
        slot = {1: 0, 3: 1, 2: 2}[k]
        loop_part(px[k] * 2 * p_dev, 2 * p_dev, into(xs, slot))

    def y_part(k):
        slot = {1: 0, 3: 1, 2: 2}[k]
        pool_weights(py[k], 0, 0)
        pool_weights(py[k], 1, p_dev)
        pool_part(2 * p_dev, into(ys, slot))

    z_of = {"x": (oz, zl), "y": (oh, zh)}
    axes = {"x": (xs, xrf, xrs, xp, xm), "y": (ys, yrf, yrs, yp, ym)}

    def piece(a, slot, role, h, n=half):
        return axes[a][0].at[slot, rows(z_of[a][role] * p_dev + h * half, n)]

    def send_far(a, role):
        _, rf, _, plus, minus = axes[a]
        send(f"{a}+s2{role}", piece(a, 2, role, 0), rf.at[0, role], plus)
        send(f"{a}-s2{role}", piece(a, 2, role, 1), rf.at[1, role], minus)

    def send_near(a, role):
        _, _, rs, plus, minus = axes[a]
        send(f"{a}+s1{role}", piece(a, 0, role, 1), rs.at[0, role, pl.ds(half, half)], plus)
        send(f"{a}-s1{role}", piece(a, 1, role, 0), rs.at[1, role, pl.ds(0, half)], minus)

    def send_sum(a, role):
        _, rf, rs, plus, minus = axes[a]
        for d, (sign, slot, h, peer) in enumerate((("+", 0, 0, plus), ("-", 1, 1, minus))):
            arrived(f"{a}{sign}s2{role}", rf.at[d, role])
            mine = piece(a, slot, role, h)

            @pl.loop(0, width // step)
            def _(t):
                cols = rows(t * step, step, step)
                mine[:, cols] = (
                    mine[:, cols].astype(F32) + rf[d, role, :, cols].astype(F32)
                ).astype(BF16)

            send(f"{a}{sign}s0{role}", mine, rs.at[d, role, pl.ds(h * half, half)], peer)

    def sums_arrived(a, role):
        rs = axes[a][2]
        for d, sign in enumerate("+-"):
            near = 1 - d
            arrived(f"{a}{sign}s1{role}", rs.at[d, role, pl.ds(near * half, half)])
            arrived(f"{a}{sign}s0{role}", rs.at[d, role, pl.ds(d * half, half)])

    x_part(2)
    send_far("x", 0)
    arrived("w", w2.at[1])
    loss_start(0)
    y_part(2)
    send_far("y", 0)
    send("o4", prow(py[3], oh), orow(py[3], oh), sib)
    send("o5", prow(py[1], oh), orow(py[1], oh), sib)
    send("o6", prow(py[2], oh), orow(py[2], oh), sib)
    x_part(1)
    x_part(3)
    send_near("x", 0)
    loss_finish(0)
    loss_start(1)
    y_part(1)
    y_part(3)
    send_near("y", 0)
    send_sum("x", 0)
    send_sum("y", 0)
    send_far("x", 1)
    send_far("y", 1)
    send_near("x", 1)
    send_near("y", 1)
    loss_finish(1)
    loss_start(2)

    for a in "xy":
        sent(f"{a}+s20")
        sent(f"{a}-s20")

    hand_x = xs.at[2, rows(oz * p_dev, p_dev)]
    hand_y = ys.at[2, rows(oh * p_dev, p_dev)]

    def store_hand_x(cols, value):
        hand_x[:, cols] = value.astype(BF16)

    def store_hand_y(cols, value):
        hand_y[:, cols] = value.astype(BF16)

    def store_own(cols, value):
        s[:, cols] = value

    def add_own(cols, value):
        s[:, cols] += value

    pool_weights(y, oh, 0)
    pool_part(p_dev, store_hand_y)
    loop_part((x * 2 + oz) * p_dev, p_dev, store_hand_x)
    loop_part((x * 2 + zl) * p_dev, p_dev, store_own)
    pool_weights(y, zh, 0)
    pool_part(p_dev, add_own)
    loss_finish(2)
    loss_start(3)

    for c in range(blocks):
        wall[:, c * p_dev:(c + 1) * p_dev] = (
            wt[c * p_dev:(c + 1) * p_dev, :].astype(F32).T.astype(BF16)
        )
    loop_rows = blocks * p_dev

    @pl.loop(0, q_dev // 128)
    def _(n):
        part = rows(n * 128, 128, 128)
        names = jnp.broadcast_to(ids[0, 0:1, part].astype(F32), (128, 128)).T
        values = jnp.broadcast_to(w2[0, 0:1, part], (128, 128)).T
        lane = lax.broadcasted_iota(jnp.int32, (128, 128), 1)
        for k in range(2):
            cc = core if k == 0 else 1 - core
            for slot in range(8):
                base = pool_base(slot // 2, slot % 2, cc)
                at = loop_rows + (k * 8 + slot) * p_dev
                wall[part, at:at + p_dev] = jnp.where(
                    names == (lane + base).astype(F32), values, 0.0
                ).astype(BF16)

    arrived("oo", orow(y, zh))
    arrived("o3", orow(py[3], zh))
    arrived("o1", orow(py[1], zh))
    arrived("op", orow(y, oh))
    arrived("o2", orow(py[2], zh))
    arrived("o4", orow(py[3], oh))
    arrived("o5", orow(py[1], oh))
    arrived("o6", orow(py[2], oh))

    tile = dqt.shape[2]
    tiles = width // tile
    pool_rows = pbuf.shape[0]

    def tile_in(t):
        k = lax.rem(t, 2)
        return pltpu.make_async_copy(
            other_hbm.at[:, rows(t * tile, tile, tile)], otile.at[k], csem.at[k]
        )

    def tile_out(t):
        k = lax.rem(t, 2)
        return pltpu.make_async_copy(
            dqt.at[k], dq_hbm.at[:, rows(t * tile, tile, tile)], csem.at[2 + k]
        )

    tile_in(0).start()

    def query_slope(first, last):
        @pl.loop(first, last)
        def _(t):
            k = lax.rem(t, 2)

            @pl.when(t + 1 < tiles)
            def _():
                tile_in(t + 1).start()

            @pl.when(t >= 2)
            def _():
                tile_out(t - 2).wait()

            cols = rows(t * tile, tile, tile)
            tile_in(t).wait()
            acc = jnp.dot(
                wall[:, 0:loop_rows], lbuf[:, cols], preferred_element_type=F32
            )
            acc += jnp.dot(
                wall[:, loop_rows:loop_rows + pool_rows], pbuf[:, cols],
                preferred_element_type=F32,
            )
            acc += jnp.dot(
                wall[:, loop_rows + pool_rows:], otile[k], preferred_element_type=F32
            )
            dqt[k] = (scale * acc).astype(BF16)
            tile_out(t).start()

    query_slope(0, tiles // 4)
    loss_finish(3)
    loss_start(4)
    query_slope(tiles // 4, tiles // 2)

    sums_arrived("y", 0)
    for h in range(2):
        part = pl.ds(h * half, half)

        @pl.loop(0, width // step)
        def _(t):
            cols = rows(t * step, step, step)
            hand_y[part, cols] = (
                hand_y[part, cols].astype(F32)
                + yrs[0, 0, part, cols].astype(F32)
                + yrs[1, 0, part, cols].astype(F32)
            ).astype(BF16)

        send(f"zh{h}", hand_y.at[part], zrh.at[part], p2)
    loss_finish(4)
    loss_start(5)
    query_slope(tiles // 2, tiles * 3 // 4)
    send_sum("x", 1)
    send_sum("y", 1)
    loss_finish(5)
    loss_start(6)
    sums_arrived("x", 0)
    for h in range(2):
        part = pl.ds(h * half, half)
        arrived(f"zh{h}", zrh.at[part])

        @pl.loop(0, width // step)
        def _(t):
            cols = rows(t * step, step, step)
            hand_x[part, cols] = (
                hand_x[part, cols].astype(F32)
                + xrs[0, 0, part, cols].astype(F32)
                + xrs[1, 0, part, cols].astype(F32)
                + zrh[part, cols].astype(F32)
            ).astype(BF16)

        send(f"zl{h}", hand_x.at[part], zrl.at[part], p1)
    query_slope(tiles * 3 // 4, tiles)
    loss_finish(6)
    loss_ref[...] = lsum[...]

    sums_arrived("x", 1)
    sums_arrived("y", 1)
    sent("y+s21")
    sent("y-s21")
    result = ys.at[2, rows(zh * p_dev, p_dev)]
    outs = []
    for h in range(2):
        part = pl.ds(h * half, half)
        arrived(f"zl{h}", zrl.at[part])

        @pl.loop(0, width // step)
        def _(t):
            cols = rows(t * step, step, step)
            result[part, cols] = (
                s[part, cols]
                + xrs[0, 1, part, cols].astype(F32)
                + xrs[1, 1, part, cols].astype(F32)
                + yrs[0, 1, part, cols].astype(F32)
                + yrs[1, 1, part, cols].astype(F32)
                + zrl[part, cols].astype(F32)
            ).astype(BF16)

        copy = pltpu.make_async_copy(result.at[part], dp_hbm.at[part], csem.at[h])
        copy.start()
        outs.append(copy)
    tile_out(tiles - 2).wait()
    tile_out(tiles - 1).wait()
    for copy in outs:
        copy.wait()
    for name in list(started):
        sent(name)


def shards(queries, passages, positive_ids, hard_ids):
    q_dev, width = queries.shape
    p_dev = passages.shape[0]
    half = p_dev // 2
    vmem = pltpu.VMEM
    hbm = pl.BlockSpec(memory_space=pl.ANY)
    block = pl.BlockSpec(memory_space=pltpu.VMEM)
    loss, slope, grad, _ = pl.pallas_call(
        kernel,
        out_shape=(
            jax.ShapeDtypeStruct((8, 128), F32),
            jax.ShapeDtypeStruct((q_dev, width), BF16),
            jax.ShapeDtypeStruct((p_dev, width), BF16),
            jax.ShapeDtypeStruct((8 * p_dev, width), BF16),
        ),
        in_specs=[hbm, hbm, block, block],
        out_specs=(block, hbm, hbm, hbm),
        scratch_shapes=[
            vmem((8 * p_dev, width), BF16),
            vmem((8 * p_dev, width), BF16),
            vmem((2 * q_dev, width), BF16),
            vmem((p_dev, 8 * q_dev), F32),
            vmem((8 * p_dev, q_dev), BF16),
            vmem((q_dev, 24 * p_dev), BF16),
            vmem((2 * p_dev, 2 * q_dev), BF16),
            vmem((3, 2 * p_dev, width), BF16),
            vmem((3, 2 * p_dev, width), BF16),
            vmem((2, 2, half, width), BF16),
            vmem((2, 2, p_dev, width), BF16),
            vmem((2, 2, half, width), BF16),
            vmem((2, 2, p_dev, width), BF16),
            vmem((p_dev, width), BF16),
            vmem((p_dev, width), BF16),
            vmem((2, 8, q_dev), jnp.int32),
            vmem((2, 8, q_dev), F32),
            vmem((8, q_dev), F32),
            vmem((2, 8, q_dev), F32),
            vmem((8, q_dev), F32),
            vmem((8, 128), F32),
            vmem((7, 8, 128), F32),
            vmem((7, 8, 128), F32),
            vmem((2, 8 * p_dev, 256), BF16),
            vmem((2, q_dev, 256), BF16),
            pltpu.SemaphoreType.DMA((COPIES,)),
            pltpu.SemaphoreType.DMA((COPIES,)),
            pltpu.SemaphoreType.DMA((4,)),
        ],
        compiler_params=pltpu.CompilerParams(
            collective_id=0, has_side_effects=True, vmem_limit_bytes=63 * 2**20
        ),
        cost_estimate=pl.CostEstimate(
            flops=2 * q_dev * width * 9 * 8 * p_dev,
            bytes_accessed=40 * 2**20,
            transcendentals=2 * 8 * p_dev * q_dev,
        ),
    )(
        queries,
        passages,
        positive_ids.reshape(1, q_dev),
        hard_ids.reshape(1, q_dev),
    )
    total = q_dev * lax.axis_size("blk") * lax.axis_size("grp")
    return loss[0, 0] / total, slope, grad


def solution(mesh):
    return jax.shard_map(
        shards,
        mesh=mesh,
        in_specs=(
            P(("blk", "grp"), None),
            P(("blk", "grp"), None),
            P(("blk", "grp")),
            P(("blk", "grp"), None),
        ),
        out_specs=(P(), P(("blk", "grp"), None), P(("blk", "grp"), None)),
        check_vma=False,
    )
```

```python
import functools

import jax
import jax.numpy as jnp
from jax import lax
from jax.experimental import pallas as pl
from jax.experimental.pallas import tpu as pltpu
from jax.sharding import PartitionSpec as P

logit_scaling_coefficient = 20.0
MESH = pl.DeviceIdType.MESH
BF16 = jnp.bfloat16
F32 = jnp.float32
COPIES = 80
NT = (((1,), (1,)), ((), ()))


def rows(start, size, multiple=64):
    return pl.ds(pl.multiple_of(start, multiple), size)


def kernel(
    q_hbm, p_hbm, pos_ref, hid_ref,
    loss_ref, dq_hbm, dp_hbm, other_hbm,
    lbuf, pbuf, qbuf, s, wt, wall, wht, xs, ys, xrf, xrs, yrf, yrs, zrh, zrl,
    ids, hs, hin, w2, top, lsum, lsend, lrecv, otile, dqt,
    ssem, rsem, csem,
):
    q_dev, width = q_hbm.shape
    p_dev = p_hbm.shape[0]
    half = p_dev // 2
    scale = logit_scaling_coefficient

    b = lax.axis_index("blk")
    g = lax.axis_index("grp")
    x, zl = lax.div(b, 2), lax.rem(b, 2)
    zh, y, core = lax.div(g, 8), lax.div(lax.rem(g, 8), 2), lax.rem(g, 2)
    pb = x * 2 + 1 - zl
    px = [lax.rem(x + k, 4) for k in range(4)]
    py = [lax.rem(y + k, 4) for k in range(4)]
    xp = (px[1] * 2 + zl, g)
    xm = (px[3] * 2 + zl, g)
    yp = (b, zh * 8 + py[1] * 2 + core)
    ym = (b, zh * 8 + py[3] * 2 + core)
    p1 = (pb, g)
    p2 = (pb, lax.rem(g + 8, 16))
    sib = (b, zh * 8 + y * 2 + 1 - core)

    number = {}
    started = {}

    def describe(name, src, dst, peer):
        k = number.setdefault(name, len(number))
        return pltpu.make_async_remote_copy(
            src_ref=src, dst_ref=dst, send_sem=ssem.at[k], recv_sem=rsem.at[k],
            device_id=peer, device_id_type=MESH,
        )

    def send(name, src, dst, peer):
        copy = describe(name, src, dst, peer)
        copy.start()
        started[name] = copy

    def sent(name):
        started.pop(name).wait_send()

    def arrived(name, dst):
        describe(name, dst, dst, sib).wait_recv()

    barrier = pltpu.get_barrier_semaphore()
    for peer in (xp, xm, yp, ym, p1, p2, sib):
        pl.semaphore_signal(barrier, inc=1, device_id=peer, device_id_type=MESH)
    pl.semaphore_wait(barrier, 7)

    def lrow(xx, zz, h=0, n=p_dev):
        return lbuf.at[rows((xx * 2 + zz) * p_dev + h * half, n)]

    def prow(yy, zz, h=0, n=p_dev):
        return pbuf.at[rows((yy * 2 + zz) * p_dev + h * half, n)]

    def orow(yy, zz):
        return other_hbm.at[rows((yy * 2 + zz) * p_dev, p_dev)]

    own = [p_hbm.at[pl.ds(h * half, half)] for h in range(2)]

    for h in range(2):
        send(f"z{h}", own[h], lrow(x, zl, h, half), p1)
    for h in range(2):
        send(f"x+o{h}", own[h], lrow(x, zl, h, half), xp)
        send(f"x-o{1 - h}", own[1 - h], lrow(x, zl, 1 - h, half), xm)
        send(f"y+o{h}", own[h], prow(y, zh, h, half), yp)
        send(f"y-o{1 - h}", own[1 - h], prow(y, zh, 1 - h, half), ym)
    local = [
        pltpu.make_async_copy(q_hbm, qbuf.at[pl.ds(0, q_dev)], csem.at[0]),
        pltpu.make_async_copy(p_hbm, lrow(x, zl), csem.at[1]),
        pltpu.make_async_copy(p_hbm, prow(y, zh), csem.at[2]),
    ]
    for copy in local:
        copy.start()
    ids[0] = jnp.broadcast_to(hid_ref[...], ids.shape[1:])
    send("ids", ids.at[0], ids.at[1], sib)
    send("q", q_hbm, qbuf.at[pl.ds(q_dev, q_dev)], sib)
    send("oo", p_hbm, orow(y, zh), sib)

    hs[...] = jnp.zeros(hs.shape, F32)
    top[...] = jnp.full(top.shape, -jnp.inf, F32)

    def score_loop(xx, zz):
        c = xx * 2 + zz

        @pl.loop(0, q_dev // 256)
        def _(n):
            cols = rows(n * 256, 256, 256)
            acc = scale * lax.dot_general(
                lbuf[rows(c * p_dev, p_dev), :], qbuf[cols, :], NT, preferred_element_type=F32
            )
            s[:, rows(c * q_dev + n * 256, 256, 256)] = acc
            top[:, cols] = jnp.maximum(top[:, cols], jnp.max(acc, axis=0, keepdims=True))

    def pool_base(yy, zz, cc):
        return (zz * 8 + yy * 2 + cc) * p_dev

    def score_pool(yy, zz):
        slot = yy * 2 + zz
        base = pool_base(yy, zz, core)
        for k in range(2):

            @pl.loop(0, q_dev // 256)
            def _(n):
                cols = rows(n * 256, 256, 256)
                acc = lax.dot_general(
                    pbuf[rows(slot * p_dev, p_dev), :],
                    qbuf[rows(k * q_dev + n * 256, 256, 256), :],
                    NT,
                    preferred_element_type=F32,
                )
                row = lax.broadcasted_iota(jnp.int32, acc.shape, 0) + base
                named = jnp.where(row == ids[k, 0:1, cols], scale * acc, 0.0)
                hs[k, :, cols] += jnp.sum(named, axis=0, keepdims=True)

    oz, oh = 1 - zl, 1 - zh

    for copy in local:
        copy.wait()
    score_loop(x, zl)

    arrived("x+o0", lrow(px[3], zl, 0, half))
    send("x+f", lrow(px[3], zl, 0, half), lrow(px[3], zl, 0, half), xp)
    arrived("x-o1", lrow(px[1], zl, 1, half))
    send("x-f", lrow(px[1], zl, 1, half), lrow(px[1], zl, 1, half), xm)
    arrived("y+o0", prow(py[3], zh, 0, half))
    send("y+f", prow(py[3], zh, 0, half), prow(py[3], zh, 0, half), yp)
    arrived("y-o1", prow(py[1], zh, 1, half))
    send("y-f", prow(py[1], zh, 1, half), prow(py[1], zh, 1, half), ym)
    arrived("z0", lrow(x, oz, 0, half))
    send("h0", lrow(x, oz, 0, half), prow(y, zh, 0, half), p2)
    send("x+p0", lrow(x, oz, 0, half), lrow(x, oz, 0, half), xp)
    arrived("ids", ids.at[1])
    arrived("q", qbuf.at[pl.ds(q_dev, q_dev)])
    score_pool(y, zh)

    arrived("z1", lrow(x, oz, 1, half))
    send("h1", lrow(x, oz, 1, half), prow(y, zh, 1, half), p2)
    send("x-p1", lrow(x, oz, 1, half), lrow(x, oz, 1, half), xm)
    send("x+p1", lrow(x, oz, 1, half), lrow(x, oz, 1, half), xp)
    send("x-p0", lrow(x, oz, 0, half), lrow(x, oz, 0, half), xm)
    arrived("h0", prow(y, oh, 0, half))
    send("y+p0", prow(y, oh, 0, half), prow(y, oh, 0, half), yp)
    score_loop(x, oz)
    arrived("x+o1", lrow(px[3], zl, 1, half))
    score_loop(px[3], zl)
    arrived("x-o0", lrow(px[1], zl, 0, half))
    score_loop(px[1], zl)
    arrived("y+o1", prow(py[3], zh, 1, half))
    send("o3", prow(py[3], zh), orow(py[3], zh), sib)
    score_pool(py[3], zh)
    arrived("y-o0", prow(py[1], zh, 0, half))
    send("o1", prow(py[1], zh), orow(py[1], zh), sib)
    arrived("h1", prow(y, oh, 1, half))
    send("y-p1", prow(y, oh, 1, half), prow(y, oh, 1, half), ym)
    send("y+p1", prow(y, oh, 1, half), prow(y, oh, 1, half), yp)
    send("y-p0", prow(y, oh, 0, half), prow(y, oh, 0, half), ym)
    send("op", prow(y, oh), orow(y, oh), sib)
    score_pool(py[1], zh)
    arrived("x+f", lrow(px[2], zl, 0, half))
    arrived("x-f", lrow(px[2], zl, 1, half))
    score_loop(px[2], zl)
    arrived("y+f", prow(py[2], zh, 0, half))
    arrived("y-f", prow(py[2], zh, 1, half))
    send("o2", prow(py[2], zh), orow(py[2], zh), sib)
    arrived("x+p0", lrow(px[3], oz, 0, half))
    send("x+g", lrow(px[3], oz, 0, half), lrow(px[3], oz, 0, half), xp)
    arrived("x-p1", lrow(px[1], oz, 1, half))
    send("x-g", lrow(px[1], oz, 1, half), lrow(px[1], oz, 1, half), xm)
    arrived("y+p0", prow(py[3], oh, 0, half))
    send("y+g", prow(py[3], oh, 0, half), prow(py[3], oh, 0, half), yp)
    arrived("y-p1", prow(py[1], oh, 1, half))
    send("y-g", prow(py[1], oh, 1, half), prow(py[1], oh, 1, half), ym)
    score_pool(y, oh)
    score_pool(py[2], zh)
    arrived("x+p1", lrow(px[3], oz, 1, half))
    score_loop(px[3], oz)
    arrived("x-p0", lrow(px[1], oz, 0, half))
    score_loop(px[1], oz)
    arrived("y+p1", prow(py[3], oh, 1, half))
    score_pool(py[3], oh)
    arrived("y-p0", prow(py[1], oh, 0, half))
    score_pool(py[1], oh)
    arrived("y+g", prow(py[2], oh, 0, half))
    arrived("y-g", prow(py[2], oh, 1, half))
    score_pool(py[2], oh)
    send("hs", hs.at[1], hin, sib)
    arrived("x+g", lrow(px[2], oz, 0, half))
    arrived("x-g", lrow(px[2], oz, 1, half))
    score_loop(px[2], oz)

    arrived("hs", hin)
    hard = hs[0] + hin[...]
    hard = hard[0:1]
    peak = jnp.maximum(top[0:1], hard)
    total = jnp.exp(hard - peak)
    positive = jnp.zeros_like(peak)
    blocks = s.shape[1] // q_dev
    for c in range(blocks):
        part = s[:, c * q_dev:(c + 1) * q_dev]
        total += jnp.sum(jnp.exp(part - peak), axis=0, keepdims=True)
        row = lax.broadcasted_iota(jnp.int32, part.shape, 0) + c * p_dev
        positive += jnp.sum(jnp.where(row == pos_ref[...], part, 0.0), axis=0, keepdims=True)
    log_total = peak + jnp.log(total)
    w_hard = jnp.exp(hard - log_total).astype(BF16).astype(F32)
    w2[0] = jnp.broadcast_to(w_hard, w2.shape[1:])
    send("w", w2.at[0], w2.at[1], sib)
    for c in range(blocks):
        part = s[:, c * q_dev:(c + 1) * q_dev]
        row = lax.broadcasted_iota(jnp.int32, part.shape, 0) + c * p_dev
        hit = jnp.where(row == pos_ref[...], 1.0, 0.0)
        wt[c * p_dev:(c + 1) * p_dev, :] = (jnp.exp(part - log_total) - hit).astype(BF16)
    lsum[...] = jnp.broadcast_to(
        jnp.sum(log_total - positive, axis=1, keepdims=True), lsum.shape
    )

    loss_peers = [
        (lax.rem(b + 2 + 4 * lax.rem(x, 2), 8), g),
        (b, zh * 8 + lax.rem(y + 1 + 2 * lax.rem(y, 2), 4) * 2 + core),
        p1,
        p2,
        sib,
        ((3 - x) * 2 + zl, g),
        (b, zh * 8 + (3 - y) * 2 + core),
    ]

    def loss_start(k):
        lsend[k] = lsum[...]
        send(f"l{k}", lsend.at[k], lrecv.at[k], loss_peers[k])

    def loss_finish(k):
        arrived(f"l{k}", lrecv.at[k])
        lsum[...] = lsend[k] + lrecv[k]

    loss_start(0)

    step = 512

    def loop_part(start, count, store):
        @pl.loop(0, width // step, unroll=4)
        def _(t):
            cols = rows(t * step, step, step)
            store(cols, scale * jnp.dot(
                wt[rows(start, count), :], qbuf[pl.ds(0, q_dev), cols],
                preferred_element_type=F32,
            ))

    def pool_weights(yy, zz, at):
        base = pool_base(yy, zz, core)
        for k in range(2):
            row = lax.broadcasted_iota(jnp.int32, (p_dev, q_dev), 0) + base
            wht[at:at + p_dev, k * q_dev:(k + 1) * q_dev] = jnp.where(
                row == ids[k, 0:1, :], w2[k, 0:1, :], 0.0
            ).astype(BF16)

    def pool_part(count, store):
        @pl.loop(0, width // step, unroll=4)
        def _(t):
            cols = rows(t * step, step, step)
            store(cols, scale * jnp.dot(
                wht[pl.ds(0, count), :], qbuf[:, cols], preferred_element_type=F32
            ))

    def into(ref, k):
        def store(cols, value):
            ref[k, :, cols] = value.astype(BF16)
        return store

    def x_part(k):
        slot = {1: 0, 3: 1, 2: 2}[k]
        loop_part(px[k] * 2 * p_dev, 2 * p_dev, into(xs, slot))

    def y_part(k):
        slot = {1: 0, 3: 1, 2: 2}[k]
        pool_weights(py[k], 0, 0)
        pool_weights(py[k], 1, p_dev)
        pool_part(2 * p_dev, into(ys, slot))

    z_of = {"x": (oz, zl), "y": (oh, zh)}
    axes = {"x": (xs, xrf, xrs, xp, xm), "y": (ys, yrf, yrs, yp, ym)}

    def piece(a, slot, role, h, n=half):
        return axes[a][0].at[slot, rows(z_of[a][role] * p_dev + h * half, n)]

    def send_far(a, role):
        _, rf, _, plus, minus = axes[a]
        send(f"{a}+s2{role}", piece(a, 2, role, 0), rf.at[0, role], plus)
        send(f"{a}-s2{role}", piece(a, 2, role, 1), rf.at[1, role], minus)

    def send_near(a, role):
        _, _, rs, plus, minus = axes[a]
        send(f"{a}+s1{role}", piece(a, 0, role, 1), rs.at[0, role, pl.ds(half, half)], plus)
        send(f"{a}-s1{role}", piece(a, 1, role, 0), rs.at[1, role, pl.ds(0, half)], minus)

    def send_sum(a, role):
        _, rf, rs, plus, minus = axes[a]
        for d, (sign, slot, h, peer) in enumerate((("+", 0, 0, plus), ("-", 1, 1, minus))):
            arrived(f"{a}{sign}s2{role}", rf.at[d, role])
            mine = piece(a, slot, role, h)

            @pl.loop(0, width // step)
            def _(t):
                cols = rows(t * step, step, step)
                mine[:, cols] = (
                    mine[:, cols].astype(F32) + rf[d, role, :, cols].astype(F32)
                ).astype(BF16)

            send(f"{a}{sign}s0{role}", mine, rs.at[d, role, pl.ds(h * half, half)], peer)

    def sums_arrived(a, role):
        rs = axes[a][2]
        for d, sign in enumerate("+-"):
            near = 1 - d
            arrived(f"{a}{sign}s1{role}", rs.at[d, role, pl.ds(near * half, half)])
            arrived(f"{a}{sign}s0{role}", rs.at[d, role, pl.ds(d * half, half)])

    x_part(2)
    send_far("x", 0)
    loss_finish(0)
    loss_start(1)
    arrived("w", w2.at[1])
    y_part(2)
    loss_finish(1)
    send_far("y", 0)
    loss_start(2)
    send("o4", prow(py[3], oh), orow(py[3], oh), sib)
    send("o5", prow(py[1], oh), orow(py[1], oh), sib)
    send("o6", prow(py[2], oh), orow(py[2], oh), sib)
    x_part(1)
    x_part(3)
    send_near("x", 0)
    loss_finish(2)
    loss_start(3)
    y_part(1)
    y_part(3)
    send_near("y", 0)
    loss_finish(3)
    loss_start(4)
    send_sum("x", 0)
    send_sum("y", 0)
    loss_finish(4)
    loss_start(5)
    send_far("x", 1)
    send_far("y", 1)
    send_near("x", 1)
    send_near("y", 1)

    for a in "xy":
        sent(f"{a}+s20")
        sent(f"{a}-s20")

    hand_x = xs.at[2, rows(oz * p_dev, p_dev)]
    hand_y = ys.at[2, rows(oh * p_dev, p_dev)]

    def split(first, value):
        low, high = value[:p_dev], value[p_dev:]
        return jnp.where(first, low, high), jnp.where(first, high, low)

    def store_x(cols, value):
        mine, handed = split(zl == 0, value)
        s[:, cols] = mine
        hand_x[:, cols] = handed.astype(BF16)

    def store_y(cols, value):
        mine, handed = split(zh == 0, value)
        s[:, cols] += mine
        hand_y[:, cols] = handed.astype(BF16)

    loop_part(x * 2 * p_dev, 2 * p_dev, store_x)
    pool_weights(y, 0, 0)
    pool_weights(y, 1, p_dev)
    pool_part(2 * p_dev, store_y)

    for c in range(blocks):
        wall[:, c * p_dev:(c + 1) * p_dev] = (
            wt[c * p_dev:(c + 1) * p_dev, :].astype(F32).T.astype(BF16)
        )
    loop_rows = blocks * p_dev

    @pl.loop(0, q_dev // 128)
    def _(n):
        part = rows(n * 128, 128, 128)
        names = jnp.broadcast_to(ids[0, 0:1, part].astype(F32), (128, 128)).T
        values = jnp.broadcast_to(w2[0, 0:1, part], (128, 128)).T
        lane = lax.broadcasted_iota(jnp.int32, (128, 128), 1)
        for k in range(2):
            cc = core if k == 0 else 1 - core
            for slot in range(8):
                base = pool_base(slot // 2, slot % 2, cc)
                at = loop_rows + (k * 8 + slot) * p_dev
                wall[part, at:at + p_dev] = jnp.where(
                    names == (lane + base).astype(F32), values, 0.0
                ).astype(BF16)

    arrived("oo", orow(y, zh))
    arrived("o3", orow(py[3], zh))
    arrived("o1", orow(py[1], zh))
    arrived("op", orow(y, oh))
    arrived("o2", orow(py[2], zh))
    arrived("o4", orow(py[3], oh))
    arrived("o5", orow(py[1], oh))
    arrived("o6", orow(py[2], oh))

    tile = dqt.shape[2]
    tiles = width // tile
    pool_rows = pbuf.shape[0]

    def tile_in(t):
        k = lax.rem(t, 2)
        return pltpu.make_async_copy(
            other_hbm.at[:, rows(t * tile, tile, tile)], otile.at[k], csem.at[k]
        )

    def tile_out(t):
        k = lax.rem(t, 2)
        return pltpu.make_async_copy(
            dqt.at[k], dq_hbm.at[:, rows(t * tile, tile, tile)], csem.at[2 + k]
        )

    tile_in(0).start()

    def query_slope(first, last):
        @pl.loop(first, last)
        def _(t):
            k = lax.rem(t, 2)

            @pl.when(t + 1 < tiles)
            def _():
                tile_in(t + 1).start()

            @pl.when(t >= 2)
            def _():
                tile_out(t - 2).wait()

            cols = rows(t * tile, tile, tile)
            tile_in(t).wait()
            acc = jnp.dot(
                wall[:, 0:loop_rows], lbuf[:, cols], preferred_element_type=F32
            )
            acc += jnp.dot(
                wall[:, loop_rows:loop_rows + pool_rows], pbuf[:, cols],
                preferred_element_type=F32,
            )
            acc += jnp.dot(
                wall[:, loop_rows + pool_rows:], otile[k], preferred_element_type=F32
            )
            dqt[k] = (scale * acc).astype(BF16)
            tile_out(t).start()

    query_slope(0, tiles * 3 // 4)
    loss_finish(5)
    loss_start(6)

    quarter = half // 2
    parts = [pl.ds(k * quarter, quarter) for k in range(4)]
    sums_arrived("y", 0)
    for k, part in enumerate(parts):

        @pl.loop(0, width // step, unroll=2)
        def _(t):
            cols = rows(t * step, step, step)
            hand_y[part, cols] = (
                hand_y[part, cols].astype(F32)
                + yrs[0, 0, part, cols].astype(F32)
                + yrs[1, 0, part, cols].astype(F32)
            ).astype(BF16)

        send(f"zh{k}", hand_y.at[part], zrh.at[part], p2)
    sums_arrived("x", 0)
    send_sum("x", 1)
    send_sum("y", 1)
    for k, part in enumerate(parts):
        arrived(f"zh{k}", zrh.at[part])

        @pl.loop(0, width // step, unroll=2)
        def _(t):
            cols = rows(t * step, step, step)
            hand_x[part, cols] = (
                hand_x[part, cols].astype(F32)
                + xrs[0, 0, part, cols].astype(F32)
                + xrs[1, 0, part, cols].astype(F32)
                + zrh[part, cols].astype(F32)
            ).astype(BF16)

        send(f"zl{k}", hand_x.at[part], zrl.at[part], p1)
        query_slope(tiles * (12 + k) // 16, tiles * (13 + k) // 16)
    loss_finish(6)
    loss_ref[...] = lsum[...]

    sums_arrived("x", 1)
    sums_arrived("y", 1)
    sent("y+s21")
    sent("y-s21")
    result = ys.at[2, rows(zh * p_dev, p_dev)]
    outs = []
    for h in range(2):
        part = pl.ds(h * half, half)
        arrived(f"zl{2 * h}", zrl.at[parts[2 * h]])
        arrived(f"zl{2 * h + 1}", zrl.at[parts[2 * h + 1]])

        @pl.loop(0, width // step)
        def _(t):
            cols = rows(t * step, step, step)
            result[part, cols] = (
                s[part, cols]
                + xrs[0, 1, part, cols].astype(F32)
                + xrs[1, 1, part, cols].astype(F32)
                + yrs[0, 1, part, cols].astype(F32)
                + yrs[1, 1, part, cols].astype(F32)
                + zrl[part, cols].astype(F32)
            ).astype(BF16)

        copy = pltpu.make_async_copy(result.at[part], dp_hbm.at[part], csem.at[h])
        copy.start()
        outs.append(copy)
    tile_out(tiles - 2).wait()
    tile_out(tiles - 1).wait()
    for copy in outs:
        copy.wait()
    for name in list(started):
        sent(name)


def shards(queries, passages, positive_ids, hard_ids):
    q_dev, width = queries.shape
    p_dev = passages.shape[0]
    half = p_dev // 2
    vmem = pltpu.VMEM
    hbm = pl.BlockSpec(memory_space=pl.ANY)
    block = pl.BlockSpec(memory_space=pltpu.VMEM)
    loss, slope, grad, _ = pl.pallas_call(
        kernel,
        out_shape=(
            jax.ShapeDtypeStruct((8, 128), F32),
            jax.ShapeDtypeStruct((q_dev, width), BF16),
            jax.ShapeDtypeStruct((p_dev, width), BF16),
            jax.ShapeDtypeStruct((8 * p_dev, width), BF16),
        ),
        in_specs=[hbm, hbm, block, block],
        out_specs=(block, hbm, hbm, hbm),
        scratch_shapes=[
            vmem((8 * p_dev, width), BF16),
            vmem((8 * p_dev, width), BF16),
            vmem((2 * q_dev, width), BF16),
            vmem((p_dev, 8 * q_dev), F32),
            vmem((8 * p_dev, q_dev), BF16),
            vmem((q_dev, 24 * p_dev), BF16),
            vmem((2 * p_dev, 2 * q_dev), BF16),
            vmem((3, 2 * p_dev, width), BF16),
            vmem((3, 2 * p_dev, width), BF16),
            vmem((2, 2, half, width), BF16),
            vmem((2, 2, p_dev, width), BF16),
            vmem((2, 2, half, width), BF16),
            vmem((2, 2, p_dev, width), BF16),
            vmem((p_dev, width), BF16),
            vmem((p_dev, width), BF16),
            vmem((2, 8, q_dev), jnp.int32),
            vmem((2, 8, q_dev), F32),
            vmem((8, q_dev), F32),
            vmem((2, 8, q_dev), F32),
            vmem((8, q_dev), F32),
            vmem((8, 128), F32),
            vmem((7, 8, 128), F32),
            vmem((7, 8, 128), F32),
            vmem((2, 8 * p_dev, 256), BF16),
            vmem((2, q_dev, 256), BF16),
            pltpu.SemaphoreType.DMA((COPIES,)),
            pltpu.SemaphoreType.DMA((COPIES,)),
            pltpu.SemaphoreType.DMA((4,)),
        ],
        compiler_params=pltpu.CompilerParams(
            collective_id=0, has_side_effects=True, vmem_limit_bytes=63 * 2**20
        ),
        cost_estimate=pl.CostEstimate(
            flops=2 * q_dev * width * 9 * 8 * p_dev,
            bytes_accessed=40 * 2**20,
            transcendentals=2 * 8 * p_dev * q_dev,
        ),
    )(
        queries,
        passages,
        positive_ids.reshape(1, q_dev),
        hard_ids.reshape(1, q_dev),
    )
    total = q_dev * lax.axis_size("blk") * lax.axis_size("grp")
    return loss[0, 0] / total, slope, grad


def solution(mesh):
    return jax.shard_map(
        shards,
        mesh=mesh,
        in_specs=(
            P(("blk", "grp"), None),
            P(("blk", "grp"), None),
            P(("blk", "grp")),
            P(("blk", "grp"), None),
        ),
        out_specs=(P(), P(("blk", "grp"), None), P(("blk", "grp"), None)),
        check_vma=False,
    )
```

```python
import functools

import jax
import jax.numpy as jnp
from jax import lax
from jax.experimental import pallas as pl
from jax.experimental.pallas import tpu as pltpu
from jax.sharding import PartitionSpec as P

logit_scaling_coefficient = 20.0
MESH = pl.DeviceIdType.MESH
BF16 = jnp.bfloat16
F32 = jnp.float32
COPIES = 112
NT = (((1,), (1,)), ((), ()))


def rows(start, size, multiple=64):
    return pl.ds(pl.multiple_of(start, multiple), size)


def kernel(
    q_hbm, p_hbm, pos_ref, hid_ref,
    loss_ref, dq_hbm, dp_hbm, other_hbm,
    lbuf, pbuf, qbuf, s, wt, wall, wht, xs, ys, xrf, xrs, yrf, yrs, zrh, zrl, via, mix,
    ids, hs, hin, w2, top, lsum, lsend, lrecv, otile, dqt,
    ssem, rsem, csem,
):
    q_dev, width = q_hbm.shape
    p_dev = p_hbm.shape[0]
    half = p_dev // 2
    scale = logit_scaling_coefficient

    b = lax.axis_index("blk")
    g = lax.axis_index("grp")
    x, zl = lax.div(b, 2), lax.rem(b, 2)
    zh, y, core = lax.div(g, 8), lax.div(lax.rem(g, 8), 2), lax.rem(g, 2)
    pb = x * 2 + 1 - zl
    px = [lax.rem(x + k, 4) for k in range(4)]
    py = [lax.rem(y + k, 4) for k in range(4)]
    xp = (px[1] * 2 + zl, g)
    xm = (px[3] * 2 + zl, g)
    yp = (b, zh * 8 + py[1] * 2 + core)
    ym = (b, zh * 8 + py[3] * 2 + core)
    p1 = (pb, g)
    p2 = (pb, lax.rem(g + 8, 16))
    sib = (b, zh * 8 + y * 2 + 1 - core)

    number = {}
    started = {}

    def describe(name, src, dst, peer):
        k = number.setdefault(name, len(number))
        return pltpu.make_async_remote_copy(
            src_ref=src, dst_ref=dst, send_sem=ssem.at[k], recv_sem=rsem.at[k],
            device_id=peer, device_id_type=MESH,
        )

    def send(name, src, dst, peer):
        copy = describe(name, src, dst, peer)
        copy.start()
        started[name] = copy

    def sent(name):
        started.pop(name).wait_send()

    def arrived(name, dst):
        describe(name, dst, dst, sib).wait_recv()

    barrier = pltpu.get_barrier_semaphore()
    for peer in (xp, xm, yp, ym, p1, p2, sib):
        pl.semaphore_signal(barrier, inc=1, device_id=peer, device_id_type=MESH)
    pl.semaphore_wait(barrier, 7)

    quarter = half // 2
    moved = half * 3 // 4
    halves = [(0, half), (half, half)]
    by_z = [(0, moved), (p_dev - moved, moved)]
    direct = [(moved, half - moved), (half, half - moved)]
    whole = (0, p_dev)

    def lrow(xx, zz, part=whole):
        return lbuf.at[rows((xx * 2 + zz) * p_dev + part[0], part[1], 16)]

    def prow(yy, zz, part=whole):
        return pbuf.at[rows((yy * 2 + zz) * p_dev + part[0], part[1], 16)]

    def orow(yy, zz):
        return other_hbm.at[rows((yy * 2 + zz) * p_dev, p_dev)]

    own = [p_hbm.at[pl.ds(h * half, half)] for h in range(2)]
    quarters = [(k * quarter, quarter) for k in range(4)]

    for k in range(4):
        send(f"z{k}", p_hbm.at[pl.ds(k * quarter, quarter)], lrow(x, zl, quarters[k]), p1)
    for h in range(2):
        r = 1 - h
        send(f"x+o{h}", own[h], lrow(x, zl, halves[h]), xp)
        send(f"x-o{r}", own[r], lrow(x, zl, halves[r]), xm)
        send(f"y+o{h}", own[h], prow(y, zh, halves[h]), yp)
        send(f"y-o{r}", own[r], prow(y, zh, halves[r]), ym)
    local = [
        pltpu.make_async_copy(q_hbm, qbuf.at[pl.ds(0, q_dev)], csem.at[0]),
        pltpu.make_async_copy(p_hbm, lrow(x, zl), csem.at[1]),
        pltpu.make_async_copy(p_hbm, prow(y, zh), csem.at[2]),
    ]
    for copy in local:
        copy.start()
    ids[0] = jnp.broadcast_to(hid_ref[...], ids.shape[1:])
    send("ids", ids.at[0], ids.at[1], sib)
    send("q", q_hbm, qbuf.at[pl.ds(q_dev, q_dev)], sib)
    send("oo", p_hbm, orow(y, zh), sib)

    hs[...] = jnp.zeros(hs.shape, F32)
    top[...] = jnp.full(top.shape, -jnp.inf, F32)

    def score_loop(xx, zz):
        c = xx * 2 + zz

        @pl.loop(0, q_dev // 256)
        def _(n):
            cols = rows(n * 256, 256, 256)
            acc = scale * lax.dot_general(
                lbuf[rows(c * p_dev, p_dev), :], qbuf[cols, :], NT, preferred_element_type=F32
            )
            s[:, rows(c * q_dev + n * 256, 256, 256)] = acc
            top[:, cols] = jnp.maximum(top[:, cols], jnp.max(acc, axis=0, keepdims=True))

    def pool_base(yy, zz, cc):
        return (zz * 8 + yy * 2 + cc) * p_dev

    def score_pool(yy, zz):
        slot = yy * 2 + zz
        base = pool_base(yy, zz, core)
        for k in range(2):

            @pl.loop(0, q_dev // 256)
            def _(n):
                cols = rows(n * 256, 256, 256)
                acc = lax.dot_general(
                    pbuf[rows(slot * p_dev, p_dev), :],
                    qbuf[rows(k * q_dev + n * 256, 256, 256), :],
                    NT,
                    preferred_element_type=F32,
                )
                row = lax.broadcasted_iota(jnp.int32, acc.shape, 0) + base
                named = jnp.where(row == ids[k, 0:1, cols], scale * acc, 0.0)
                hs[k, :, cols] += jnp.sum(named, axis=0, keepdims=True)

    oz, oh = 1 - zl, 1 - zh

    for copy in local:
        copy.wait()
    score_loop(x, zl)

    def pass_x(name, xx, zz, part, peer):
        send(name, lrow(xx, zz, part), lrow(xx, zz, part), peer)

    def pass_y(name, yy, zz, part, peer):
        send(name, prow(yy, zz, part), prow(yy, zz, part), peer)

    def pass_z(k):
        arrived(f"z{k}", lrow(x, oz, quarters[k]))
        send(f"h{k}", lrow(x, oz, quarters[k]), prow(y, zh, quarters[k]), p2)

    pass_z(0)
    pass_z(1)
    arrived("x+o0", lrow(px[3], zl, halves[0]))
    pass_x("x+f", px[3], zl, halves[0], xp)
    arrived("x-o1", lrow(px[1], zl, halves[1]))
    pass_x("x-f", px[1], zl, halves[1], xm)
    arrived("y+o0", prow(py[3], zh, halves[0]))
    pass_y("y+f", py[3], zh, halves[0], yp)
    arrived("y-o1", prow(py[1], zh, halves[1]))
    pass_y("y-f", py[1], zh, halves[1], ym)
    pass_x("x+p0", x, oz, halves[0], xp)
    arrived("ids", ids.at[1])
    arrived("q", qbuf.at[pl.ds(q_dev, q_dev)])
    score_pool(y, zh)

    pass_z(2)
    arrived("h0", prow(y, oh, quarters[0]))
    arrived("h1", prow(y, oh, quarters[1]))
    pass_y("y+p0", y, oh, halves[0], yp)
    pass_z(3)
    pass_x("x-p1", x, oz, halves[1], xm)
    pass_x("x+p1", x, oz, direct[1], xp)
    pass_x("x-p0", x, oz, direct[0], xm)
    arrived("x+o1", lrow(px[3], zl, halves[1]))
    pass_x("zx1", px[3], zl, by_z[1], p1)
    arrived("x-o0", lrow(px[1], zl, halves[0]))
    pass_x("zx0", px[1], zl, by_z[0], p1)
    arrived("y+o1", prow(py[3], zh, halves[1]))
    send("ty1", prow(py[3], zh, by_z[1]), via.at[1], p2)
    arrived("y-o0", prow(py[1], zh, halves[0]))
    send("ty0", prow(py[1], zh, by_z[0]), via.at[0], p2)
    send("o3", prow(py[3], zh), orow(py[3], zh), sib)
    send("o1", prow(py[1], zh), orow(py[1], zh), sib)
    score_loop(x, oz)
    score_loop(px[3], zl)
    score_loop(px[1], zl)
    arrived("h2", prow(y, oh, quarters[2]))
    arrived("h3", prow(y, oh, quarters[3]))
    pass_y("y-p1", y, oh, halves[1], ym)
    pass_y("y+p1", y, oh, direct[1], yp)
    pass_y("y-p0", y, oh, direct[0], ym)
    send("op", prow(y, oh), orow(y, oh), sib)
    score_pool(py[3], zh)
    score_pool(py[1], zh)
    arrived("x+f", lrow(px[2], zl, halves[0]))
    arrived("x-f", lrow(px[2], zl, halves[1]))
    score_loop(px[2], zl)
    arrived("ty1", via.at[1])
    send("tz1", via.at[1], prow(py[3], oh, by_z[1]), p1)
    score_pool(y, oh)
    arrived("y+f", prow(py[2], zh, halves[0]))
    arrived("y-f", prow(py[2], zh, halves[1]))
    send("o2", prow(py[2], zh), orow(py[2], zh), sib)
    score_pool(py[2], zh)
    arrived("x+p0", lrow(px[3], oz, halves[0]))
    pass_x("x+g", px[3], oz, halves[0], xp)
    arrived("x-p1", lrow(px[1], oz, halves[1]))
    pass_x("x-g", px[1], oz, halves[1], xm)
    arrived("y+p0", prow(py[3], oh, halves[0]))
    pass_y("y+g", py[3], oh, halves[0], yp)
    arrived("y-p1", prow(py[1], oh, halves[1]))
    pass_y("y-g", py[1], oh, halves[1], ym)
    arrived("ty0", via.at[0])
    send("tz0", via.at[0], prow(py[1], oh, by_z[0]), p1)
    arrived("x+p1", lrow(px[3], oz, direct[1]))
    arrived("zx1", lrow(px[3], oz, by_z[1]))
    score_loop(px[3], oz)
    arrived("x-p0", lrow(px[1], oz, direct[0]))
    arrived("zx0", lrow(px[1], oz, by_z[0]))
    score_loop(px[1], oz)
    arrived("y+p1", prow(py[3], oh, direct[1]))
    arrived("tz1", prow(py[3], oh, by_z[1]))
    score_pool(py[3], oh)
    arrived("y-p0", prow(py[1], oh, direct[0]))
    arrived("tz0", prow(py[1], oh, by_z[0]))
    score_pool(py[1], oh)
    arrived("y+g", prow(py[2], oh, halves[0]))
    arrived("y-g", prow(py[2], oh, halves[1]))
    score_pool(py[2], oh)
    send("hs", hs.at[1], hin, sib)
    arrived("x+g", lrow(px[2], oz, halves[0]))
    arrived("x-g", lrow(px[2], oz, halves[1]))
    score_loop(px[2], oz)

    arrived("hs", hin)
    hard = hs[0] + hin[...]
    hard = hard[0:1]
    peak = jnp.maximum(top[0:1], hard)
    total = jnp.exp(hard - peak)
    positive = jnp.zeros_like(peak)
    blocks = s.shape[1] // q_dev
    for c in range(blocks):
        part = s[:, c * q_dev:(c + 1) * q_dev]
        total += jnp.sum(jnp.exp(part - peak), axis=0, keepdims=True)
        row = lax.broadcasted_iota(jnp.int32, part.shape, 0) + c * p_dev
        positive += jnp.sum(jnp.where(row == pos_ref[...], part, 0.0), axis=0, keepdims=True)
    log_total = peak + jnp.log(total)
    w_hard = jnp.exp(hard - log_total).astype(BF16).astype(F32)
    w2[0] = jnp.broadcast_to(w_hard, w2.shape[1:])
    send("w", w2.at[0], w2.at[1], sib)
    for c in range(blocks):
        part = s[:, c * q_dev:(c + 1) * q_dev]
        row = lax.broadcasted_iota(jnp.int32, part.shape, 0) + c * p_dev
        hit = jnp.where(row == pos_ref[...], 1.0, 0.0)
        wt[c * p_dev:(c + 1) * p_dev, :] = (jnp.exp(part - log_total) - hit).astype(BF16)
    lsum[...] = jnp.broadcast_to(
        jnp.sum(log_total - positive, axis=1, keepdims=True), lsum.shape
    )

    loss_peers = [
        (lax.rem(b + 2 + 4 * lax.rem(x, 2), 8), g),
        (b, zh * 8 + lax.rem(y + 1 + 2 * lax.rem(y, 2), 4) * 2 + core),
        p1,
        p2,
        sib,
        ((3 - x) * 2 + zl, g),
        (b, zh * 8 + (3 - y) * 2 + core),
    ]

    def loss_start(k):
        lsend[k] = lsum[...]
        send(f"l{k}", lsend.at[k], lrecv.at[k], loss_peers[k])

    def loss_finish(k):
        arrived(f"l{k}", lrecv.at[k])
        lsum[...] = lsend[k] + lrecv[k]

    loss_start(0)

    step = 512

    def loop_part(start, count, store):
        @pl.loop(0, width // step, unroll=4)
        def _(t):
            cols = rows(t * step, step, step)
            store(cols, scale * jnp.dot(
                wt[rows(start, count), :], qbuf[pl.ds(0, q_dev), cols],
                preferred_element_type=F32,
            ))

    def pool_weights(yy, zz, at):
        base = pool_base(yy, zz, core)
        for k in range(2):
            row = lax.broadcasted_iota(jnp.int32, (p_dev, q_dev), 0) + base
            wht[at:at + p_dev, k * q_dev:(k + 1) * q_dev] = jnp.where(
                row == ids[k, 0:1, :], w2[k, 0:1, :], 0.0
            ).astype(BF16)

    def pool_part(count, store):
        @pl.loop(0, width // step, unroll=4)
        def _(t):
            cols = rows(t * step, step, step)
            store(cols, scale * jnp.dot(
                wht[pl.ds(0, count), :], qbuf[:, cols], preferred_element_type=F32
            ))

    def into(ref, k):
        def store(cols, value):
            ref[k, :, cols] = value.astype(BF16)
        return store

    def x_part(k):
        slot = {1: 0, 3: 1, 2: 2}[k]
        loop_part(px[k] * 2 * p_dev, 2 * p_dev, into(xs, slot))

    def y_part(k):
        slot = {1: 0, 3: 1, 2: 2}[k]
        pool_weights(py[k], 0, 0)
        pool_weights(py[k], 1, p_dev)
        pool_part(2 * p_dev, into(ys, slot))

    z_of = {"x": (oz, zl), "y": (oh, zh)}
    axes = {"x": (xs, xrf, xrs, xp, xm), "y": (ys, yrf, yrs, yp, ym)}

    def piece(a, slot, role, part):
        return axes[a][0].at[slot, rows(z_of[a][role] * p_dev + part[0], part[1], 16)]

    def at(part):
        return pl.ds(part[0], part[1])

    def add_to(dst, *terms):
        @pl.loop(0, width // step, unroll=2)
        def _(t):
            cols = rows(t * step, step, step)
            total = dst[:, cols].astype(F32)
            for term in terms:
                total += term[:, cols].astype(F32)
            dst[:, cols] = total.astype(BF16)

    def send_far(a, role):
        _, rf, _, plus, minus = axes[a]
        send(f"{a}+s2{role}", piece(a, 2, role, halves[0]), rf.at[0, role], plus)
        send(f"{a}-s2{role}", piece(a, 2, role, halves[1]), rf.at[1, role], minus)

    def send_near(a, role):
        _, _, rs, plus, minus = axes[a]
        send(f"{a}+s1{role}", piece(a, 0, role, direct[1]), rs.at[0, role, at(direct[1])], plus)
        send(f"{a}-s1{role}", piece(a, 1, role, direct[0]), rs.at[1, role, at(direct[0])], minus)

    def send_mix_x():
        send("mx1", piece("x", 0, 0, by_z[1]), mix.at[1], p1)
        send("mx0", piece("x", 1, 0, by_z[0]), mix.at[0], p1)

    hop = [xrs.at[1, 0, at(by_z[0])], xrs.at[0, 0, at(by_z[1])]]
    end = [yrs.at[1, 0, at(by_z[0])], yrs.at[0, 0, at(by_z[1])]]

    def send_mix_y():
        send("my1", piece("y", 0, 0, by_z[1]), hop[1], p2)
        send("my0", piece("y", 1, 0, by_z[0]), hop[0], p2)

    def pass_mix_y(h):
        arrived(f"my{h}", hop[h])
        send(f"mz{h}", hop[h], end[h], p1)

    def send_mixed(a, h):
        _, _, rs, plus, minus = axes[a]
        term = mix.at[h] if a == "x" else end[h]
        arrived(f"mx{h}" if a == "x" else f"mz{h}", term)
        mine = piece(a, 1 - h, 1, by_z[h])
        add_to(mine, term)
        send(f"{a}m{h}", mine, rs.at[1 - h, 1, at(by_z[h])], plus if h else minus)

    def send_sum(a, role):
        _, rf, rs, plus, minus = axes[a]
        for d, (sign, peer) in enumerate((("+", plus), ("-", minus))):
            arrived(f"{a}{sign}s2{role}", rf.at[d, role])
            mine = piece(a, d, role, halves[d])
            add_to(mine, rf.at[d, role])
            send(f"{a}{sign}s0{role}", mine, rs.at[d, role, at(halves[d])], peer)

    def sums_arrived(a, role):
        rs = axes[a][2]
        for d, sign in enumerate("+-"):
            arrived(f"{a}{sign}s1{role}", rs.at[d, role, at(direct[1 - d])])
            if role:
                arrived(f"{a}m{1 - d}", rs.at[d, role, at(by_z[1 - d])])
            arrived(f"{a}{sign}s0{role}", rs.at[d, role, at(halves[d])])

    x_part(2)
    send_far("x", 0)
    loss_finish(0)
    loss_start(1)
    arrived("w", w2.at[1])
    y_part(2)
    loss_finish(1)
    send_far("y", 0)
    loss_start(2)
    send("o4", prow(py[3], oh), orow(py[3], oh), sib)
    send("o5", prow(py[1], oh), orow(py[1], oh), sib)
    send("o6", prow(py[2], oh), orow(py[2], oh), sib)
    x_part(1)
    x_part(3)
    send_near("x", 0)
    send_mix_x()
    loss_finish(2)
    loss_start(3)
    y_part(1)
    y_part(3)
    send_near("y", 0)
    send_mix_y()
    loss_finish(3)
    loss_start(4)
    send_sum("x", 0)
    send_sum("y", 0)
    loss_finish(4)
    loss_start(5)
    send_far("x", 1)
    send_far("y", 1)
    send_near("x", 1)
    send_near("y", 1)

    for a in "xy":
        sent(f"{a}+s20")
        sent(f"{a}-s20")

    hand_x = xs.at[2, rows(oz * p_dev, p_dev)]
    hand_y = ys.at[2, rows(oh * p_dev, p_dev)]

    def split(first, value):
        low, high = value[:p_dev], value[p_dev:]
        return jnp.where(first, low, high), jnp.where(first, high, low)

    def store_x(cols, value):
        mine, handed = split(zl == 0, value)
        s[:, cols] = mine
        hand_x[:, cols] = handed.astype(BF16)

    def store_y(cols, value):
        mine, handed = split(zh == 0, value)
        s[:, cols] += mine
        hand_y[:, cols] = handed.astype(BF16)

    loop_part(x * 2 * p_dev, 2 * p_dev, store_x)
    pool_weights(y, 0, 0)
    pool_weights(y, 1, p_dev)
    pool_part(2 * p_dev, store_y)
    pass_mix_y(1)
    send_mixed("x", 1)
    send_mixed("x", 0)

    for c in range(blocks):
        wall[:, c * p_dev:(c + 1) * p_dev] = (
            wt[c * p_dev:(c + 1) * p_dev, :].astype(F32).T.astype(BF16)
        )
    loop_rows = blocks * p_dev

    @pl.loop(0, q_dev // 128)
    def _(n):
        part = rows(n * 128, 128, 128)
        names = jnp.broadcast_to(ids[0, 0:1, part].astype(F32), (128, 128)).T
        values = jnp.broadcast_to(w2[0, 0:1, part], (128, 128)).T
        lane = lax.broadcasted_iota(jnp.int32, (128, 128), 1)
        for k in range(2):
            cc = core if k == 0 else 1 - core
            for slot in range(8):
                base = pool_base(slot // 2, slot % 2, cc)
                at = loop_rows + (k * 8 + slot) * p_dev
                wall[part, at:at + p_dev] = jnp.where(
                    names == (lane + base).astype(F32), values, 0.0
                ).astype(BF16)

    arrived("oo", orow(y, zh))
    arrived("o3", orow(py[3], zh))
    arrived("o1", orow(py[1], zh))
    arrived("op", orow(y, oh))
    arrived("o2", orow(py[2], zh))
    arrived("o4", orow(py[3], oh))
    arrived("o5", orow(py[1], oh))
    arrived("o6", orow(py[2], oh))

    tile = dqt.shape[2]
    tiles = width // tile
    pool_rows = pbuf.shape[0]

    def tile_in(t):
        k = lax.rem(t, 2)
        return pltpu.make_async_copy(
            other_hbm.at[:, rows(t * tile, tile, tile)], otile.at[k], csem.at[k]
        )

    def tile_out(t):
        k = lax.rem(t, 2)
        return pltpu.make_async_copy(
            dqt.at[k], dq_hbm.at[:, rows(t * tile, tile, tile)], csem.at[2 + k]
        )

    tile_in(0).start()

    def query_slope(first, last):
        @pl.loop(first, last)
        def _(t):
            k = lax.rem(t, 2)

            @pl.when(t + 1 < tiles)
            def _():
                tile_in(t + 1).start()

            @pl.when(t >= 2)
            def _():
                tile_out(t - 2).wait()

            cols = rows(t * tile, tile, tile)
            tile_in(t).wait()
            acc = jnp.dot(
                wall[:, 0:loop_rows], lbuf[:, cols], preferred_element_type=F32
            )
            acc += jnp.dot(
                wall[:, loop_rows:loop_rows + pool_rows], pbuf[:, cols],
                preferred_element_type=F32,
            )
            acc += jnp.dot(
                wall[:, loop_rows + pool_rows:], otile[k], preferred_element_type=F32
            )
            dqt[k] = (scale * acc).astype(BF16)
            tile_out(t).start()

    query_slope(0, tiles // 4)
    pass_mix_y(0)
    loss_finish(5)
    loss_start(6)
    query_slope(tiles // 4, tiles * 3 // 8)

    parts = [pl.ds(0, moved), pl.ds(moved, p_dev - 2 * moved), pl.ds(p_dev - moved, moved)]
    signs = [(0,), (0, 1), (1,)]
    sums_arrived("y", 0)
    for k, part in enumerate(parts):
        add_to(hand_y.at[part], *(yrs.at[d, 0, part] for d in signs[k]))
        send(f"zh{k}", hand_y.at[part], zrh.at[part], p2)
    send_mixed("y", 1)
    query_slope(tiles * 3 // 8, tiles * 5 // 8)
    sums_arrived("x", 0)
    send_mixed("y", 0)
    send_sum("x", 1)
    send_sum("y", 1)
    for k, part in enumerate(parts):
        arrived(f"zh{k}", zrh.at[part])
        add_to(hand_x.at[part], zrh.at[part], *(xrs.at[d, 0, part] for d in signs[k]))
        send(f"zl{k}", hand_x.at[part], zrl.at[part], p1)
        query_slope(tiles * (10 + 2 * k) // 16, tiles * (12 + 2 * k) // 16)
    loss_finish(6)
    loss_ref[...] = lsum[...]

    sums_arrived("x", 1)
    sums_arrived("y", 1)
    sent("y+s21")
    sent("y-s21")
    result = ys.at[2, rows(zh * p_dev, p_dev)]
    outs = []
    for h, part in enumerate(parts):
        arrived(f"zl{h}", zrl.at[part])

        @pl.loop(0, width // step, unroll=2)
        def _(t):
            cols = rows(t * step, step, step)
            result[part, cols] = (
                s[part, cols]
                + xrs[0, 1, part, cols].astype(F32)
                + xrs[1, 1, part, cols].astype(F32)
                + yrs[0, 1, part, cols].astype(F32)
                + yrs[1, 1, part, cols].astype(F32)
                + zrl[part, cols].astype(F32)
            ).astype(BF16)

        copy = pltpu.make_async_copy(result.at[part], dp_hbm.at[part], csem.at[4 + h])
        copy.start()
        outs.append(copy)
    tile_out(tiles - 2).wait()
    tile_out(tiles - 1).wait()
    for copy in outs:
        copy.wait()
    for name in list(started):
        sent(name)


def shards(queries, passages, positive_ids, hard_ids):
    q_dev, width = queries.shape
    p_dev = passages.shape[0]
    half = p_dev // 2
    moved = half * 3 // 4
    vmem = pltpu.VMEM
    hbm = pl.BlockSpec(memory_space=pl.ANY)
    block = pl.BlockSpec(memory_space=pltpu.VMEM)
    loss, slope, grad, _ = pl.pallas_call(
        kernel,
        out_shape=(
            jax.ShapeDtypeStruct((8, 128), F32),
            jax.ShapeDtypeStruct((q_dev, width), BF16),
            jax.ShapeDtypeStruct((p_dev, width), BF16),
            jax.ShapeDtypeStruct((8 * p_dev, width), BF16),
        ),
        in_specs=[hbm, hbm, block, block],
        out_specs=(block, hbm, hbm, hbm),
        scratch_shapes=[
            vmem((8 * p_dev, width), BF16),
            vmem((8 * p_dev, width), BF16),
            vmem((2 * q_dev, width), BF16),
            vmem((p_dev, 8 * q_dev), F32),
            vmem((8 * p_dev, q_dev), BF16),
            vmem((q_dev, 24 * p_dev), BF16),
            vmem((2 * p_dev, 2 * q_dev), BF16),
            vmem((3, 2 * p_dev, width), BF16),
            vmem((3, 2 * p_dev, width), BF16),
            vmem((2, 2, half, width), BF16),
            vmem((2, 2, p_dev, width), BF16),
            vmem((2, 2, half, width), BF16),
            vmem((2, 2, p_dev, width), BF16),
            vmem((p_dev, width), BF16),
            vmem((p_dev, width), BF16),
            vmem((2, moved, width), BF16),
            vmem((2, moved, width), BF16),
            vmem((2, 8, q_dev), jnp.int32),
            vmem((2, 8, q_dev), F32),
            vmem((8, q_dev), F32),
            vmem((2, 8, q_dev), F32),
            vmem((8, q_dev), F32),
            vmem((8, 128), F32),
            vmem((7, 8, 128), F32),
            vmem((7, 8, 128), F32),
            vmem((2, 8 * p_dev, 256), BF16),
            vmem((2, q_dev, 256), BF16),
            pltpu.SemaphoreType.DMA((COPIES,)),
            pltpu.SemaphoreType.DMA((COPIES,)),
            pltpu.SemaphoreType.DMA((7,)),
        ],
        compiler_params=pltpu.CompilerParams(
            collective_id=0, has_side_effects=True, vmem_limit_bytes=63 * 2**20
        ),
        cost_estimate=pl.CostEstimate(
            flops=2 * q_dev * width * 9 * 8 * p_dev,
            bytes_accessed=40 * 2**20,
            transcendentals=2 * 8 * p_dev * q_dev,
        ),
    )(
        queries,
        passages,
        positive_ids.reshape(1, q_dev),
        hard_ids.reshape(1, q_dev),
    )
    total = q_dev * lax.axis_size("blk") * lax.axis_size("grp")
    return loss[0, 0] / total, slope, grad


def solution(mesh):
    return jax.shard_map(
        shards,
        mesh=mesh,
        in_specs=(
            P(("blk", "grp"), None),
            P(("blk", "grp"), None),
            P(("blk", "grp")),
            P(("blk", "grp"), None),
        ),
        out_specs=(P(), P(("blk", "grp"), None), P(("blk", "grp"), None)),
        check_vma=False,
    )
```

```python
import functools

import jax
import jax.numpy as jnp
from jax import lax
from jax.experimental import pallas as pl
from jax.experimental.pallas import tpu as pltpu
from jax.sharding import PartitionSpec as P

logit_scaling_coefficient = 20.0
MESH = pl.DeviceIdType.MESH
BF16 = jnp.bfloat16
F32 = jnp.float32
COPIES = 112
NT = (((1,), (1,)), ((), ()))


def rows(start, size, multiple=64):
    return pl.ds(pl.multiple_of(start, multiple), size)


def kernel(
    q_hbm, p_hbm, pos_ref, hid_ref,
    loss_ref, dq_hbm, dp_hbm, other_hbm,
    lbuf, pbuf, qbuf, s, wt, wall, wht, xs, ys, xrf, xrs, yrf, yrs, zrh, zrl, via, mix,
    ids, hs, hin, w2, top, run, hit, lsum, lsend, lrecv, otile, dqt,
    ssem, rsem, csem,
):
    q_dev, width = q_hbm.shape
    p_dev = p_hbm.shape[0]
    half = p_dev // 2
    scale = logit_scaling_coefficient

    b = lax.axis_index("blk")
    g = lax.axis_index("grp")
    x, zl = lax.div(b, 2), lax.rem(b, 2)
    zh, y, core = lax.div(g, 8), lax.div(lax.rem(g, 8), 2), lax.rem(g, 2)
    pb = x * 2 + 1 - zl
    px = [lax.rem(x + k, 4) for k in range(4)]
    py = [lax.rem(y + k, 4) for k in range(4)]
    xp = (px[1] * 2 + zl, g)
    xm = (px[3] * 2 + zl, g)
    yp = (b, zh * 8 + py[1] * 2 + core)
    ym = (b, zh * 8 + py[3] * 2 + core)
    p1 = (pb, g)
    p2 = (pb, lax.rem(g + 8, 16))
    sib = (b, zh * 8 + y * 2 + 1 - core)

    number = {}
    started = {}

    def describe(name, src, dst, peer):
        k = number.setdefault(name, len(number))
        return pltpu.make_async_remote_copy(
            src_ref=src, dst_ref=dst, send_sem=ssem.at[k], recv_sem=rsem.at[k],
            device_id=peer, device_id_type=MESH,
        )

    def send(name, src, dst, peer):
        copy = describe(name, src, dst, peer)
        copy.start()
        started[name] = copy

    def sent(name):
        started.pop(name).wait_send()

    def arrived(name, dst):
        describe(name, dst, dst, sib).wait_recv()

    quarter = half // 2
    moved = half * 3 // 4
    halves = [(0, half), (half, half)]
    by_z = [(0, moved), (p_dev - moved, moved)]
    direct = [(moved, half - moved), (half, half - moved)]
    whole = (0, p_dev)

    def lrow(xx, zz, part=whole):
        return lbuf.at[rows((xx * 2 + zz) * p_dev + part[0], part[1], 16)]

    def prow(yy, zz, part=whole):
        return pbuf.at[rows((yy * 2 + zz) * p_dev + part[0], part[1], 16)]

    def orow(yy, zz):
        return other_hbm.at[rows((yy * 2 + zz) * p_dev, p_dev)]

    local = [
        pltpu.make_async_copy(q_hbm, qbuf.at[pl.ds(0, q_dev)], csem.at[0]),
        pltpu.make_async_copy(p_hbm, lrow(x, zl), csem.at[1]),
        pltpu.make_async_copy(p_hbm, prow(y, zh), csem.at[2]),
    ]
    for copy in local:
        copy.start()
    ids[0] = jnp.broadcast_to(hid_ref[...], ids.shape[1:])
    hs[...] = jnp.zeros(hs.shape, F32)
    top[...] = jnp.full(top.shape, -jnp.inf, F32)
    run[...] = jnp.zeros(run.shape, F32)
    hit[...] = jnp.zeros(hit.shape, F32)

    barrier = pltpu.get_barrier_semaphore()
    for peer in (xp, xm, yp, ym, p1, p2, sib):
        pl.semaphore_signal(barrier, inc=1, device_id=peer, device_id_type=MESH)
    pl.semaphore_wait(barrier, 7)

    own = [p_hbm.at[pl.ds(h * half, half)] for h in range(2)]
    quarters = [(k * quarter, quarter) for k in range(4)]

    for k in range(4):
        send(f"z{k}", p_hbm.at[pl.ds(k * quarter, quarter)], lrow(x, zl, quarters[k]), p1)
    for h in range(2):
        r = 1 - h
        send(f"x+o{h}", own[h], lrow(x, zl, halves[h]), xp)
        send(f"x-o{r}", own[r], lrow(x, zl, halves[r]), xm)
        send(f"y+o{h}", own[h], prow(y, zh, halves[h]), yp)
        send(f"y-o{r}", own[r], prow(y, zh, halves[r]), ym)
    send("ids", ids.at[0], ids.at[1], sib)
    send("q", q_hbm, qbuf.at[pl.ds(q_dev, q_dev)], sib)

    def score_loop(xx, zz):
        c = xx * 2 + zz
        acc = scale * lax.dot_general(
            lbuf[rows(c * p_dev, p_dev), :], qbuf[pl.ds(0, q_dev), :], NT,
            preferred_element_type=F32,
        )
        s[:, rows(c * q_dev, q_dev, q_dev)] = acc
        old = top[0:1]
        peak = jnp.maximum(old, jnp.max(acc, axis=0, keepdims=True))
        total = run[0:1] * jnp.exp(old - peak) + jnp.sum(
            jnp.exp(acc - peak), axis=0, keepdims=True
        )
        row = lax.broadcasted_iota(jnp.int32, acc.shape, 0) + c * p_dev
        top[...] = jnp.broadcast_to(peak, top.shape)
        run[...] = jnp.broadcast_to(total, run.shape)
        hit[...] += jnp.sum(jnp.where(row == pos_ref[...], acc, 0.0), axis=0, keepdims=True)

    def pool_base(yy, zz, cc):
        return (zz * 8 + yy * 2 + cc) * p_dev

    def score_pool(yy, zz):
        slot = yy * 2 + zz
        base = pool_base(yy, zz, core)
        for k in range(2):
            acc = lax.dot_general(
                pbuf[rows(slot * p_dev, p_dev), :], qbuf[pl.ds(k * q_dev, q_dev), :], NT,
                preferred_element_type=F32,
            )
            row = lax.broadcasted_iota(jnp.int32, acc.shape, 0) + base
            named = jnp.where(row == ids[k, 0:1, :], scale * acc, 0.0)
            hs[k] += jnp.sum(named, axis=0, keepdims=True)

    oz, oh = 1 - zl, 1 - zh

    for copy in local:
        copy.wait()
    send("oo", prow(y, zh), orow(y, zh), sib)
    score_loop(x, zl)

    def pass_x(name, xx, zz, part, peer):
        send(name, lrow(xx, zz, part), lrow(xx, zz, part), peer)

    def pass_y(name, yy, zz, part, peer):
        send(name, prow(yy, zz, part), prow(yy, zz, part), peer)

    def pass_z(k):
        arrived(f"z{k}", lrow(x, oz, quarters[k]))
        send(f"h{k}", lrow(x, oz, quarters[k]), prow(y, zh, quarters[k]), p2)

    pass_z(0)
    pass_z(1)
    arrived("x+o0", lrow(px[3], zl, halves[0]))
    pass_x("x+f", px[3], zl, halves[0], xp)
    arrived("x-o1", lrow(px[1], zl, halves[1]))
    pass_x("x-f", px[1], zl, halves[1], xm)
    arrived("y+o0", prow(py[3], zh, halves[0]))
    pass_y("y+f", py[3], zh, halves[0], yp)
    arrived("y-o1", prow(py[1], zh, halves[1]))
    pass_y("y-f", py[1], zh, halves[1], ym)
    pass_x("x+p0", x, oz, halves[0], xp)
    arrived("ids", ids.at[1])
    arrived("q", qbuf.at[pl.ds(q_dev, q_dev)])
    score_pool(y, zh)

    pass_z(2)
    arrived("h0", prow(y, oh, quarters[0]))
    arrived("h1", prow(y, oh, quarters[1]))
    pass_y("y+p0", y, oh, halves[0], yp)
    pass_z(3)
    pass_x("x-p1", x, oz, halves[1], xm)
    pass_x("x+p1", x, oz, direct[1], xp)
    pass_x("x-p0", x, oz, direct[0], xm)
    arrived("x+o1", lrow(px[3], zl, halves[1]))
    pass_x("zx1", px[3], zl, by_z[1], p1)
    arrived("x-o0", lrow(px[1], zl, halves[0]))
    pass_x("zx0", px[1], zl, by_z[0], p1)
    arrived("y+o1", prow(py[3], zh, halves[1]))
    send("ty1", prow(py[3], zh, by_z[1]), via.at[1], p2)
    arrived("y-o0", prow(py[1], zh, halves[0]))
    send("ty0", prow(py[1], zh, by_z[0]), via.at[0], p2)
    send("o3", prow(py[3], zh), orow(py[3], zh), sib)
    send("o1", prow(py[1], zh), orow(py[1], zh), sib)
    score_loop(x, oz)
    score_loop(px[3], zl)
    score_loop(px[1], zl)
    arrived("h2", prow(y, oh, quarters[2]))
    arrived("h3", prow(y, oh, quarters[3]))
    pass_y("y-p1", y, oh, halves[1], ym)
    pass_y("y+p1", y, oh, direct[1], yp)
    pass_y("y-p0", y, oh, direct[0], ym)
    send("op", prow(y, oh), orow(y, oh), sib)
    score_pool(py[3], zh)
    score_pool(py[1], zh)
    arrived("x+f", lrow(px[2], zl, halves[0]))
    arrived("x-f", lrow(px[2], zl, halves[1]))
    score_loop(px[2], zl)
    arrived("ty1", via.at[1])
    send("tz1", via.at[1], prow(py[3], oh, by_z[1]), p1)
    score_pool(y, oh)
    arrived("y+f", prow(py[2], zh, halves[0]))
    arrived("y-f", prow(py[2], zh, halves[1]))
    send("o2", prow(py[2], zh), orow(py[2], zh), sib)
    score_pool(py[2], zh)
    arrived("x+p0", lrow(px[3], oz, halves[0]))
    pass_x("x+g", px[3], oz, halves[0], xp)
    arrived("x-p1", lrow(px[1], oz, halves[1]))
    pass_x("x-g", px[1], oz, halves[1], xm)
    arrived("y+p0", prow(py[3], oh, halves[0]))
    pass_y("y+g", py[3], oh, halves[0], yp)
    arrived("y-p1", prow(py[1], oh, halves[1]))
    pass_y("y-g", py[1], oh, halves[1], ym)
    arrived("ty0", via.at[0])
    send("tz0", via.at[0], prow(py[1], oh, by_z[0]), p1)
    arrived("x+p1", lrow(px[3], oz, direct[1]))
    arrived("zx1", lrow(px[3], oz, by_z[1]))
    score_loop(px[3], oz)
    arrived("x-p0", lrow(px[1], oz, direct[0]))
    arrived("zx0", lrow(px[1], oz, by_z[0]))
    score_loop(px[1], oz)
    arrived("y+p1", prow(py[3], oh, direct[1]))
    arrived("tz1", prow(py[3], oh, by_z[1]))
    score_pool(py[3], oh)
    arrived("y-p0", prow(py[1], oh, direct[0]))
    arrived("tz0", prow(py[1], oh, by_z[0]))
    score_pool(py[1], oh)
    arrived("y+g", prow(py[2], oh, halves[0]))
    arrived("y-g", prow(py[2], oh, halves[1]))
    score_pool(py[2], oh)
    send("hs", hs.at[1], hin, sib)
    arrived("x+g", lrow(px[2], oz, halves[0]))
    arrived("x-g", lrow(px[2], oz, halves[1]))
    score_loop(px[2], oz)

    arrived("hs", hin)
    hard = hs[0, 0:1, :] + hin[0:1, :]
    peak = jnp.maximum(top[0:1], hard)
    total = run[0:1] * jnp.exp(top[0:1] - peak) + jnp.exp(hard - peak)
    log_total = peak + jnp.log(total)
    w_hard = jnp.exp(hard - log_total).astype(BF16).astype(F32)
    w2[0] = jnp.broadcast_to(w_hard, w2.shape[1:])
    send("w", w2.at[0], w2.at[1], sib)
    lsum[...] = jnp.broadcast_to(
        jnp.sum(log_total - hit[0:1], axis=1, keepdims=True), lsum.shape
    )
    blocks = s.shape[1] // q_dev

    def weigh(xx, zz):
        c = xx * 2 + zz
        part = s[:, rows(c * q_dev, q_dev, q_dev)]
        row = lax.broadcasted_iota(jnp.int32, part.shape, 0) + c * p_dev
        one = jnp.where(row == pos_ref[...], 1.0, 0.0)
        wt[rows(c * p_dev, p_dev), :] = (jnp.exp(part - log_total) - one).astype(BF16)

    loss_peers = [
        (lax.rem(b + 2 + 4 * lax.rem(x, 2), 8), g),
        (b, zh * 8 + lax.rem(y + 1 + 2 * lax.rem(y, 2), 4) * 2 + core),
        p1,
        p2,
        sib,
        ((3 - x) * 2 + zl, g),
        (b, zh * 8 + (3 - y) * 2 + core),
    ]

    def loss_start(k):
        lsend[k] = lsum[...]
        send(f"l{k}", lsend.at[k], lrecv.at[k], loss_peers[k])

    def loss_finish(k):
        arrived(f"l{k}", lrecv.at[k])
        lsum[...] = lsend[k] + lrecv[k]

    loss_start(0)

    step = 512

    def columns(count):
        return width // 2 if count == p_dev else step

    def loop_part(start, count, store):
        n = columns(count)

        @pl.loop(0, width // n, unroll=min(4, width // n // 2))
        def _(t):
            cols = rows(t * n, n, n)
            store(cols, scale * jnp.dot(
                wt[rows(start, count), :], qbuf[pl.ds(0, q_dev), cols],
                preferred_element_type=F32,
            ))

    def pool_weights(yy, zz, at):
        base = pool_base(yy, zz, core)
        for k in range(2):
            row = lax.broadcasted_iota(jnp.int32, (p_dev, q_dev), 0) + base
            wht[at:at + p_dev, k * q_dev:(k + 1) * q_dev] = jnp.where(
                row == ids[k, 0:1, :], w2[k, 0:1, :], 0.0
            ).astype(BF16)

    def pool_part(count, store):
        n = columns(count)

        @pl.loop(0, width // n, unroll=min(4, width // n // 2))
        def _(t):
            cols = rows(t * n, n, n)
            store(cols, scale * jnp.dot(
                wht[pl.ds(0, count), :], qbuf[:, cols], preferred_element_type=F32
            ))

    z_of = {"x": (oz, zl), "y": (oh, zh)}
    axes = {"x": (xs, xrf, xrs, xp, xm), "y": (ys, yrf, yrs, yp, ym)}

    def piece(a, slot, role, part):
        return axes[a][0].at[slot, rows(z_of[a][role] * p_dev + part[0], part[1], 16)]

    def at(part):
        return pl.ds(part[0], part[1])

    def add_to(dst, *terms):
        @pl.loop(0, width // step, unroll=2)
        def _(t):
            cols = rows(t * step, step, step)
            total = dst[:, cols].astype(F32)
            for term in terms:
                total += term[:, cols].astype(F32)
            dst[:, cols] = total.astype(BF16)

    def send_far(a, role):
        _, rf, _, plus, minus = axes[a]
        send(f"{a}+s2{role}", piece(a, 2, role, halves[0]), rf.at[0, role], plus)
        send(f"{a}-s2{role}", piece(a, 2, role, halves[1]), rf.at[1, role], minus)

    def send_near(a, role):
        _, _, rs, plus, minus = axes[a]
        send(f"{a}+s1{role}", piece(a, 0, role, direct[1]), rs.at[0, role, at(direct[1])], plus)
        send(f"{a}-s1{role}", piece(a, 1, role, direct[0]), rs.at[1, role, at(direct[0])], minus)

    def send_mix_x():
        send("mx1", piece("x", 0, 0, by_z[1]), mix.at[1], p1)
        send("mx0", piece("x", 1, 0, by_z[0]), mix.at[0], p1)

    hop = [xrs.at[1, 0, at(by_z[0])], xrs.at[0, 0, at(by_z[1])]]
    end = [yrs.at[1, 0, at(by_z[0])], yrs.at[0, 0, at(by_z[1])]]

    def send_mix_y():
        send("my1", piece("y", 0, 0, by_z[1]), hop[1], p2)
        send("my0", piece("y", 1, 0, by_z[0]), hop[0], p2)

    def pass_mix_y(h):
        arrived(f"my{h}", hop[h])
        send(f"mz{h}", hop[h], end[h], p1)

    def send_mixed(a, h):
        _, _, rs, plus, minus = axes[a]
        term = mix.at[h] if a == "x" else end[h]
        arrived(f"mx{h}" if a == "x" else f"mz{h}", term)
        mine = piece(a, 1 - h, 1, by_z[h])
        add_to(mine, term)
        send(f"{a}m{h}", mine, rs.at[1 - h, 1, at(by_z[h])], plus if h else minus)

    def send_sum(a, role):
        _, rf, rs, plus, minus = axes[a]
        for d, (sign, peer) in enumerate((("+", plus), ("-", minus))):
            arrived(f"{a}{sign}s2{role}", rf.at[d, role])
            mine = piece(a, d, role, halves[d])
            add_to(mine, rf.at[d, role])
            send(f"{a}{sign}s0{role}", mine, rs.at[d, role, at(halves[d])], peer)

    def sums_arrived(a, role):
        rs = axes[a][2]
        for d, sign in enumerate("+-"):
            arrived(f"{a}{sign}s1{role}", rs.at[d, role, at(direct[1 - d])])
            if role:
                arrived(f"{a}m{1 - d}", rs.at[d, role, at(by_z[1 - d])])
            arrived(f"{a}{sign}s0{role}", rs.at[d, role, at(halves[d])])

    def store_to(ref):
        def store(cols, value):
            ref[:, cols] = value.astype(BF16)
        return store

    place = {1: 0, 3: 1, 2: 2}

    def x_part(k, role):
        zz = z_of["x"][role]
        weigh(px[k], zz)
        loop_part((px[k] * 2 + zz) * p_dev, p_dev, store_to(piece("x", place[k], role, whole)))

    def y_part(k, role):
        pool_weights(py[k], z_of["y"][role], 0)
        pool_part(p_dev, store_to(piece("y", place[k], role, whole)))

    x_part(2, 0)
    send_far("x", 0)
    loss_finish(0)
    loss_start(1)
    arrived("w", w2.at[1])
    y_part(2, 0)
    loss_finish(1)
    send_far("y", 0)
    loss_start(2)
    send("o4", prow(py[3], oh), orow(py[3], oh), sib)
    send("o5", prow(py[1], oh), orow(py[1], oh), sib)
    send("o6", prow(py[2], oh), orow(py[2], oh), sib)
    x_part(1, 0)
    x_part(3, 0)
    send_near("x", 0)
    loss_finish(2)
    loss_start(3)
    send_mix_x()
    y_part(1, 0)
    y_part(3, 0)
    send_near("y", 0)
    loss_finish(3)
    send_mix_y()
    loss_start(4)
    for k in (2, 1, 3):
        x_part(k, 1)
    weigh(x, 0)
    weigh(x, 1)
    send_sum("x", 0)
    y_part(2, 1)
    send_sum("y", 0)
    loss_finish(4)
    loss_start(5)
    send_far("x", 1)
    send_far("y", 1)
    y_part(1, 1)
    y_part(3, 1)
    send_near("x", 1)
    send_near("y", 1)

    for a in "xy":
        sent(f"{a}+s20")
        sent(f"{a}-s20")

    hand_x = xs.at[2, rows(oz * p_dev, p_dev)]
    hand_y = ys.at[2, rows(oh * p_dev, p_dev)]

    def split(first, value):
        low, high = value[:p_dev], value[p_dev:]
        return jnp.where(first, low, high), jnp.where(first, high, low)

    def store_x(cols, value):
        mine, handed = split(zl == 0, value)
        s[:, cols] = mine
        hand_x[:, cols] = handed.astype(BF16)

    def store_y(cols, value):
        mine, handed = split(zh == 0, value)
        s[:, cols] += mine
        hand_y[:, cols] = handed.astype(BF16)

    loop_part(x * 2 * p_dev, 2 * p_dev, store_x)
    pool_weights(y, 0, 0)
    pool_weights(y, 1, p_dev)
    pool_part(2 * p_dev, store_y)
    pass_mix_y(1)
    send_mixed("x", 1)
    send_mixed("x", 0)

    for c in range(blocks):
        wall[:, c * p_dev:(c + 1) * p_dev] = (
            wt[c * p_dev:(c + 1) * p_dev, :].astype(F32).T.astype(BF16)
        )
    loop_rows = blocks * p_dev

    @pl.loop(0, q_dev // 128)
    def _(n):
        part = rows(n * 128, 128, 128)
        names = jnp.broadcast_to(ids[0, 0:1, part].astype(F32), (128, 128)).T
        values = jnp.broadcast_to(w2[0, 0:1, part], (128, 128)).T
        lane = lax.broadcasted_iota(jnp.int32, (128, 128), 1)
        for k in range(2):
            cc = core if k == 0 else 1 - core
            for slot in range(8):
                base = pool_base(slot // 2, slot % 2, cc)
                at = loop_rows + (k * 8 + slot) * p_dev
                wall[part, at:at + p_dev] = jnp.where(
                    names == (lane + base).astype(F32), values, 0.0
                ).astype(BF16)

    arrived("oo", orow(y, zh))
    arrived("o3", orow(py[3], zh))
    arrived("o1", orow(py[1], zh))
    arrived("op", orow(y, oh))
    arrived("o2", orow(py[2], zh))
    arrived("o4", orow(py[3], oh))
    arrived("o5", orow(py[1], oh))
    arrived("o6", orow(py[2], oh))

    tile = dqt.shape[2]
    tiles = width // tile
    pool_rows = pbuf.shape[0]

    def tile_in(t):
        k = lax.rem(t, 2)
        return pltpu.make_async_copy(
            other_hbm.at[:, rows(t * tile, tile, tile)], otile.at[k], csem.at[k]
        )

    def tile_out(t):
        k = lax.rem(t, 2)
        return pltpu.make_async_copy(
            dqt.at[k], dq_hbm.at[:, rows(t * tile, tile, tile)], csem.at[2 + k]
        )

    tile_in(0).start()

    def query_slope(first, last):
        @pl.loop(first, last)
        def _(t):
            k = lax.rem(t, 2)

            @pl.when(t + 1 < tiles)
            def _():
                tile_in(t + 1).start()

            @pl.when(t >= 2)
            def _():
                tile_out(t - 2).wait()

            cols = rows(t * tile, tile, tile)
            tile_in(t).wait()
            acc = jnp.dot(
                wall[:, 0:loop_rows], lbuf[:, cols], preferred_element_type=F32
            )
            acc += jnp.dot(
                wall[:, loop_rows:loop_rows + pool_rows], pbuf[:, cols],
                preferred_element_type=F32,
            )
            acc += jnp.dot(
                wall[:, loop_rows + pool_rows:], otile[k], preferred_element_type=F32
            )
            dqt[k] = (scale * acc).astype(BF16)
            tile_out(t).start()

    query_slope(0, tiles // 4)
    pass_mix_y(0)
    loss_finish(5)
    loss_start(6)
    query_slope(tiles // 4, tiles * 3 // 8)

    parts = [pl.ds(0, moved), pl.ds(moved, p_dev - 2 * moved), pl.ds(p_dev - moved, moved)]
    signs = [(0,), (0, 1), (1,)]
    sums_arrived("y", 0)
    for k, part in enumerate(parts):
        add_to(hand_y.at[part], *(yrs.at[d, 0, part] for d in signs[k]))
        send(f"zh{k}", hand_y.at[part], zrh.at[part], p2)
    send_mixed("y", 1)
    query_slope(tiles * 3 // 8, tiles * 5 // 8)
    sums_arrived("x", 0)
    send_mixed("y", 0)
    send_sum("x", 1)
    send_sum("y", 1)
    for k, part in enumerate(parts):
        arrived(f"zh{k}", zrh.at[part])
        add_to(hand_x.at[part], zrh.at[part], *(xrs.at[d, 0, part] for d in signs[k]))
        send(f"zl{k}", hand_x.at[part], zrl.at[part], p1)
        query_slope(tiles * (10 + 2 * k) // 16, tiles * (12 + 2 * k) // 16)
    loss_finish(6)
    loss_ref[0] = jnp.max(lsum[...]) / (q_dev * lax.axis_size("blk") * lax.axis_size("grp"))

    sums_arrived("x", 1)
    for h, part in enumerate(parts):
        arrived(f"zl{h}", zrl.at[part])

        @pl.loop(0, width // step, unroll=2)
        def _(t):
            cols = rows(t * step, step, step)
            s[part, cols] += (
                xrs[0, 1, part, cols].astype(F32)
                + xrs[1, 1, part, cols].astype(F32)
                + zrl[part, cols].astype(F32)
            )

    sums_arrived("y", 1)
    sent("y+s21")
    sent("y-s21")
    result = ys.at[2, rows(zh * p_dev, p_dev)]
    outs = []
    for h, part in enumerate(parts):
        @pl.loop(0, width // step, unroll=2)
        def _(t):
            cols = rows(t * step, step, step)
            result[part, cols] = (
                s[part, cols]
                + yrs[0, 1, part, cols].astype(F32)
                + yrs[1, 1, part, cols].astype(F32)
            ).astype(BF16)

        copy = pltpu.make_async_copy(result.at[part], dp_hbm.at[part], csem.at[4 + h])
        copy.start()
        outs.append(copy)
    tile_out(tiles - 2).wait()
    tile_out(tiles - 1).wait()
    for copy in outs:
        copy.wait()
    for name in list(started):
        sent(name)


def write(loss_in, slope_in, grad_in, loss_out, slope_out, grad_out, loss, slope, grad, sem):
    pieces = 4
    n = slope.shape[0] // pieces
    moves = [
        (slope_in.at[part], slope.at[part], slope_out.at[part])
        for part in (pl.ds(k * n, n) for k in range(pieces))
    ]
    moves.insert(1, (grad_in, grad, grad_out))
    moves.insert(2, (loss_in, loss, loss_out))
    reads = [
        pltpu.make_async_copy(src, buf, sem.at[0, k]) for k, (src, buf, _) in enumerate(moves)
    ]
    writes = [
        pltpu.make_async_copy(buf, dst, sem.at[1, k]) for k, (_, buf, dst) in enumerate(moves)
    ]
    for copy in reads:
        copy.start()
    for read, copy in zip(reads, writes):
        read.wait()
        copy.start()
    for copy in writes:
        copy.wait()


def shards(queries, passages, positive_ids, hard_ids):
    q_dev, width = queries.shape
    p_dev = passages.shape[0]
    half = p_dev // 2
    moved = half * 3 // 4
    vmem = pltpu.VMEM
    hbm = pl.BlockSpec(memory_space=pl.ANY)
    block = pl.BlockSpec(memory_space=pltpu.VMEM)
    loss, slope, grad, _ = pl.pallas_call(
        kernel,
        out_shape=(
            jax.ShapeDtypeStruct((1,), F32),
            jax.ShapeDtypeStruct((q_dev, width), BF16),
            jax.ShapeDtypeStruct((p_dev, width), BF16),
            jax.ShapeDtypeStruct((8 * p_dev, width), BF16),
        ),
        in_specs=[hbm, hbm, block, block],
        out_specs=(pl.BlockSpec(memory_space=pltpu.SMEM), hbm, hbm, hbm),
        scratch_shapes=[
            vmem((8 * p_dev, width), BF16),
            vmem((8 * p_dev, width), BF16),
            vmem((2 * q_dev, width), BF16),
            vmem((p_dev, 8 * q_dev), F32),
            vmem((8 * p_dev, q_dev), BF16),
            vmem((q_dev, 24 * p_dev), BF16),
            vmem((2 * p_dev, 2 * q_dev), BF16),
            vmem((3, 2 * p_dev, width), BF16),
            vmem((3, 2 * p_dev, width), BF16),
            vmem((2, 2, half, width), BF16),
            vmem((2, 2, p_dev, width), BF16),
            vmem((2, 2, half, width), BF16),
            vmem((2, 2, p_dev, width), BF16),
            vmem((p_dev, width), BF16),
            vmem((p_dev, width), BF16),
            vmem((2, moved, width), BF16),
            vmem((2, moved, width), BF16),
            vmem((2, 8, q_dev), jnp.int32),
            vmem((2, 8, q_dev), F32),
            vmem((8, q_dev), F32),
            vmem((2, 8, q_dev), F32),
            vmem((8, q_dev), F32),
            vmem((8, q_dev), F32),
            vmem((8, q_dev), F32),
            vmem((8, 128), F32),
            vmem((7, 8, 128), F32),
            vmem((7, 8, 128), F32),
            vmem((2, 8 * p_dev, 256), BF16),
            vmem((2, q_dev, 256), BF16),
            pltpu.SemaphoreType.DMA((COPIES,)),
            pltpu.SemaphoreType.DMA((COPIES,)),
            pltpu.SemaphoreType.DMA((7,)),
        ],
        compiler_params=pltpu.CompilerParams(
            collective_id=0, has_side_effects=True, vmem_limit_bytes=63 * 2**20
        ),
        cost_estimate=pl.CostEstimate(
            flops=2 * q_dev * width * 9 * 8 * p_dev,
            bytes_accessed=40 * 2**20,
            transcendentals=2 * 8 * p_dev * q_dev,
        ),
    )(
        queries,
        passages,
        positive_ids.reshape(1, q_dev),
        hard_ids.reshape(1, q_dev),
    )
    loss, slope, grad = pl.pallas_call(
        write,
        out_shape=(
            jax.ShapeDtypeStruct((1,), F32),
            jax.ShapeDtypeStruct(slope.shape, BF16),
            jax.ShapeDtypeStruct(grad.shape, BF16),
        ),
        in_specs=[hbm, hbm, hbm],
        out_specs=(hbm, hbm, hbm),
        scratch_shapes=[
            pltpu.SMEM((1,), F32),
            vmem(slope.shape, BF16),
            vmem(grad.shape, BF16),
            pltpu.SemaphoreType.DMA((2, 6)),
        ],
        compiler_params=pltpu.CompilerParams(vmem_limit_bytes=63 * 2**20),
    )(loss, slope, grad)
    return loss[0], slope, grad


def solution(mesh):
    return jax.shard_map(
        shards,
        mesh=mesh,
        in_specs=(
            P(("blk", "grp"), None),
            P(("blk", "grp"), None),
            P(("blk", "grp")),
            P(("blk", "grp"), None),
        ),
        out_specs=(P(), P(("blk", "grp"), None), P(("blk", "grp"), None)),
        check_vma=False,
    )
```

```python
import functools

import jax
import jax.numpy as jnp
from jax import lax
from jax.experimental import pallas as pl
from jax.experimental.pallas import tpu as pltpu
from jax.sharding import PartitionSpec as P

logit_scaling_coefficient = 20.0
MESH = pl.DeviceIdType.MESH
BF16 = jnp.bfloat16
F32 = jnp.float32
COPIES = 112
NT = (((1,), (1,)), ((), ()))


def rows(start, size, multiple=64):
    return pl.ds(pl.multiple_of(start, multiple), size)


def kernel(
    q_hbm, p_hbm, pos_ref, hid_ref,
    loss_ref, dq_hbm, dp_hbm, other_hbm,
    lbuf, pbuf, qbuf, s, wt, wall, wht, xs, ys, xrf, xrs, yrf, yrs, zrh, zrl, via, mix,
    ids, hs, hin, w2, top, run, hit, lsum, lsend, lrecv, otile, dqt,
    ssem, rsem, csem,
):
    q_dev, width = q_hbm.shape
    p_dev = p_hbm.shape[0]
    half = p_dev // 2
    scale = logit_scaling_coefficient

    b = lax.axis_index("blk")
    g = lax.axis_index("grp")
    x, zl = lax.div(b, 2), lax.rem(b, 2)
    zh, y, core = lax.div(g, 8), lax.div(lax.rem(g, 8), 2), lax.rem(g, 2)
    pb = x * 2 + 1 - zl
    px = [lax.rem(x + k, 4) for k in range(4)]
    py = [lax.rem(y + k, 4) for k in range(4)]
    xp = (px[1] * 2 + zl, g)
    xm = (px[3] * 2 + zl, g)
    yp = (b, zh * 8 + py[1] * 2 + core)
    ym = (b, zh * 8 + py[3] * 2 + core)
    p1 = (pb, g)
    p2 = (pb, lax.rem(g + 8, 16))
    sib = (b, zh * 8 + y * 2 + 1 - core)

    number = {}
    started = {}

    def describe(name, src, dst, peer):
        k = number.setdefault(name, len(number))
        return pltpu.make_async_remote_copy(
            src_ref=src, dst_ref=dst, send_sem=ssem.at[k], recv_sem=rsem.at[k],
            device_id=peer, device_id_type=MESH,
        )

    def send(name, src, dst, peer):
        copy = describe(name, src, dst, peer)
        copy.start()
        started[name] = copy

    def sent(name):
        started.pop(name).wait_send()

    def arrived(name, dst):
        describe(name, dst, dst, sib).wait_recv()

    quarter = half // 2
    moved = half * 3 // 4
    halves = [(0, half), (half, half)]
    by_z = [(0, moved), (p_dev - moved, moved)]
    direct = [(moved, half - moved), (half, half - moved)]
    whole = (0, p_dev)

    def lrow(xx, zz, part=whole):
        return lbuf.at[rows((xx * 2 + zz) * p_dev + part[0], part[1], 16)]

    def prow(yy, zz, part=whole):
        return pbuf.at[rows((yy * 2 + zz) * p_dev + part[0], part[1], 16)]

    def orow(yy, zz):
        return other_hbm.at[rows((yy * 2 + zz) * p_dev, p_dev)]

    local = [
        pltpu.make_async_copy(q_hbm, qbuf.at[pl.ds(0, q_dev)], csem.at[0]),
        pltpu.make_async_copy(p_hbm, lrow(x, zl), csem.at[1]),
        pltpu.make_async_copy(p_hbm, prow(y, zh), csem.at[2]),
    ]
    for copy in local:
        copy.start()
    ids[0] = jnp.broadcast_to(hid_ref[...], ids.shape[1:])
    hs[...] = jnp.zeros(hs.shape, F32)
    top[...] = jnp.full(top.shape, -jnp.inf, F32)
    run[...] = jnp.zeros(run.shape, F32)
    hit[...] = jnp.zeros(hit.shape, F32)

    barrier = pltpu.get_barrier_semaphore()
    for peer in (xp, xm, yp, ym, p1, p2, sib):
        pl.semaphore_signal(barrier, inc=1, device_id=peer, device_id_type=MESH)
    pl.semaphore_wait(barrier, 7)

    own = [p_hbm.at[pl.ds(h * half, half)] for h in range(2)]
    quarters = [(k * quarter, quarter) for k in range(4)]

    for k in range(4):
        send(f"z{k}", p_hbm.at[pl.ds(k * quarter, quarter)], lrow(x, zl, quarters[k]), p1)
    for h in range(2):
        r = 1 - h
        send(f"x+o{h}", own[h], lrow(x, zl, halves[h]), xp)
        send(f"x-o{r}", own[r], lrow(x, zl, halves[r]), xm)
        send(f"y+o{h}", own[h], prow(y, zh, halves[h]), yp)
        send(f"y-o{r}", own[r], prow(y, zh, halves[r]), ym)
    send("ids", ids.at[0], ids.at[1], sib)
    send("q", q_hbm, qbuf.at[pl.ds(q_dev, q_dev)], sib)

    def score_loop(xx, zz):
        c = xx * 2 + zz
        acc = scale * lax.dot_general(
            lbuf[rows(c * p_dev, p_dev), :], qbuf[pl.ds(0, q_dev), :], NT,
            preferred_element_type=F32,
        )
        s[:, rows(c * q_dev, q_dev, q_dev)] = acc
        old = top[0:1]
        peak = jnp.maximum(old, jnp.max(acc, axis=0, keepdims=True))
        total = run[0:1] * jnp.exp(old - peak) + jnp.sum(
            jnp.exp(acc - peak), axis=0, keepdims=True
        )
        row = lax.broadcasted_iota(jnp.int32, acc.shape, 0) + c * p_dev
        top[...] = jnp.broadcast_to(peak, top.shape)
        run[...] = jnp.broadcast_to(total, run.shape)
        hit[...] += jnp.sum(jnp.where(row == pos_ref[...], acc, 0.0), axis=0, keepdims=True)

    def pool_base(yy, zz, cc):
        return (zz * 8 + yy * 2 + cc) * p_dev

    def score_pool(yy, zz):
        slot = yy * 2 + zz
        base = pool_base(yy, zz, core)
        for k in range(2):
            acc = lax.dot_general(
                pbuf[rows(slot * p_dev, p_dev), :], qbuf[pl.ds(k * q_dev, q_dev), :], NT,
                preferred_element_type=F32,
            )
            row = lax.broadcasted_iota(jnp.int32, acc.shape, 0) + base
            named = jnp.where(row == ids[k, 0:1, :], scale * acc, 0.0)
            hs[k] += jnp.sum(named, axis=0, keepdims=True)

    oz, oh = 1 - zl, 1 - zh

    for copy in local:
        copy.wait()
    send("oo", prow(y, zh), orow(y, zh), sib)
    score_loop(x, zl)

    def pass_x(name, xx, zz, part, peer):
        send(name, lrow(xx, zz, part), lrow(xx, zz, part), peer)

    def pass_y(name, yy, zz, part, peer):
        send(name, prow(yy, zz, part), prow(yy, zz, part), peer)

    def pass_z(k):
        arrived(f"z{k}", lrow(x, oz, quarters[k]))
        send(f"h{k}", lrow(x, oz, quarters[k]), prow(y, zh, quarters[k]), p2)

    pass_z(0)
    pass_z(1)
    arrived("x+o0", lrow(px[3], zl, halves[0]))
    pass_x("x+f", px[3], zl, halves[0], xp)
    arrived("x-o1", lrow(px[1], zl, halves[1]))
    pass_x("x-f", px[1], zl, halves[1], xm)
    arrived("y+o0", prow(py[3], zh, halves[0]))
    pass_y("y+f", py[3], zh, halves[0], yp)
    arrived("y-o1", prow(py[1], zh, halves[1]))
    pass_y("y-f", py[1], zh, halves[1], ym)
    pass_x("x+p0", x, oz, halves[0], xp)
    arrived("ids", ids.at[1])
    arrived("q", qbuf.at[pl.ds(q_dev, q_dev)])
    score_pool(y, zh)

    pass_z(2)
    arrived("h0", prow(y, oh, quarters[0]))
    arrived("h1", prow(y, oh, quarters[1]))
    pass_y("y+p0", y, oh, halves[0], yp)
    pass_z(3)
    pass_x("x-p1", x, oz, halves[1], xm)
    pass_x("x+p1", x, oz, direct[1], xp)
    pass_x("x-p0", x, oz, direct[0], xm)
    arrived("x+o1", lrow(px[3], zl, halves[1]))
    pass_x("zx1", px[3], zl, by_z[1], p1)
    arrived("x-o0", lrow(px[1], zl, halves[0]))
    pass_x("zx0", px[1], zl, by_z[0], p1)
    arrived("y+o1", prow(py[3], zh, halves[1]))
    send("ty1", prow(py[3], zh, by_z[1]), via.at[1], p2)
    arrived("y-o0", prow(py[1], zh, halves[0]))
    send("ty0", prow(py[1], zh, by_z[0]), via.at[0], p2)
    send("o3", prow(py[3], zh), orow(py[3], zh), sib)
    send("o1", prow(py[1], zh), orow(py[1], zh), sib)
    score_loop(x, oz)
    score_loop(px[3], zl)
    score_loop(px[1], zl)
    arrived("h2", prow(y, oh, quarters[2]))
    arrived("h3", prow(y, oh, quarters[3]))
    pass_y("y-p1", y, oh, halves[1], ym)
    pass_y("y+p1", y, oh, direct[1], yp)
    pass_y("y-p0", y, oh, direct[0], ym)
    send("op", prow(y, oh), orow(y, oh), sib)
    score_pool(py[3], zh)
    score_pool(py[1], zh)
    arrived("x+f", lrow(px[2], zl, halves[0]))
    arrived("x-f", lrow(px[2], zl, halves[1]))
    score_loop(px[2], zl)
    arrived("ty1", via.at[1])
    send("tz1", via.at[1], prow(py[3], oh, by_z[1]), p1)
    score_pool(y, oh)
    arrived("y+f", prow(py[2], zh, halves[0]))
    arrived("y-f", prow(py[2], zh, halves[1]))
    send("o2", prow(py[2], zh), orow(py[2], zh), sib)
    score_pool(py[2], zh)
    arrived("x+p0", lrow(px[3], oz, halves[0]))
    pass_x("x+g", px[3], oz, halves[0], xp)
    arrived("x-p1", lrow(px[1], oz, halves[1]))
    pass_x("x-g", px[1], oz, halves[1], xm)
    arrived("y+p0", prow(py[3], oh, halves[0]))
    pass_y("y+g", py[3], oh, halves[0], yp)
    arrived("y-p1", prow(py[1], oh, halves[1]))
    pass_y("y-g", py[1], oh, halves[1], ym)
    arrived("ty0", via.at[0])
    send("tz0", via.at[0], prow(py[1], oh, by_z[0]), p1)
    arrived("x+p1", lrow(px[3], oz, direct[1]))
    arrived("zx1", lrow(px[3], oz, by_z[1]))
    score_loop(px[3], oz)
    arrived("x-p0", lrow(px[1], oz, direct[0]))
    arrived("zx0", lrow(px[1], oz, by_z[0]))
    score_loop(px[1], oz)
    arrived("y+p1", prow(py[3], oh, direct[1]))
    arrived("tz1", prow(py[3], oh, by_z[1]))
    score_pool(py[3], oh)
    arrived("y-p0", prow(py[1], oh, direct[0]))
    arrived("tz0", prow(py[1], oh, by_z[0]))
    score_pool(py[1], oh)
    arrived("y+g", prow(py[2], oh, halves[0]))
    arrived("y-g", prow(py[2], oh, halves[1]))
    score_pool(py[2], oh)
    send("hs", hs.at[1], hin, sib)
    arrived("x+g", lrow(px[2], oz, halves[0]))
    arrived("x-g", lrow(px[2], oz, halves[1]))
    score_loop(px[2], oz)

    arrived("hs", hin)
    hard = hs[0, 0:1, :] + hin[0:1, :]
    peak = jnp.maximum(top[0:1], hard)
    total = run[0:1] * jnp.exp(top[0:1] - peak) + jnp.exp(hard - peak)
    log_total = peak + jnp.log(total)
    w_hard = jnp.exp(hard - log_total).astype(BF16).astype(F32)
    w2[0] = jnp.broadcast_to(w_hard, w2.shape[1:])
    send("w", w2.at[0], w2.at[1], sib)
    lsum[...] = jnp.broadcast_to(
        jnp.sum(log_total - hit[0:1], axis=1, keepdims=True), lsum.shape
    )
    blocks = s.shape[1] // q_dev

    def weigh(xx, zz):
        c = xx * 2 + zz
        part = s[:, rows(c * q_dev, q_dev, q_dev)]
        row = lax.broadcasted_iota(jnp.int32, part.shape, 0) + c * p_dev
        one = jnp.where(row == pos_ref[...], 1.0, 0.0)
        wt[rows(c * p_dev, p_dev), :] = (jnp.exp(part - log_total) - one).astype(BF16)

    loss_peers = [
        (lax.rem(b + 2 + 4 * lax.rem(x, 2), 8), g),
        (b, zh * 8 + lax.rem(y + 1 + 2 * lax.rem(y, 2), 4) * 2 + core),
        p1,
        p2,
        sib,
        ((3 - x) * 2 + zl, g),
        (b, zh * 8 + (3 - y) * 2 + core),
    ]

    def loss_start(k):
        lsend[k] = lsum[...]
        send(f"l{k}", lsend.at[k], lrecv.at[k], loss_peers[k])

    def loss_finish(k):
        arrived(f"l{k}", lrecv.at[k])
        lsum[...] = lsend[k] + lrecv[k]

    loss_start(0)

    step = 512

    def columns(count):
        return width // 2 if count == p_dev else step

    def loop_part(start, count, store):
        n = columns(count)

        @pl.loop(0, width // n, unroll=min(4, width // n // 2))
        def _(t):
            cols = rows(t * n, n, n)
            store(cols, scale * jnp.dot(
                wt[rows(start, count), :], qbuf[pl.ds(0, q_dev), cols],
                preferred_element_type=F32,
            ))

    def pool_weights(yy, zz, at):
        base = pool_base(yy, zz, core)
        for k in range(2):
            row = lax.broadcasted_iota(jnp.int32, (p_dev, q_dev), 0) + base
            wht[at:at + p_dev, k * q_dev:(k + 1) * q_dev] = jnp.where(
                row == ids[k, 0:1, :], w2[k, 0:1, :], 0.0
            ).astype(BF16)

    def pool_part(count, store):
        n = columns(count)

        @pl.loop(0, width // n, unroll=min(4, width // n // 2))
        def _(t):
            cols = rows(t * n, n, n)
            store(cols, scale * jnp.dot(
                wht[pl.ds(0, count), :], qbuf[:, cols], preferred_element_type=F32
            ))

    z_of = {"x": (oz, zl), "y": (oh, zh)}
    axes = {"x": (xs, xrf, xrs, xp, xm), "y": (ys, yrf, yrs, yp, ym)}

    def piece(a, slot, role, part):
        return axes[a][0].at[slot, rows(z_of[a][role] * p_dev + part[0], part[1], 16)]

    def at(part):
        return pl.ds(part[0], part[1])

    def add_to(dst, *terms):
        @pl.loop(0, width // step, unroll=2)
        def _(t):
            cols = rows(t * step, step, step)
            total = dst[:, cols].astype(F32)
            for term in terms:
                total += term[:, cols].astype(F32)
            dst[:, cols] = total.astype(BF16)

    def send_far(a, role):
        _, rf, _, plus, minus = axes[a]
        send(f"{a}+s2{role}", piece(a, 2, role, halves[0]), rf.at[0, role], plus)
        send(f"{a}-s2{role}", piece(a, 2, role, halves[1]), rf.at[1, role], minus)

    def send_near(a, role):
        _, _, rs, plus, minus = axes[a]
        send(f"{a}+s1{role}", piece(a, 0, role, direct[1]), rs.at[0, role, at(direct[1])], plus)
        send(f"{a}-s1{role}", piece(a, 1, role, direct[0]), rs.at[1, role, at(direct[0])], minus)

    def send_mix_x():
        send("mx1", piece("x", 0, 0, by_z[1]), mix.at[1], p1)
        send("mx0", piece("x", 1, 0, by_z[0]), mix.at[0], p1)

    hop = [xrs.at[1, 0, at(by_z[0])], xrs.at[0, 0, at(by_z[1])]]
    end = [yrs.at[1, 0, at(by_z[0])], yrs.at[0, 0, at(by_z[1])]]

    def send_mix_y():
        send("my1", piece("y", 0, 0, by_z[1]), hop[1], p2)
        send("my0", piece("y", 1, 0, by_z[0]), hop[0], p2)

    def pass_mix_y(h):
        arrived(f"my{h}", hop[h])
        send(f"mz{h}", hop[h], end[h], p1)

    def send_mixed(a, h):
        _, _, rs, plus, minus = axes[a]
        term = mix.at[h] if a == "x" else end[h]
        arrived(f"mx{h}" if a == "x" else f"mz{h}", term)
        mine = piece(a, 1 - h, 1, by_z[h])
        add_to(mine, term)
        send(f"{a}m{h}", mine, rs.at[1 - h, 1, at(by_z[h])], plus if h else minus)

    def send_sum(a, role):
        _, rf, rs, plus, minus = axes[a]
        for d, (sign, peer) in enumerate((("+", plus), ("-", minus))):
            arrived(f"{a}{sign}s2{role}", rf.at[d, role])
            mine = piece(a, d, role, halves[d])
            add_to(mine, rf.at[d, role])
            send(f"{a}{sign}s0{role}", mine, rs.at[d, role, at(halves[d])], peer)

    def sums_arrived(a, role):
        rs = axes[a][2]
        for d, sign in enumerate("+-"):
            arrived(f"{a}{sign}s1{role}", rs.at[d, role, at(direct[1 - d])])
            if role:
                arrived(f"{a}m{1 - d}", rs.at[d, role, at(by_z[1 - d])])
            arrived(f"{a}{sign}s0{role}", rs.at[d, role, at(halves[d])])

    def store_to(ref):
        def store(cols, value):
            ref[:, cols] = value.astype(BF16)
        return store

    place = {1: 0, 3: 1, 2: 2}

    def x_part(k, role):
        zz = z_of["x"][role]
        weigh(px[k], zz)
        loop_part((px[k] * 2 + zz) * p_dev, p_dev, store_to(piece("x", place[k], role, whole)))

    def y_part(k, role):
        pool_weights(py[k], z_of["y"][role], 0)
        pool_part(p_dev, store_to(piece("y", place[k], role, whole)))

    x_part(2, 0)
    send_far("x", 0)
    loss_finish(0)
    loss_start(1)
    arrived("w", w2.at[1])
    y_part(2, 0)
    loss_finish(1)
    send_far("y", 0)
    loss_start(2)
    send("o4", prow(py[3], oh), orow(py[3], oh), sib)
    send("o5", prow(py[1], oh), orow(py[1], oh), sib)
    send("o6", prow(py[2], oh), orow(py[2], oh), sib)
    x_part(1, 0)
    x_part(3, 0)
    send_near("x", 0)
    loss_finish(2)
    loss_start(3)
    send_mix_x()
    y_part(1, 0)
    y_part(3, 0)
    send_near("y", 0)
    loss_finish(3)
    send_mix_y()
    loss_start(4)
    for k in (2, 1, 3):
        x_part(k, 1)
    weigh(x, 0)
    weigh(x, 1)
    send_sum("x", 0)
    y_part(2, 1)
    send_sum("y", 0)
    loss_finish(4)
    loss_start(5)
    send_far("x", 1)
    send_far("y", 1)
    y_part(1, 1)
    y_part(3, 1)
    send_near("x", 1)
    send_near("y", 1)

    for a in "xy":
        sent(f"{a}+s20")
        sent(f"{a}-s20")

    hand_x = xs.at[2, rows(oz * p_dev, p_dev)]
    hand_y = ys.at[2, rows(oh * p_dev, p_dev)]

    def split(first, value):
        low, high = value[:p_dev], value[p_dev:]
        return jnp.where(first, low, high), jnp.where(first, high, low)

    def store_x(cols, value):
        mine, handed = split(zl == 0, value)
        s[:, cols] = mine
        hand_x[:, cols] = handed.astype(BF16)

    def store_y(cols, value):
        mine, handed = split(zh == 0, value)
        s[:, cols] += mine
        hand_y[:, cols] = handed.astype(BF16)

    loop_part(x * 2 * p_dev, 2 * p_dev, store_x)
    pool_weights(y, 0, 0)
    pool_weights(y, 1, p_dev)
    pool_part(2 * p_dev, store_y)
    pass_mix_y(1)
    send_mixed("x", 1)
    send_mixed("x", 0)

    for c in range(blocks):
        wall[:, c * p_dev:(c + 1) * p_dev] = (
            wt[c * p_dev:(c + 1) * p_dev, :].astype(F32).T.astype(BF16)
        )
    loop_rows = blocks * p_dev

    @pl.loop(0, q_dev // 128)
    def _(n):
        part = rows(n * 128, 128, 128)
        names = jnp.broadcast_to(ids[0, 0:1, part].astype(F32), (128, 128)).T
        values = jnp.broadcast_to(w2[0, 0:1, part], (128, 128)).T
        lane = lax.broadcasted_iota(jnp.int32, (128, 128), 1)
        for k in range(2):
            cc = core if k == 0 else 1 - core
            for slot in range(8):
                base = pool_base(slot // 2, slot % 2, cc)
                at = loop_rows + (k * 8 + slot) * p_dev
                wall[part, at:at + p_dev] = jnp.where(
                    names == (lane + base).astype(F32), values, 0.0
                ).astype(BF16)

    arrived("oo", orow(y, zh))
    arrived("o3", orow(py[3], zh))
    arrived("o1", orow(py[1], zh))
    arrived("op", orow(y, oh))
    arrived("o2", orow(py[2], zh))
    arrived("o4", orow(py[3], oh))
    arrived("o5", orow(py[1], oh))
    arrived("o6", orow(py[2], oh))

    tile = dqt.shape[2]
    tiles = width // tile
    pool_rows = pbuf.shape[0]

    def tile_in(t):
        k = lax.rem(t, 2)
        return pltpu.make_async_copy(
            other_hbm.at[:, rows(t * tile, tile, tile)], otile.at[k], csem.at[k]
        )

    def tile_out(t):
        k = lax.rem(t, 2)
        return pltpu.make_async_copy(
            dqt.at[k], dq_hbm.at[:, rows(t * tile, tile, tile)], csem.at[2 + k]
        )

    tile_in(0).start()

    def query_slope(first, last):
        @pl.loop(first, last)
        def _(t):
            k = lax.rem(t, 2)

            @pl.when(t + 1 < tiles)
            def _():
                tile_in(t + 1).start()

            @pl.when(t >= 2)
            def _():
                tile_out(t - 2).wait()

            cols = rows(t * tile, tile, tile)
            tile_in(t).wait()
            acc = jnp.dot(
                wall[:, 0:loop_rows], lbuf[:, cols], preferred_element_type=F32
            )
            acc += jnp.dot(
                wall[:, loop_rows:loop_rows + pool_rows], pbuf[:, cols],
                preferred_element_type=F32,
            )
            acc += jnp.dot(
                wall[:, loop_rows + pool_rows:], otile[k], preferred_element_type=F32
            )
            dqt[k] = (scale * acc).astype(BF16)
            tile_out(t).start()

    query_slope(0, tiles // 4)
    pass_mix_y(0)
    loss_finish(5)
    loss_start(6)
    query_slope(tiles // 4, tiles * 3 // 8)

    parts = [pl.ds(0, moved), pl.ds(moved, p_dev - 2 * moved), pl.ds(p_dev - moved, moved)]
    signs = [(0,), (0, 1), (1,)]
    sums_arrived("y", 0)
    for k, part in enumerate(parts):
        add_to(hand_y.at[part], *(yrs.at[d, 0, part] for d in signs[k]))
        send(f"zh{k}", hand_y.at[part], zrh.at[part], p2)
    send_mixed("y", 1)
    query_slope(tiles * 3 // 8, tiles * 5 // 8)
    sums_arrived("x", 0)
    send_mixed("y", 0)
    send_sum("x", 1)
    send_sum("y", 1)
    for k, part in enumerate(parts):
        arrived(f"zh{k}", zrh.at[part])
        add_to(hand_x.at[part], zrh.at[part], *(xrs.at[d, 0, part] for d in signs[k]))
        send(f"zl{k}", hand_x.at[part], zrl.at[part], p1)
        query_slope(tiles * (10 + 2 * k) // 16, tiles * (12 + 2 * k) // 16)
    loss_finish(6)
    loss_ref[0] = jnp.max(lsum[...]) / (q_dev * lax.axis_size("blk") * lax.axis_size("grp"))

    sums_arrived("x", 1)
    for h, part in enumerate(parts):
        arrived(f"zl{h}", zrl.at[part])

        @pl.loop(0, width // step, unroll=2)
        def _(t):
            cols = rows(t * step, step, step)
            s[part, cols] += (
                xrs[0, 1, part, cols].astype(F32)
                + xrs[1, 1, part, cols].astype(F32)
                + zrl[part, cols].astype(F32)
            )

    sums_arrived("y", 1)
    sent("y+s21")
    sent("y-s21")
    result = ys.at[2, rows(zh * p_dev, p_dev)]
    outs = []
    for h, part in enumerate(parts):
        @pl.loop(0, width // step, unroll=2)
        def _(t):
            cols = rows(t * step, step, step)
            result[part, cols] = (
                s[part, cols]
                + yrs[0, 1, part, cols].astype(F32)
                + yrs[1, 1, part, cols].astype(F32)
            ).astype(BF16)

        copy = pltpu.make_async_copy(result.at[part], dp_hbm.at[part], csem.at[4 + h])
        copy.start()
        outs.append(copy)
    tile_out(tiles - 2).wait()
    tile_out(tiles - 1).wait()
    for copy in outs:
        copy.wait()
    for name in list(started):
        sent(name)


def write(slope_in, slope_out, slope, sem):
    pieces = 4
    n = slope.shape[0] // pieces
    parts = [pl.ds(k * n, n) for k in range(pieces)]
    reads = [
        pltpu.make_async_copy(slope_in.at[part], slope.at[part], sem.at[0, k])
        for k, part in enumerate(parts)
    ]
    writes = [
        pltpu.make_async_copy(slope.at[part], slope_out.at[part], sem.at[1, k])
        for k, part in enumerate(parts)
    ]
    for copy in reads:
        copy.start()
    for read, copy in zip(reads, writes):
        read.wait()
        copy.start()
    for copy in writes:
        copy.wait()


def shards(queries, passages, positive_ids, hard_ids):
    q_dev, width = queries.shape
    p_dev = passages.shape[0]
    half = p_dev // 2
    moved = half * 3 // 4
    vmem = pltpu.VMEM
    hbm = pl.BlockSpec(memory_space=pl.ANY)
    block = pl.BlockSpec(memory_space=pltpu.VMEM)
    loss, slope, grad, _ = pl.pallas_call(
        kernel,
        out_shape=(
            jax.ShapeDtypeStruct((1,), F32),
            jax.ShapeDtypeStruct((q_dev, width), BF16),
            jax.ShapeDtypeStruct((p_dev, width), BF16),
            jax.ShapeDtypeStruct((8 * p_dev, width), BF16),
        ),
        in_specs=[hbm, hbm, block, block],
        out_specs=(pl.BlockSpec(memory_space=pltpu.SMEM), hbm, hbm, hbm),
        scratch_shapes=[
            vmem((8 * p_dev, width), BF16),
            vmem((8 * p_dev, width), BF16),
            vmem((2 * q_dev, width), BF16),
            vmem((p_dev, 8 * q_dev), F32),
            vmem((8 * p_dev, q_dev), BF16),
            vmem((q_dev, 24 * p_dev), BF16),
            vmem((2 * p_dev, 2 * q_dev), BF16),
            vmem((3, 2 * p_dev, width), BF16),
            vmem((3, 2 * p_dev, width), BF16),
            vmem((2, 2, half, width), BF16),
            vmem((2, 2, p_dev, width), BF16),
            vmem((2, 2, half, width), BF16),
            vmem((2, 2, p_dev, width), BF16),
            vmem((p_dev, width), BF16),
            vmem((p_dev, width), BF16),
            vmem((2, moved, width), BF16),
            vmem((2, moved, width), BF16),
            vmem((2, 8, q_dev), jnp.int32),
            vmem((2, 8, q_dev), F32),
            vmem((8, q_dev), F32),
            vmem((2, 8, q_dev), F32),
            vmem((8, q_dev), F32),
            vmem((8, q_dev), F32),
            vmem((8, q_dev), F32),
            vmem((8, 128), F32),
            vmem((7, 8, 128), F32),
            vmem((7, 8, 128), F32),
            vmem((2, 8 * p_dev, 256), BF16),
            vmem((2, q_dev, 256), BF16),
            pltpu.SemaphoreType.DMA((COPIES,)),
            pltpu.SemaphoreType.DMA((COPIES,)),
            pltpu.SemaphoreType.DMA((7,)),
        ],
        compiler_params=pltpu.CompilerParams(
            collective_id=0, has_side_effects=True, vmem_limit_bytes=63 * 2**20
        ),
        cost_estimate=pl.CostEstimate(
            flops=2 * q_dev * width * 9 * 8 * p_dev,
            bytes_accessed=40 * 2**20,
            transcendentals=2 * 8 * p_dev * q_dev,
        ),
    )(
        queries,
        passages,
        positive_ids.reshape(1, q_dev),
        hard_ids.reshape(1, q_dev),
    )
    slope = pl.pallas_call(
        write,
        out_shape=jax.ShapeDtypeStruct(slope.shape, BF16),
        in_specs=[hbm],
        out_specs=hbm,
        scratch_shapes=[vmem(slope.shape, BF16), pltpu.SemaphoreType.DMA((2, 4))],
        compiler_params=pltpu.CompilerParams(vmem_limit_bytes=63 * 2**20),
    )(slope)
    slope, grad, loss = lax.optimization_barrier((slope, grad, loss))
    return loss[0], slope, grad


def solution(mesh):
    return jax.shard_map(
        shards,
        mesh=mesh,
        in_specs=(
            P(("blk", "grp"), None),
            P(("blk", "grp"), None),
            P(("blk", "grp")),
            P(("blk", "grp"), None),
        ),
        out_specs=(P(), P(("blk", "grp"), None), P(("blk", "grp"), None)),
        check_vma=False,
    )
```

```python
import functools

import jax
import jax.numpy as jnp
from jax import lax
from jax.experimental import pallas as pl
from jax.experimental.pallas import tpu as pltpu
from jax.sharding import PartitionSpec as P

logit_scaling_coefficient = 20.0
MESH = pl.DeviceIdType.MESH
BF16 = jnp.bfloat16
F32 = jnp.float32
COPIES = 112
NT = (((1,), (1,)), ((), ()))


def rows(start, size, multiple=64):
    return pl.ds(pl.multiple_of(start, multiple), size)


def kernel(
    q_hbm, p_hbm, pos_ref, hid_ref,
    loss_ref, dq_hbm, dp_hbm, other_hbm,
    lbuf, pbuf, qbuf, s, wt, wall, wht, xs, ys, xrf, xrs, yrf, yrs, zrh, zrl, via, mix,
    ids, hs, hin, w2, top, run, hit, lsum, lsend, lrecv, otile, dqt,
    ssem, rsem, csem,
):
    q_dev, width = q_hbm.shape
    p_dev = p_hbm.shape[0]
    half = p_dev // 2
    scale = logit_scaling_coefficient

    b = lax.axis_index("blk")
    g = lax.axis_index("grp")
    x, zl = lax.div(b, 2), lax.rem(b, 2)
    zh, y, core = lax.div(g, 8), lax.div(lax.rem(g, 8), 2), lax.rem(g, 2)
    pb = x * 2 + 1 - zl
    px = [lax.rem(x + k, 4) for k in range(4)]
    py = [lax.rem(y + k, 4) for k in range(4)]
    xp = (px[1] * 2 + zl, g)
    xm = (px[3] * 2 + zl, g)
    yp = (b, zh * 8 + py[1] * 2 + core)
    ym = (b, zh * 8 + py[3] * 2 + core)
    p1 = (pb, g)
    p2 = (pb, lax.rem(g + 8, 16))
    sib = (b, zh * 8 + y * 2 + 1 - core)

    number = {}
    started = {}

    def describe(name, src, dst, peer):
        k = number.setdefault(name, len(number))
        return pltpu.make_async_remote_copy(
            src_ref=src, dst_ref=dst, send_sem=ssem.at[k], recv_sem=rsem.at[k],
            device_id=peer, device_id_type=MESH,
        )

    def send(name, src, dst, peer):
        copy = describe(name, src, dst, peer)
        copy.start()
        started[name] = copy

    def sent(name):
        started.pop(name).wait_send()

    def arrived(name, dst):
        describe(name, dst, dst, sib).wait_recv()

    quarter = half // 2
    moved = half * 3 // 4
    halves = [(0, half), (half, half)]
    by_z = [(0, moved), (p_dev - moved, moved)]
    direct = [(moved, half - moved), (half, half - moved)]
    whole = (0, p_dev)

    def lrow(xx, zz, part=whole):
        return lbuf.at[rows((xx * 2 + zz) * p_dev + part[0], part[1], 16)]

    def prow(yy, zz, part=whole):
        return pbuf.at[rows((yy * 2 + zz) * p_dev + part[0], part[1], 16)]

    def orow(yy, zz):
        return other_hbm.at[rows((yy * 2 + zz) * p_dev, p_dev)]

    local = [
        pltpu.make_async_copy(q_hbm, qbuf.at[pl.ds(0, q_dev)], csem.at[0]),
        pltpu.make_async_copy(p_hbm, lrow(x, zl), csem.at[1]),
        pltpu.make_async_copy(p_hbm, prow(y, zh), csem.at[2]),
    ]
    for copy in local:
        copy.start()
    ids[0] = jnp.broadcast_to(hid_ref[...], ids.shape[1:])
    hs[...] = jnp.zeros(hs.shape, F32)
    top[...] = jnp.full(top.shape, -jnp.inf, F32)
    run[...] = jnp.zeros(run.shape, F32)
    hit[...] = jnp.zeros(hit.shape, F32)

    barrier = pltpu.get_barrier_semaphore()
    for peer in (xp, xm, yp, ym, p1, p2, sib):
        pl.semaphore_signal(barrier, inc=1, device_id=peer, device_id_type=MESH)
    pl.semaphore_wait(barrier, 7)

    own = [p_hbm.at[pl.ds(h * half, half)] for h in range(2)]
    quarters = [(k * quarter, quarter) for k in range(4)]

    for k in range(4):
        send(f"z{k}", p_hbm.at[pl.ds(k * quarter, quarter)], lrow(x, zl, quarters[k]), p1)
    for h in range(2):
        r = 1 - h
        send(f"x+o{h}", own[h], lrow(x, zl, halves[h]), xp)
        send(f"x-o{r}", own[r], lrow(x, zl, halves[r]), xm)
        send(f"y+o{h}", own[h], prow(y, zh, halves[h]), yp)
        send(f"y-o{r}", own[r], prow(y, zh, halves[r]), ym)
    send("ids", ids.at[0], ids.at[1], sib)
    send("q", q_hbm, qbuf.at[pl.ds(q_dev, q_dev)], sib)

    def score_loop(xx, zz):
        c = xx * 2 + zz
        acc = scale * lax.dot_general(
            lbuf[rows(c * p_dev, p_dev), :], qbuf[pl.ds(0, q_dev), :], NT,
            preferred_element_type=F32,
        )
        s[:, rows(c * q_dev, q_dev, q_dev)] = acc
        old = top[0:1]
        peak = jnp.maximum(old, jnp.max(acc, axis=0, keepdims=True))
        total = run[0:1] * jnp.exp(old - peak) + jnp.sum(
            jnp.exp(acc - peak), axis=0, keepdims=True
        )
        row = lax.broadcasted_iota(jnp.int32, acc.shape, 0) + c * p_dev
        top[...] = jnp.broadcast_to(peak, top.shape)
        run[...] = jnp.broadcast_to(total, run.shape)
        hit[...] += jnp.sum(jnp.where(row == pos_ref[...], acc, 0.0), axis=0, keepdims=True)

    def pool_base(yy, zz, cc):
        return (zz * 8 + yy * 2 + cc) * p_dev

    def score_pool(yy, zz):
        slot = yy * 2 + zz
        base = pool_base(yy, zz, core)

        @pl.loop(0, 2)
        def _(k):
            acc = lax.dot_general(
                pbuf[rows(slot * p_dev, p_dev), :], qbuf[rows(k * q_dev, q_dev, q_dev), :], NT,
                preferred_element_type=F32,
            )
            row = lax.broadcasted_iota(jnp.int32, acc.shape, 0) + base
            named = jnp.where(row == ids[k, 0:1, :], scale * acc, 0.0)
            hs[k] += jnp.sum(named, axis=0, keepdims=True)

    oz, oh = 1 - zl, 1 - zh

    for copy in local:
        copy.wait()
    send("oo", prow(y, zh), orow(y, zh), sib)
    score_loop(x, zl)

    def pass_x(name, xx, zz, part, peer):
        send(name, lrow(xx, zz, part), lrow(xx, zz, part), peer)

    def pass_y(name, yy, zz, part, peer):
        send(name, prow(yy, zz, part), prow(yy, zz, part), peer)

    def pass_z(k):
        arrived(f"z{k}", lrow(x, oz, quarters[k]))
        send(f"h{k}", lrow(x, oz, quarters[k]), prow(y, zh, quarters[k]), p2)

    pass_z(0)
    pass_z(1)
    arrived("x+o0", lrow(px[3], zl, halves[0]))
    pass_x("x+f", px[3], zl, halves[0], xp)
    arrived("x-o1", lrow(px[1], zl, halves[1]))
    pass_x("x-f", px[1], zl, halves[1], xm)
    arrived("y+o0", prow(py[3], zh, halves[0]))
    pass_y("y+f", py[3], zh, halves[0], yp)
    arrived("y-o1", prow(py[1], zh, halves[1]))
    pass_y("y-f", py[1], zh, halves[1], ym)
    pass_x("x+p0", x, oz, halves[0], xp)
    arrived("ids", ids.at[1])
    arrived("q", qbuf.at[pl.ds(q_dev, q_dev)])
    score_pool(y, zh)

    pass_z(2)
    arrived("h0", prow(y, oh, quarters[0]))
    arrived("h1", prow(y, oh, quarters[1]))
    pass_y("y+p0", y, oh, halves[0], yp)
    pass_z(3)
    pass_x("x-p1", x, oz, halves[1], xm)
    pass_x("x+p1", x, oz, direct[1], xp)
    pass_x("x-p0", x, oz, direct[0], xm)
    arrived("x+o1", lrow(px[3], zl, halves[1]))
    pass_x("zx1", px[3], zl, by_z[1], p1)
    arrived("x-o0", lrow(px[1], zl, halves[0]))
    pass_x("zx0", px[1], zl, by_z[0], p1)
    arrived("y+o1", prow(py[3], zh, halves[1]))
    send("ty1", prow(py[3], zh, by_z[1]), via.at[1], p2)
    arrived("y-o0", prow(py[1], zh, halves[0]))
    send("ty0", prow(py[1], zh, by_z[0]), via.at[0], p2)
    send("o3", prow(py[3], zh), orow(py[3], zh), sib)
    send("o1", prow(py[1], zh), orow(py[1], zh), sib)
    score_loop(x, oz)
    score_loop(px[3], zl)
    score_loop(px[1], zl)
    arrived("h2", prow(y, oh, quarters[2]))
    arrived("h3", prow(y, oh, quarters[3]))
    pass_y("y-p1", y, oh, halves[1], ym)
    pass_y("y+p1", y, oh, direct[1], yp)
    pass_y("y-p0", y, oh, direct[0], ym)
    send("op", prow(y, oh), orow(y, oh), sib)
    score_pool(py[3], zh)
    score_pool(py[1], zh)
    arrived("x+f", lrow(px[2], zl, halves[0]))
    arrived("x-f", lrow(px[2], zl, halves[1]))
    score_loop(px[2], zl)
    arrived("ty1", via.at[1])
    send("tz1", via.at[1], prow(py[3], oh, by_z[1]), p1)
    score_pool(y, oh)
    arrived("y+f", prow(py[2], zh, halves[0]))
    arrived("y-f", prow(py[2], zh, halves[1]))
    send("o2", prow(py[2], zh), orow(py[2], zh), sib)
    score_pool(py[2], zh)
    arrived("x+p0", lrow(px[3], oz, halves[0]))
    pass_x("x+g", px[3], oz, halves[0], xp)
    arrived("x-p1", lrow(px[1], oz, halves[1]))
    pass_x("x-g", px[1], oz, halves[1], xm)
    arrived("y+p0", prow(py[3], oh, halves[0]))
    pass_y("y+g", py[3], oh, halves[0], yp)
    arrived("y-p1", prow(py[1], oh, halves[1]))
    pass_y("y-g", py[1], oh, halves[1], ym)
    arrived("ty0", via.at[0])
    send("tz0", via.at[0], prow(py[1], oh, by_z[0]), p1)
    arrived("x+p1", lrow(px[3], oz, direct[1]))
    arrived("zx1", lrow(px[3], oz, by_z[1]))
    score_loop(px[3], oz)
    arrived("x-p0", lrow(px[1], oz, direct[0]))
    arrived("zx0", lrow(px[1], oz, by_z[0]))
    score_loop(px[1], oz)
    arrived("y+p1", prow(py[3], oh, direct[1]))
    arrived("tz1", prow(py[3], oh, by_z[1]))
    score_pool(py[3], oh)
    arrived("y-p0", prow(py[1], oh, direct[0]))
    arrived("tz0", prow(py[1], oh, by_z[0]))
    score_pool(py[1], oh)
    arrived("y+g", prow(py[2], oh, halves[0]))
    arrived("y-g", prow(py[2], oh, halves[1]))
    score_pool(py[2], oh)
    send("hs", hs.at[1], hin, sib)
    arrived("x+g", lrow(px[2], oz, halves[0]))
    arrived("x-g", lrow(px[2], oz, halves[1]))
    score_loop(px[2], oz)

    arrived("hs", hin)
    hard = hs[0, 0:1, :] + hin[0:1, :]
    peak = jnp.maximum(top[0:1], hard)
    total = run[0:1] * jnp.exp(top[0:1] - peak) + jnp.exp(hard - peak)
    log_total = peak + jnp.log(total)
    w_hard = jnp.exp(hard - log_total).astype(BF16).astype(F32)
    w2[0] = jnp.broadcast_to(w_hard, w2.shape[1:])
    send("w", w2.at[0], w2.at[1], sib)
    lsum[...] = jnp.broadcast_to(
        jnp.sum(log_total - hit[0:1], axis=1, keepdims=True), lsum.shape
    )
    blocks = s.shape[1] // q_dev

    def weigh(xx, zz):
        c = xx * 2 + zz
        part = s[:, rows(c * q_dev, q_dev, q_dev)]
        row = lax.broadcasted_iota(jnp.int32, part.shape, 0) + c * p_dev
        one = jnp.where(row == pos_ref[...], 1.0, 0.0)
        wt[rows(c * p_dev, p_dev), :] = (jnp.exp(part - log_total) - one).astype(BF16)

    loss_peers = [
        (lax.rem(b + 2 + 4 * lax.rem(x, 2), 8), g),
        (b, zh * 8 + lax.rem(y + 1 + 2 * lax.rem(y, 2), 4) * 2 + core),
        p1,
        p2,
        sib,
        ((3 - x) * 2 + zl, g),
        (b, zh * 8 + (3 - y) * 2 + core),
    ]

    def loss_start(k):
        lsend[k] = lsum[...]
        send(f"l{k}", lsend.at[k], lrecv.at[k], loss_peers[k])

    def loss_finish(k):
        arrived(f"l{k}", lrecv.at[k])
        lsum[...] = lsend[k] + lrecv[k]

    loss_start(0)

    step = 512

    def columns(count):
        return width // 2 if count == p_dev else step

    def loop_part(start, count, store):
        n = columns(count)

        @pl.loop(0, width // n, unroll=min(4, width // n // 2))
        def _(t):
            cols = rows(t * n, n, n)
            store(cols, scale * jnp.dot(
                wt[rows(start, count), :], qbuf[pl.ds(0, q_dev), cols],
                preferred_element_type=F32,
            ))

    def pool_weights(yy, zz, at):
        base = pool_base(yy, zz, core)
        for k in range(2):
            row = lax.broadcasted_iota(jnp.int32, (p_dev, q_dev), 0) + base
            wht[at:at + p_dev, k * q_dev:(k + 1) * q_dev] = jnp.where(
                row == ids[k, 0:1, :], w2[k, 0:1, :], 0.0
            ).astype(BF16)

    def pool_part(count, store):
        n = columns(count)

        @pl.loop(0, width // n, unroll=min(4, width // n // 2))
        def _(t):
            cols = rows(t * n, n, n)
            store(cols, scale * jnp.dot(
                wht[pl.ds(0, count), :], qbuf[:, cols], preferred_element_type=F32
            ))

    z_of = {"x": (oz, zl), "y": (oh, zh)}
    axes = {"x": (xs, xrf, xrs, xp, xm), "y": (ys, yrf, yrs, yp, ym)}

    def piece(a, slot, role, part):
        return axes[a][0].at[slot, rows(z_of[a][role] * p_dev + part[0], part[1], 16)]

    def at(part):
        return pl.ds(part[0], part[1])

    def add_to(dst, *terms):
        @pl.loop(0, width // step, unroll=2)
        def _(t):
            cols = rows(t * step, step, step)
            total = dst[:, cols].astype(F32)
            for term in terms:
                total += term[:, cols].astype(F32)
            dst[:, cols] = total.astype(BF16)

    def send_far(a, role):
        _, rf, _, plus, minus = axes[a]
        send(f"{a}+s2{role}", piece(a, 2, role, halves[0]), rf.at[0, role], plus)
        send(f"{a}-s2{role}", piece(a, 2, role, halves[1]), rf.at[1, role], minus)

    def send_near(a, role):
        _, _, rs, plus, minus = axes[a]
        send(f"{a}+s1{role}", piece(a, 0, role, direct[1]), rs.at[0, role, at(direct[1])], plus)
        send(f"{a}-s1{role}", piece(a, 1, role, direct[0]), rs.at[1, role, at(direct[0])], minus)

    def send_mix_x():
        send("mx1", piece("x", 0, 0, by_z[1]), mix.at[1], p1)
        send("mx0", piece("x", 1, 0, by_z[0]), mix.at[0], p1)

    hop = [xrs.at[1, 0, at(by_z[0])], xrs.at[0, 0, at(by_z[1])]]
    end = [yrs.at[1, 0, at(by_z[0])], yrs.at[0, 0, at(by_z[1])]]

    def send_mix_y():
        send("my1", piece("y", 0, 0, by_z[1]), hop[1], p2)
        send("my0", piece("y", 1, 0, by_z[0]), hop[0], p2)

    def pass_mix_y(h):
        arrived(f"my{h}", hop[h])
        send(f"mz{h}", hop[h], end[h], p1)

    def send_mixed(a, h):
        _, _, rs, plus, minus = axes[a]
        term = mix.at[h] if a == "x" else end[h]
        arrived(f"mx{h}" if a == "x" else f"mz{h}", term)
        mine = piece(a, 1 - h, 1, by_z[h])
        add_to(mine, term)
        send(f"{a}m{h}", mine, rs.at[1 - h, 1, at(by_z[h])], plus if h else minus)

    def send_sum(a, role):
        _, rf, rs, plus, minus = axes[a]
        for d, (sign, peer) in enumerate((("+", plus), ("-", minus))):
            arrived(f"{a}{sign}s2{role}", rf.at[d, role])
            mine = piece(a, d, role, halves[d])
            add_to(mine, rf.at[d, role])
            send(f"{a}{sign}s0{role}", mine, rs.at[d, role, at(halves[d])], peer)

    def sums_arrived(a, role):
        rs = axes[a][2]
        for d, sign in enumerate("+-"):
            arrived(f"{a}{sign}s1{role}", rs.at[d, role, at(direct[1 - d])])
            if role:
                arrived(f"{a}m{1 - d}", rs.at[d, role, at(by_z[1 - d])])
            arrived(f"{a}{sign}s0{role}", rs.at[d, role, at(halves[d])])

    def store_to(ref):
        def store(cols, value):
            ref[:, cols] = value.astype(BF16)
        return store

    place = {1: 0, 3: 1, 2: 2}

    def x_part(k, role):
        zz = z_of["x"][role]
        weigh(px[k], zz)
        loop_part((px[k] * 2 + zz) * p_dev, p_dev, store_to(piece("x", place[k], role, whole)))

    def y_part(k, role):
        pool_weights(py[k], z_of["y"][role], 0)
        pool_part(p_dev, store_to(piece("y", place[k], role, whole)))

    x_part(2, 0)
    send_far("x", 0)
    loss_finish(0)
    loss_start(1)
    arrived("w", w2.at[1])
    y_part(2, 0)
    loss_finish(1)
    send_far("y", 0)
    loss_start(2)
    send("o4", prow(py[3], oh), orow(py[3], oh), sib)
    send("o5", prow(py[1], oh), orow(py[1], oh), sib)
    send("o6", prow(py[2], oh), orow(py[2], oh), sib)
    x_part(1, 0)
    x_part(3, 0)
    send_near("x", 0)
    loss_finish(2)
    loss_start(3)
    send_mix_x()
    y_part(1, 0)
    y_part(3, 0)
    send_near("y", 0)
    loss_finish(3)
    send_mix_y()
    loss_start(4)
    for k in (2, 1, 3):
        x_part(k, 1)
    weigh(x, 0)
    weigh(x, 1)
    send_sum("x", 0)
    y_part(2, 1)
    send_sum("y", 0)
    loss_finish(4)
    loss_start(5)
    send_far("x", 1)
    send_far("y", 1)
    y_part(1, 1)
    y_part(3, 1)
    send_near("x", 1)
    send_near("y", 1)

    for a in "xy":
        sent(f"{a}+s20")
        sent(f"{a}-s20")

    hand_x = xs.at[2, rows(oz * p_dev, p_dev)]
    hand_y = ys.at[2, rows(oh * p_dev, p_dev)]

    def split(first, value):
        low, high = value[:p_dev], value[p_dev:]
        return jnp.where(first, low, high), jnp.where(first, high, low)

    def store_x(cols, value):
        mine, handed = split(zl == 0, value)
        s[:, cols] = mine
        hand_x[:, cols] = handed.astype(BF16)

    def store_y(cols, value):
        mine, handed = split(zh == 0, value)
        s[:, cols] += mine
        hand_y[:, cols] = handed.astype(BF16)

    loop_part(x * 2 * p_dev, 2 * p_dev, store_x)
    pool_weights(y, 0, 0)
    pool_weights(y, 1, p_dev)
    pool_part(2 * p_dev, store_y)
    pass_mix_y(1)
    send_mixed("x", 1)
    send_mixed("x", 0)

    for c in range(blocks):
        wall[:, c * p_dev:(c + 1) * p_dev] = (
            wt[c * p_dev:(c + 1) * p_dev, :].astype(F32).T.astype(BF16)
        )
    loop_rows = blocks * p_dev

    @pl.loop(0, q_dev // 128)
    def _(n):
        part = rows(n * 128, 128, 128)
        names = jnp.broadcast_to(ids[0, 0:1, part].astype(F32), (128, 128)).T
        values = jnp.broadcast_to(w2[0, 0:1, part], (128, 128)).T
        lane = lax.broadcasted_iota(jnp.int32, (128, 128), 1)
        for k in range(2):
            cc = core if k == 0 else 1 - core
            for slot in range(8):
                base = pool_base(slot // 2, slot % 2, cc)
                at = loop_rows + (k * 8 + slot) * p_dev
                wall[part, at:at + p_dev] = jnp.where(
                    names == (lane + base).astype(F32), values, 0.0
                ).astype(BF16)

    arrived("oo", orow(y, zh))
    arrived("o3", orow(py[3], zh))
    arrived("o1", orow(py[1], zh))
    arrived("op", orow(y, oh))
    arrived("o2", orow(py[2], zh))
    arrived("o4", orow(py[3], oh))
    arrived("o5", orow(py[1], oh))
    arrived("o6", orow(py[2], oh))

    tile = dqt.shape[2]
    tiles = width // tile
    pool_rows = pbuf.shape[0]

    def tile_in(t):
        k = lax.rem(t, 2)
        return pltpu.make_async_copy(
            other_hbm.at[:, rows(t * tile, tile, tile)], otile.at[k], csem.at[k]
        )

    def tile_out(t):
        k = lax.rem(t, 2)
        return pltpu.make_async_copy(
            dqt.at[k], dq_hbm.at[:, rows(t * tile, tile, tile)], csem.at[2 + k]
        )

    tile_in(0).start()

    def query_slope(first, last):
        @pl.loop(first, last)
        def _(t):
            k = lax.rem(t, 2)

            @pl.when(t + 1 < tiles)
            def _():
                tile_in(t + 1).start()

            @pl.when(t >= 2)
            def _():
                tile_out(t - 2).wait()

            cols = rows(t * tile, tile, tile)
            tile_in(t).wait()
            acc = jnp.dot(
                wall[:, 0:loop_rows], lbuf[:, cols], preferred_element_type=F32
            )
            acc += jnp.dot(
                wall[:, loop_rows:loop_rows + pool_rows], pbuf[:, cols],
                preferred_element_type=F32,
            )
            acc += jnp.dot(
                wall[:, loop_rows + pool_rows:], otile[k], preferred_element_type=F32
            )
            dqt[k] = (scale * acc).astype(BF16)
            tile_out(t).start()

    query_slope(0, tiles // 4)
    pass_mix_y(0)
    loss_finish(5)
    loss_start(6)
    query_slope(tiles // 4, tiles * 3 // 8)

    parts = [pl.ds(0, moved), pl.ds(moved, p_dev - 2 * moved), pl.ds(p_dev - moved, moved)]
    signs = [(0,), (0, 1), (1,)]
    sums_arrived("y", 0)
    for k, part in enumerate(parts):
        add_to(hand_y.at[part], *(yrs.at[d, 0, part] for d in signs[k]))
        send(f"zh{k}", hand_y.at[part], zrh.at[part], p2)
    send_mixed("y", 1)
    query_slope(tiles * 3 // 8, tiles * 5 // 8)
    sums_arrived("x", 0)
    send_mixed("y", 0)
    send_sum("x", 1)
    send_sum("y", 1)
    for k, part in enumerate(parts):
        arrived(f"zh{k}", zrh.at[part])
        add_to(hand_x.at[part], zrh.at[part], *(xrs.at[d, 0, part] for d in signs[k]))
        send(f"zl{k}", hand_x.at[part], zrl.at[part], p1)
        query_slope(tiles * (10 + 2 * k) // 16, tiles * (12 + 2 * k) // 16)
    loss_finish(6)
    loss_ref[0] = jnp.max(lsum[...]) / (q_dev * lax.axis_size("blk") * lax.axis_size("grp"))

    sums_arrived("x", 1)
    for h, part in enumerate(parts):
        arrived(f"zl{h}", zrl.at[part])

        @pl.loop(0, width // step, unroll=2)
        def _(t):
            cols = rows(t * step, step, step)
            s[part, cols] += (
                xrs[0, 1, part, cols].astype(F32)
                + xrs[1, 1, part, cols].astype(F32)
                + zrl[part, cols].astype(F32)
            )

    sums_arrived("y", 1)
    sent("y+s21")
    sent("y-s21")
    result = ys.at[2, rows(zh * p_dev, p_dev)]
    outs = []
    for h, part in enumerate(parts):
        @pl.loop(0, width // step, unroll=2)
        def _(t):
            cols = rows(t * step, step, step)
            result[part, cols] = (
                s[part, cols]
                + yrs[0, 1, part, cols].astype(F32)
                + yrs[1, 1, part, cols].astype(F32)
            ).astype(BF16)

        copy = pltpu.make_async_copy(result.at[part], dp_hbm.at[part], csem.at[4 + h])
        copy.start()
        outs.append(copy)
    tile_out(tiles - 2).wait()
    tile_out(tiles - 1).wait()
    for copy in outs:
        copy.wait()
    for name in list(started):
        sent(name)


def shards(queries, passages, positive_ids, hard_ids):
    q_dev, width = queries.shape
    p_dev = passages.shape[0]
    half = p_dev // 2
    moved = half * 3 // 4
    vmem = pltpu.VMEM
    hbm = pl.BlockSpec(memory_space=pl.ANY)
    block = pl.BlockSpec(memory_space=pltpu.VMEM)
    loss, slope, grad, _ = pl.pallas_call(
        kernel,
        out_shape=(
            jax.ShapeDtypeStruct((1,), F32),
            jax.ShapeDtypeStruct((q_dev, width), BF16),
            jax.ShapeDtypeStruct((p_dev, width), BF16),
            jax.ShapeDtypeStruct((8 * p_dev, width), BF16),
        ),
        in_specs=[hbm, hbm, block, block],
        out_specs=(pl.BlockSpec(memory_space=pltpu.SMEM), hbm, hbm, hbm),
        scratch_shapes=[
            vmem((8 * p_dev, width), BF16),
            vmem((8 * p_dev, width), BF16),
            vmem((2 * q_dev, width), BF16),
            vmem((p_dev, 8 * q_dev), F32),
            vmem((8 * p_dev, q_dev), BF16),
            vmem((q_dev, 24 * p_dev), BF16),
            vmem((2 * p_dev, 2 * q_dev), BF16),
            vmem((3, 2 * p_dev, width), BF16),
            vmem((3, 2 * p_dev, width), BF16),
            vmem((2, 2, half, width), BF16),
            vmem((2, 2, p_dev, width), BF16),
            vmem((2, 2, half, width), BF16),
            vmem((2, 2, p_dev, width), BF16),
            vmem((p_dev, width), BF16),
            vmem((p_dev, width), BF16),
            vmem((2, moved, width), BF16),
            vmem((2, moved, width), BF16),
            vmem((2, 8, q_dev), jnp.int32),
            vmem((2, 8, q_dev), F32),
            vmem((8, q_dev), F32),
            vmem((2, 8, q_dev), F32),
            vmem((8, q_dev), F32),
            vmem((8, q_dev), F32),
            vmem((8, q_dev), F32),
            vmem((8, 128), F32),
            vmem((7, 8, 128), F32),
            vmem((7, 8, 128), F32),
            vmem((2, 8 * p_dev, 256), BF16),
            vmem((2, q_dev, 256), BF16),
            pltpu.SemaphoreType.DMA((COPIES,)),
            pltpu.SemaphoreType.DMA((COPIES,)),
            pltpu.SemaphoreType.DMA((7,)),
        ],
        compiler_params=pltpu.CompilerParams(
            collective_id=0, has_side_effects=True, vmem_limit_bytes=63 * 2**20
        ),
        cost_estimate=pl.CostEstimate(
            flops=2 * q_dev * width * 9 * 8 * p_dev,
            bytes_accessed=40 * 2**20,
            transcendentals=2 * 8 * p_dev * q_dev,
        ),
    )(
        queries,
        passages,
        positive_ids.reshape(1, q_dev),
        hard_ids.reshape(1, q_dev),
    )
    return loss[0], slope, grad


def solution(mesh):
    return jax.shard_map(
        shards,
        mesh=mesh,
        in_specs=(
            P(("blk", "grp"), None),
            P(("blk", "grp"), None),
            P(("blk", "grp")),
            P(("blk", "grp"), None),
        ),
        out_specs=(P(), P(("blk", "grp"), None), P(("blk", "grp"), None)),
        check_vma=False,
    )
```

```python
import functools

import jax
import jax.numpy as jnp
from jax import lax
from jax.experimental import pallas as pl
from jax.experimental.pallas import tpu as pltpu
from jax.sharding import PartitionSpec as P

logit_scaling_coefficient = 20.0
MESH = pl.DeviceIdType.MESH
BF16 = jnp.bfloat16
F32 = jnp.float32
COPIES = 112
NT = (((1,), (1,)), ((), ()))


def rows(start, size, multiple=64):
    return pl.ds(pl.multiple_of(start, multiple), size)


def kernel(
    q_hbm, p_hbm, pos_ref, hid_ref,
    loss_ref, dq_hbm, dp_hbm, other_hbm,
    lbuf, pbuf, qbuf, s, wt, wall, wht, xs, ys, xrf, xrs, yrf, yrs, zrh, zrl, via, mix,
    ids, hs, hin, w2, top, run, hit, lsum, lsend, lrecv, otile, dqt,
    ssem, rsem, csem,
):
    q_dev, width = q_hbm.shape
    p_dev = p_hbm.shape[0]
    half = p_dev // 2
    scale = logit_scaling_coefficient

    b = lax.axis_index("blk")
    g = lax.axis_index("grp")
    x, zl = lax.div(b, 2), lax.rem(b, 2)
    zh, y, core = lax.div(g, 8), lax.div(lax.rem(g, 8), 2), lax.rem(g, 2)
    pb = x * 2 + 1 - zl
    px = [lax.rem(x + k, 4) for k in range(4)]
    py = [lax.rem(y + k, 4) for k in range(4)]
    xp = (px[1] * 2 + zl, g)
    xm = (px[3] * 2 + zl, g)
    yp = (b, zh * 8 + py[1] * 2 + core)
    ym = (b, zh * 8 + py[3] * 2 + core)
    p1 = (pb, g)
    p2 = (pb, lax.rem(g + 8, 16))
    sib = (b, zh * 8 + y * 2 + 1 - core)

    number = {}
    started = {}

    def describe(name, src, dst, peer):
        k = number.setdefault(name, len(number))
        return pltpu.make_async_remote_copy(
            src_ref=src, dst_ref=dst, send_sem=ssem.at[k], recv_sem=rsem.at[k],
            device_id=peer, device_id_type=MESH,
        )

    def send(name, src, dst, peer):
        copy = describe(name, src, dst, peer)
        copy.start()
        started[name] = copy

    def sent(name):
        started.pop(name).wait_send()

    def arrived(name, dst):
        describe(name, dst, dst, sib).wait_recv()

    quarter = half // 2
    moved = half * 3 // 4
    halves = [(0, half), (half, half)]
    by_z = [(0, moved), (p_dev - moved, moved)]
    direct = [(moved, half - moved), (half, half - moved)]
    whole = (0, p_dev)

    def lrow(xx, zz, part=whole):
        return lbuf.at[rows((xx * 2 + zz) * p_dev + part[0], part[1], 16)]

    def prow(yy, zz, part=whole):
        return pbuf.at[rows((yy * 2 + zz) * p_dev + part[0], part[1], 16)]

    def orow(yy, zz):
        return other_hbm.at[rows((yy * 2 + zz) * p_dev, p_dev)]

    local = [
        pltpu.make_async_copy(q_hbm, qbuf.at[pl.ds(0, q_dev)], csem.at[0]),
        pltpu.make_async_copy(p_hbm, lrow(x, zl), csem.at[1]),
        pltpu.make_async_copy(p_hbm, prow(y, zh), csem.at[2]),
    ]
    for copy in local:
        copy.start()
    ids[0] = jnp.broadcast_to(hid_ref[...], ids.shape[1:])
    hs[...] = jnp.zeros(hs.shape, F32)
    top[...] = jnp.full(top.shape, -jnp.inf, F32)
    run[...] = jnp.zeros(run.shape, F32)
    hit[...] = jnp.zeros(hit.shape, F32)

    barrier = pltpu.get_barrier_semaphore()
    for peer in (xp, xm, yp, ym, p1, p2, sib):
        pl.semaphore_signal(barrier, inc=1, device_id=peer, device_id_type=MESH)
    pl.semaphore_wait(barrier, 7)

    own = [p_hbm.at[pl.ds(h * half, half)] for h in range(2)]
    quarters = [(k * quarter, quarter) for k in range(4)]

    for k in range(4):
        send(f"z{k}", p_hbm.at[pl.ds(k * quarter, quarter)], lrow(x, zl, quarters[k]), p1)
    for h in range(2):
        r = 1 - h
        send(f"x+o{h}", own[h], lrow(x, zl, halves[h]), xp)
        send(f"x-o{r}", own[r], lrow(x, zl, halves[r]), xm)
        send(f"y+o{h}", own[h], prow(y, zh, halves[h]), yp)
        send(f"y-o{r}", own[r], prow(y, zh, halves[r]), ym)
    send("ids", ids.at[0], ids.at[1], sib)
    send("q", q_hbm, qbuf.at[pl.ds(q_dev, q_dev)], sib)

    def score_loop(xx, zz):
        c = xx * 2 + zz
        acc = scale * lax.dot_general(
            lbuf[rows(c * p_dev, p_dev), :], qbuf[pl.ds(0, q_dev), :], NT,
            preferred_element_type=F32,
        )
        s[:, rows(c * q_dev, q_dev, q_dev)] = acc
        old = top[0:1]
        peak = jnp.maximum(old, jnp.max(acc, axis=0, keepdims=True))
        total = run[0:1] * jnp.exp(old - peak) + jnp.sum(
            jnp.exp(acc - peak), axis=0, keepdims=True
        )
        row = lax.broadcasted_iota(jnp.int32, acc.shape, 0) + c * p_dev
        top[...] = jnp.broadcast_to(peak, top.shape)
        run[...] = jnp.broadcast_to(total, run.shape)
        hit[...] += jnp.sum(jnp.where(row == pos_ref[...], acc, 0.0), axis=0, keepdims=True)

    def pool_base(yy, zz, cc):
        return (zz * 8 + yy * 2 + cc) * p_dev

    def score_pool(yy, zz):
        slot = yy * 2 + zz
        base = pool_base(yy, zz, core)

        @pl.loop(0, 2)
        def _(k):
            acc = lax.dot_general(
                pbuf[rows(slot * p_dev, p_dev), :], qbuf[rows(k * q_dev, q_dev, q_dev), :], NT,
                preferred_element_type=F32,
            )
            row = lax.broadcasted_iota(jnp.int32, acc.shape, 0) + base
            named = jnp.where(row == ids[k, 0:1, :], scale * acc, 0.0)
            hs[k] += jnp.sum(named, axis=0, keepdims=True)

    oz, oh = 1 - zl, 1 - zh

    for copy in local:
        copy.wait()
    send("oo", prow(y, zh), orow(y, zh), sib)
    score_loop(x, zl)

    def pass_x(name, xx, zz, part, peer):
        send(name, lrow(xx, zz, part), lrow(xx, zz, part), peer)

    def pass_y(name, yy, zz, part, peer):
        send(name, prow(yy, zz, part), prow(yy, zz, part), peer)

    def pass_z(k):
        arrived(f"z{k}", lrow(x, oz, quarters[k]))
        send(f"h{k}", lrow(x, oz, quarters[k]), prow(y, zh, quarters[k]), p2)

    pass_z(0)
    pass_z(1)
    arrived("x+o0", lrow(px[3], zl, halves[0]))
    pass_x("x+f", px[3], zl, halves[0], xp)
    arrived("x-o1", lrow(px[1], zl, halves[1]))
    pass_x("x-f", px[1], zl, halves[1], xm)
    arrived("y+o0", prow(py[3], zh, halves[0]))
    pass_y("y+f", py[3], zh, halves[0], yp)
    arrived("y-o1", prow(py[1], zh, halves[1]))
    pass_y("y-f", py[1], zh, halves[1], ym)
    pass_x("x+p0", x, oz, halves[0], xp)
    arrived("ids", ids.at[1])
    arrived("q", qbuf.at[pl.ds(q_dev, q_dev)])
    score_pool(y, zh)

    pass_z(2)
    arrived("h0", prow(y, oh, quarters[0]))
    arrived("h1", prow(y, oh, quarters[1]))
    pass_y("y+p0", y, oh, halves[0], yp)
    pass_z(3)
    pass_x("x-p1", x, oz, halves[1], xm)
    pass_x("x+p1", x, oz, direct[1], xp)
    pass_x("x-p0", x, oz, direct[0], xm)
    arrived("x+o1", lrow(px[3], zl, halves[1]))
    pass_x("zx1", px[3], zl, by_z[1], p1)
    arrived("x-o0", lrow(px[1], zl, halves[0]))
    pass_x("zx0", px[1], zl, by_z[0], p1)
    arrived("y+o1", prow(py[3], zh, halves[1]))
    send("ty1", prow(py[3], zh, by_z[1]), via.at[1], p2)
    arrived("y-o0", prow(py[1], zh, halves[0]))
    send("ty0", prow(py[1], zh, by_z[0]), via.at[0], p2)
    send("o3", prow(py[3], zh), orow(py[3], zh), sib)
    send("o1", prow(py[1], zh), orow(py[1], zh), sib)
    score_loop(x, oz)
    score_loop(px[3], zl)
    score_loop(px[1], zl)
    arrived("h2", prow(y, oh, quarters[2]))
    arrived("h3", prow(y, oh, quarters[3]))
    pass_y("y-p1", y, oh, halves[1], ym)
    pass_y("y+p1", y, oh, direct[1], yp)
    pass_y("y-p0", y, oh, direct[0], ym)
    send("op", prow(y, oh), orow(y, oh), sib)
    score_pool(py[3], zh)
    score_pool(py[1], zh)
    arrived("x+f", lrow(px[2], zl, halves[0]))
    arrived("x-f", lrow(px[2], zl, halves[1]))
    score_loop(px[2], zl)
    arrived("ty1", via.at[1])
    send("tz1", via.at[1], prow(py[3], oh, by_z[1]), p1)
    score_pool(y, oh)
    arrived("y+f", prow(py[2], zh, halves[0]))
    arrived("y-f", prow(py[2], zh, halves[1]))
    send("o2", prow(py[2], zh), orow(py[2], zh), sib)
    score_pool(py[2], zh)
    arrived("x+p0", lrow(px[3], oz, halves[0]))
    pass_x("x+g", px[3], oz, halves[0], xp)
    arrived("x-p1", lrow(px[1], oz, halves[1]))
    pass_x("x-g", px[1], oz, halves[1], xm)
    arrived("y+p0", prow(py[3], oh, halves[0]))
    pass_y("y+g", py[3], oh, halves[0], yp)
    arrived("y-p1", prow(py[1], oh, halves[1]))
    pass_y("y-g", py[1], oh, halves[1], ym)
    arrived("ty0", via.at[0])
    send("tz0", via.at[0], prow(py[1], oh, by_z[0]), p1)
    arrived("x+p1", lrow(px[3], oz, direct[1]))
    arrived("zx1", lrow(px[3], oz, by_z[1]))
    score_loop(px[3], oz)
    arrived("x-p0", lrow(px[1], oz, direct[0]))
    arrived("zx0", lrow(px[1], oz, by_z[0]))
    score_loop(px[1], oz)
    arrived("y+p1", prow(py[3], oh, direct[1]))
    arrived("tz1", prow(py[3], oh, by_z[1]))
    score_pool(py[3], oh)
    arrived("y-p0", prow(py[1], oh, direct[0]))
    arrived("tz0", prow(py[1], oh, by_z[0]))
    score_pool(py[1], oh)
    arrived("y+g", prow(py[2], oh, halves[0]))
    arrived("y-g", prow(py[2], oh, halves[1]))
    score_pool(py[2], oh)
    send("hs", hs.at[1], hin, sib)
    arrived("x+g", lrow(px[2], oz, halves[0]))
    arrived("x-g", lrow(px[2], oz, halves[1]))
    score_loop(px[2], oz)

    arrived("hs", hin)
    hard = hs[0, 0:1, :] + hin[0:1, :]
    peak = jnp.maximum(top[0:1], hard)
    total = run[0:1] * jnp.exp(top[0:1] - peak) + jnp.exp(hard - peak)
    log_total = peak + jnp.log(total)
    w_hard = jnp.exp(hard - log_total).astype(BF16).astype(F32)
    w2[0] = jnp.broadcast_to(w_hard, w2.shape[1:])
    send("w", w2.at[0], w2.at[1], sib)
    lsum[...] = jnp.broadcast_to(
        jnp.sum(log_total - hit[0:1], axis=1, keepdims=True), lsum.shape
    )
    blocks = s.shape[1] // q_dev

    def weigh(xx, zz):
        c = xx * 2 + zz
        part = s[:, rows(c * q_dev, q_dev, q_dev)]
        row = lax.broadcasted_iota(jnp.int32, part.shape, 0) + c * p_dev
        one = jnp.where(row == pos_ref[...], 1.0, 0.0)
        wt[rows(c * p_dev, p_dev), :] = (jnp.exp(part - log_total) - one).astype(BF16)

    loss_peers = [
        (lax.rem(b + 2 + 4 * lax.rem(x, 2), 8), g),
        (b, zh * 8 + lax.rem(y + 1 + 2 * lax.rem(y, 2), 4) * 2 + core),
        p1,
        p2,
        sib,
        ((3 - x) * 2 + zl, g),
        (b, zh * 8 + (3 - y) * 2 + core),
    ]

    def loss_start(k):
        lsend[k] = lsum[...]
        send(f"l{k}", lsend.at[k], lrecv.at[k], loss_peers[k])

    def loss_finish(k):
        arrived(f"l{k}", lrecv.at[k])
        lsum[...] = lsend[k] + lrecv[k]

    loss_start(0)

    step = 512

    def columns(count):
        return width // 2 if count == p_dev else step

    def loop_part(start, count, store):
        n = columns(count)

        @pl.loop(0, width // n, unroll=min(4, width // n // 2))
        def _(t):
            cols = rows(t * n, n, n)
            store(cols, scale * jnp.dot(
                wt[rows(start, count), :], qbuf[pl.ds(0, q_dev), cols],
                preferred_element_type=F32,
            ))

    def pool_weights(yy, zz, at):
        base = pool_base(yy, zz, core)
        for k in range(2):
            row = lax.broadcasted_iota(jnp.int32, (p_dev, q_dev), 0) + base
            wht[at:at + p_dev, k * q_dev:(k + 1) * q_dev] = jnp.where(
                row == ids[k, 0:1, :], w2[k, 0:1, :], 0.0
            ).astype(BF16)

    def pool_part(count, store):
        n = columns(count)

        @pl.loop(0, width // n, unroll=min(4, width // n // 2))
        def _(t):
            cols = rows(t * n, n, n)
            store(cols, scale * jnp.dot(
                wht[pl.ds(0, count), :], qbuf[:, cols], preferred_element_type=F32
            ))

    z_of = {"x": (oz, zl), "y": (oh, zh)}
    axes = {"x": (xs, xrf, xrs, xp, xm), "y": (ys, yrf, yrs, yp, ym)}

    def piece(a, slot, role, part):
        return axes[a][0].at[slot, rows(z_of[a][role] * p_dev + part[0], part[1], 16)]

    def at(part):
        return pl.ds(part[0], part[1])

    def add_to(dst, *terms):
        @pl.loop(0, width // step, unroll=2)
        def _(t):
            cols = rows(t * step, step, step)
            total = dst[:, cols].astype(F32)
            for term in terms:
                total += term[:, cols].astype(F32)
            dst[:, cols] = total.astype(BF16)

    def send_far(a, role):
        _, rf, _, plus, minus = axes[a]
        send(f"{a}+s2{role}", piece(a, 2, role, halves[0]), rf.at[0, role], plus)
        send(f"{a}-s2{role}", piece(a, 2, role, halves[1]), rf.at[1, role], minus)

    def send_near(a, role):
        _, _, rs, plus, minus = axes[a]
        send(f"{a}+s1{role}", piece(a, 0, role, direct[1]), rs.at[0, role, at(direct[1])], plus)
        send(f"{a}-s1{role}", piece(a, 1, role, direct[0]), rs.at[1, role, at(direct[0])], minus)

    def send_mix_x():
        send("mx1", piece("x", 0, 0, by_z[1]), mix.at[1], p1)
        send("mx0", piece("x", 1, 0, by_z[0]), mix.at[0], p1)

    hop = [xrs.at[1, 0, at(by_z[0])], xrs.at[0, 0, at(by_z[1])]]
    end = [yrs.at[1, 0, at(by_z[0])], yrs.at[0, 0, at(by_z[1])]]

    def send_mix_y():
        send("my1", piece("y", 0, 0, by_z[1]), hop[1], p2)
        send("my0", piece("y", 1, 0, by_z[0]), hop[0], p2)

    def pass_mix_y(h):
        arrived(f"my{h}", hop[h])
        send(f"mz{h}", hop[h], end[h], p1)

    def send_mixed(a, h):
        _, _, rs, plus, minus = axes[a]
        term = mix.at[h] if a == "x" else end[h]
        arrived(f"mx{h}" if a == "x" else f"mz{h}", term)
        mine = piece(a, 1 - h, 1, by_z[h])
        add_to(mine, term)
        send(f"{a}m{h}", mine, rs.at[1 - h, 1, at(by_z[h])], plus if h else minus)

    def send_sum(a, role):
        _, rf, rs, plus, minus = axes[a]
        for d, (sign, peer) in enumerate((("+", plus), ("-", minus))):
            arrived(f"{a}{sign}s2{role}", rf.at[d, role])
            mine = piece(a, d, role, halves[d])
            add_to(mine, rf.at[d, role])
            send(f"{a}{sign}s0{role}", mine, rs.at[d, role, at(halves[d])], peer)

    def sums_arrived(a, role):
        rs = axes[a][2]
        for d, sign in enumerate("+-"):
            arrived(f"{a}{sign}s1{role}", rs.at[d, role, at(direct[1 - d])])
            if role:
                arrived(f"{a}m{1 - d}", rs.at[d, role, at(by_z[1 - d])])
            arrived(f"{a}{sign}s0{role}", rs.at[d, role, at(halves[d])])

    def store_to(ref):
        def store(cols, value):
            ref[:, cols] = value.astype(BF16)
        return store

    place = {1: 0, 3: 1, 2: 2}

    def x_part(k, role):
        zz = z_of["x"][role]
        weigh(px[k], zz)
        loop_part((px[k] * 2 + zz) * p_dev, p_dev, store_to(piece("x", place[k], role, whole)))

    def y_part(k, role):
        pool_weights(py[k], z_of["y"][role], 0)
        pool_part(p_dev, store_to(piece("y", place[k], role, whole)))

    x_part(2, 0)
    send_far("x", 0)
    loss_finish(0)
    loss_start(1)
    arrived("w", w2.at[1])
    y_part(2, 0)
    loss_finish(1)
    send_far("y", 0)
    loss_start(2)
    send("o4", prow(py[3], oh), orow(py[3], oh), sib)
    send("o5", prow(py[1], oh), orow(py[1], oh), sib)
    send("o6", prow(py[2], oh), orow(py[2], oh), sib)
    x_part(1, 0)
    x_part(3, 0)
    send_near("x", 0)
    loss_finish(2)
    loss_start(3)
    send_mix_x()
    y_part(1, 0)
    y_part(3, 0)
    send_near("y", 0)
    loss_finish(3)
    send_mix_y()
    loss_start(4)
    for k in (2, 1, 3):
        x_part(k, 1)
    weigh(x, 0)
    weigh(x, 1)
    send_sum("x", 0)
    y_part(2, 1)
    send_sum("y", 0)
    loss_finish(4)
    loss_start(5)
    send_far("x", 1)
    send_far("y", 1)
    y_part(1, 1)
    y_part(3, 1)
    send_near("x", 1)
    send_near("y", 1)

    for a in "xy":
        sent(f"{a}+s20")
        sent(f"{a}-s20")

    hand_x = xs.at[2, rows(oz * p_dev, p_dev)]
    hand_y = ys.at[2, rows(oh * p_dev, p_dev)]

    def split(first, value):
        low, high = value[:p_dev], value[p_dev:]
        return jnp.where(first, low, high), jnp.where(first, high, low)

    def store_x(cols, value):
        mine, handed = split(zl == 0, value)
        s[:, cols] = mine
        hand_x[:, cols] = handed.astype(BF16)

    def store_y(cols, value):
        mine, handed = split(zh == 0, value)
        s[:, cols] += mine
        hand_y[:, cols] = handed.astype(BF16)

    loop_part(x * 2 * p_dev, 2 * p_dev, store_x)
    pool_weights(y, 0, 0)
    pool_weights(y, 1, p_dev)
    pool_part(2 * p_dev, store_y)
    pass_mix_y(1)
    send_mixed("x", 1)
    send_mixed("x", 0)

    for c in range(blocks):
        wall[:, c * p_dev:(c + 1) * p_dev] = (
            wt[c * p_dev:(c + 1) * p_dev, :].astype(F32).T.astype(BF16)
        )
    loop_rows = blocks * p_dev

    @pl.loop(0, q_dev // 128)
    def _(n):
        part = rows(n * 128, 128, 128)
        names = jnp.broadcast_to(ids[0, 0:1, part].astype(F32), (128, 128)).T
        values = jnp.broadcast_to(w2[0, 0:1, part], (128, 128)).T
        lane = lax.broadcasted_iota(jnp.int32, (128, 128), 1)
        for k in range(2):
            cc = core if k == 0 else 1 - core
            for slot in range(8):
                base = pool_base(slot // 2, slot % 2, cc)
                at = loop_rows + (k * 8 + slot) * p_dev
                wall[part, at:at + p_dev] = jnp.where(
                    names == (lane + base).astype(F32), values, 0.0
                ).astype(BF16)

    arrived("oo", orow(y, zh))
    arrived("o3", orow(py[3], zh))
    arrived("o1", orow(py[1], zh))
    arrived("op", orow(y, oh))
    arrived("o2", orow(py[2], zh))
    arrived("o4", orow(py[3], oh))
    arrived("o5", orow(py[1], oh))
    arrived("o6", orow(py[2], oh))

    tile = dqt.shape[2]
    tiles = width // tile
    pool_rows = pbuf.shape[0]

    def tile_in(t):
        k = lax.rem(t, 2)
        return pltpu.make_async_copy(
            other_hbm.at[:, rows(t * tile, tile, tile)], otile.at[k], csem.at[k]
        )

    def tile_out(t):
        k = lax.rem(t, 2)
        return pltpu.make_async_copy(
            dqt.at[k], dq_hbm.at[:, rows(t * tile, tile, tile)], csem.at[2 + k]
        )

    tile_in(0).start()

    def query_slope(first, last):
        @pl.loop(first, last)
        def _(t):
            k = lax.rem(t, 2)

            @pl.when(t + 1 < tiles)
            def _():
                tile_in(t + 1).start()

            @pl.when(t >= 2)
            def _():
                tile_out(t - 2).wait()

            cols = rows(t * tile, tile, tile)
            tile_in(t).wait()
            acc = jnp.dot(
                wall[:, 0:loop_rows], lbuf[:, cols], preferred_element_type=F32
            )
            acc += jnp.dot(
                wall[:, loop_rows:loop_rows + pool_rows], pbuf[:, cols],
                preferred_element_type=F32,
            )
            acc += jnp.dot(
                wall[:, loop_rows + pool_rows:], otile[k], preferred_element_type=F32
            )
            dqt[k] = (scale * acc).astype(BF16)
            tile_out(t).start()

    query_slope(0, tiles // 4)
    pass_mix_y(0)
    loss_finish(5)
    loss_start(6)
    query_slope(tiles // 4, tiles * 3 // 8)

    parts = [pl.ds(0, moved), pl.ds(moved, p_dev - 2 * moved), pl.ds(p_dev - moved, moved)]
    signs = [(0,), (0, 1), (1,)]
    sums_arrived("y", 0)
    for k, part in enumerate(parts):
        add_to(hand_y.at[part], *(yrs.at[d, 0, part] for d in signs[k]))
        send(f"zh{k}", hand_y.at[part], zrh.at[part], p2)
    send_mixed("y", 1)
    query_slope(tiles * 3 // 8, tiles * 5 // 8)
    sums_arrived("x", 0)
    send_mixed("y", 0)
    send_sum("x", 1)
    send_sum("y", 1)
    for k, part in enumerate(parts):
        arrived(f"zh{k}", zrh.at[part])
        add_to(hand_x.at[part], zrh.at[part], *(xrs.at[d, 0, part] for d in signs[k]))
        send(f"zl{k}", hand_x.at[part], zrl.at[part], p1)
        query_slope(tiles * (10 + 2 * k) // 16, tiles * (12 + 2 * k) // 16)
    loss_finish(6)
    loss_ref[0] = jnp.max(lsum[...]) / (q_dev * lax.axis_size("blk") * lax.axis_size("grp"))

    sums_arrived("x", 1)
    for h, part in enumerate(parts):
        arrived(f"zl{h}", zrl.at[part])

        @pl.loop(0, width // step, unroll=2)
        def _(t):
            cols = rows(t * step, step, step)
            s[part, cols] += (
                xrs[0, 1, part, cols].astype(F32)
                + xrs[1, 1, part, cols].astype(F32)
                + zrl[part, cols].astype(F32)
            )

    sums_arrived("y", 1)
    sent("y+s21")
    sent("y-s21")
    result = ys.at[2, rows(zh * p_dev, p_dev)]
    outs = []
    for h, part in enumerate(parts):
        @pl.loop(0, width // step, unroll=2)
        def _(t):
            cols = rows(t * step, step, step)
            result[part, cols] = (
                s[part, cols]
                + yrs[0, 1, part, cols].astype(F32)
                + yrs[1, 1, part, cols].astype(F32)
            ).astype(BF16)

        copy = pltpu.make_async_copy(result.at[part], dp_hbm.at[part], csem.at[4 + h])
        copy.start()
        outs.append(copy)
    tile_out(tiles - 2).wait()
    tile_out(tiles - 1).wait()
    for copy in outs:
        copy.wait()
    for name in list(started):
        sent(name)


def write(loss_in, slope_in, grad_in, loss_out, slope_out, grad_out, loss, slope, grad, sem):
    pieces = 4
    n = slope.shape[0] // pieces
    moves = [
        (slope_in.at[part], slope.at[part], slope_out.at[part])
        for part in (pl.ds(k * n, n) for k in range(pieces))
    ]
    moves.insert(1, (grad_in, grad, grad_out))
    moves.insert(2, (loss_in, loss, loss_out))
    reads = [
        pltpu.make_async_copy(src, buf, sem.at[0, k]) for k, (src, buf, _) in enumerate(moves)
    ]
    writes = [
        pltpu.make_async_copy(buf, dst, sem.at[1, k]) for k, (_, buf, dst) in enumerate(moves)
    ]
    for copy in reads:
        copy.start()
    for read, copy in zip(reads, writes):
        read.wait()
        copy.start()
    for copy in writes:
        copy.wait()


def shards(queries, passages, positive_ids, hard_ids):
    q_dev, width = queries.shape
    p_dev = passages.shape[0]
    half = p_dev // 2
    moved = half * 3 // 4
    vmem = pltpu.VMEM
    hbm = pl.BlockSpec(memory_space=pl.ANY)
    block = pl.BlockSpec(memory_space=pltpu.VMEM)
    loss, slope, grad, _ = pl.pallas_call(
        kernel,
        out_shape=(
            jax.ShapeDtypeStruct((1,), F32),
            jax.ShapeDtypeStruct((q_dev, width), BF16),
            jax.ShapeDtypeStruct((p_dev, width), BF16),
            jax.ShapeDtypeStruct((8 * p_dev, width), BF16),
        ),
        in_specs=[hbm, hbm, block, block],
        out_specs=(pl.BlockSpec(memory_space=pltpu.SMEM), hbm, hbm, hbm),
        scratch_shapes=[
            vmem((8 * p_dev, width), BF16),
            vmem((8 * p_dev, width), BF16),
            vmem((2 * q_dev, width), BF16),
            vmem((p_dev, 8 * q_dev), F32),
            vmem((8 * p_dev, q_dev), BF16),
            vmem((q_dev, 24 * p_dev), BF16),
            vmem((2 * p_dev, 2 * q_dev), BF16),
            vmem((3, 2 * p_dev, width), BF16),
            vmem((3, 2 * p_dev, width), BF16),
            vmem((2, 2, half, width), BF16),
            vmem((2, 2, p_dev, width), BF16),
            vmem((2, 2, half, width), BF16),
            vmem((2, 2, p_dev, width), BF16),
            vmem((p_dev, width), BF16),
            vmem((p_dev, width), BF16),
            vmem((2, moved, width), BF16),
            vmem((2, moved, width), BF16),
            vmem((2, 8, q_dev), jnp.int32),
            vmem((2, 8, q_dev), F32),
            vmem((8, q_dev), F32),
            vmem((2, 8, q_dev), F32),
            vmem((8, q_dev), F32),
            vmem((8, q_dev), F32),
            vmem((8, q_dev), F32),
            vmem((8, 128), F32),
            vmem((7, 8, 128), F32),
            vmem((7, 8, 128), F32),
            vmem((2, 8 * p_dev, 256), BF16),
            vmem((2, q_dev, 256), BF16),
            pltpu.SemaphoreType.DMA((COPIES,)),
            pltpu.SemaphoreType.DMA((COPIES,)),
            pltpu.SemaphoreType.DMA((7,)),
        ],
        compiler_params=pltpu.CompilerParams(
            collective_id=0, has_side_effects=True, vmem_limit_bytes=63 * 2**20
        ),
        cost_estimate=pl.CostEstimate(
            flops=2 * q_dev * width * 9 * 8 * p_dev,
            bytes_accessed=40 * 2**20,
            transcendentals=2 * 8 * p_dev * q_dev,
        ),
    )(
        queries,
        passages,
        positive_ids.reshape(1, q_dev),
        hard_ids.reshape(1, q_dev),
    )
    loss, slope, grad = pl.pallas_call(
        write,
        out_shape=(
            jax.ShapeDtypeStruct((1,), F32),
            jax.ShapeDtypeStruct(slope.shape, BF16),
            jax.ShapeDtypeStruct(grad.shape, BF16),
        ),
        in_specs=[hbm, hbm, hbm],
        out_specs=(hbm, hbm, hbm),
        scratch_shapes=[
            pltpu.SMEM((1,), F32),
            vmem(slope.shape, BF16),
            vmem(grad.shape, BF16),
            pltpu.SemaphoreType.DMA((2, 6)),
        ],
        compiler_params=pltpu.CompilerParams(vmem_limit_bytes=63 * 2**20),
    )(loss, slope, grad)
    return loss[0], slope, grad


def solution(mesh):
    return jax.shard_map(
        shards,
        mesh=mesh,
        in_specs=(
            P(("blk", "grp"), None),
            P(("blk", "grp"), None),
            P(("blk", "grp")),
            P(("blk", "grp"), None),
        ),
        out_specs=(P(), P(("blk", "grp"), None), P(("blk", "grp"), None)),
        check_vma=False,
    )
```

```python
import functools

import jax
import jax.numpy as jnp
from jax import lax
from jax.experimental import pallas as pl
from jax.experimental.pallas import tpu as pltpu
from jax.sharding import PartitionSpec as P

logit_scaling_coefficient = 20.0
MESH = pl.DeviceIdType.MESH
BF16 = jnp.bfloat16
F32 = jnp.float32
COPIES = 112


def rows(start, size, multiple=64):
    return pl.ds(pl.multiple_of(start, multiple), size)


def kernel(
    q_hbm, p_hbm, pos_ref, hid_ref,
    loss_ref, dq_hbm, dp_hbm, other_hbm,
    lbuf, pbuf, qbuf, s, wt, wall, wht, stage, xrf, xrs, yrf, yrs, zrh, zrl, via, mix,
    ids, hs, hin, w2, top, run, hit, lsum, lsend, lrecv, otile, dqt,
    ssem, rsem, csem,
):
    q_dev, width = q_hbm.shape
    p_dev = p_hbm.shape[0]
    half = p_dev // 2
    scale = logit_scaling_coefficient
    slots = 6 * p_dev
    xs = stage.at[pl.ds(0, slots)]
    ys = stage.at[pl.ds(slots, slots)]

    b = lax.axis_index("blk")
    g = lax.axis_index("grp")
    x, zl = lax.div(b, 2), lax.rem(b, 2)
    zh, y, core = lax.div(g, 8), lax.div(lax.rem(g, 8), 2), lax.rem(g, 2)
    pb = x * 2 + 1 - zl
    px = [lax.rem(x + k, 4) for k in range(4)]
    py = [lax.rem(y + k, 4) for k in range(4)]
    xp = (px[1] * 2 + zl, g)
    xm = (px[3] * 2 + zl, g)
    yp = (b, zh * 8 + py[1] * 2 + core)
    ym = (b, zh * 8 + py[3] * 2 + core)
    p1 = (pb, g)
    p2 = (pb, lax.rem(g + 8, 16))
    sib = (b, zh * 8 + y * 2 + 1 - core)

    number = {}
    started = {}

    def describe(name, src, dst, peer):
        k = number.setdefault(name, len(number))
        return pltpu.make_async_remote_copy(
            src_ref=src, dst_ref=dst, send_sem=ssem.at[k], recv_sem=rsem.at[k],
            device_id=peer, device_id_type=MESH,
        )

    def send(name, src, dst, peer):
        copy = describe(name, src, dst, peer)
        copy.start()
        started[name] = copy

    def sent(name):
        started.pop(name).wait_send()

    def arrived(name, dst):
        describe(name, dst, dst, sib).wait_recv()

    quarter = half // 2
    moved = half * 3 // 4
    halves = [(0, half), (half, half)]
    by_z = [(0, moved), (p_dev - moved, moved)]
    direct = [(moved, half - moved), (half, half - moved)]
    whole = (0, p_dev)

    def lrow(xx, zz, part=whole):
        return lbuf.at[rows((xx * 2 + zz) * p_dev + part[0], part[1], 16)]

    def prow(yy, zz, part=whole):
        return pbuf.at[rows((yy * 2 + zz) * p_dev + part[0], part[1], 16)]

    def orow(yy, zz):
        return other_hbm.at[rows((yy * 2 + zz) * p_dev, p_dev)]

    local = [
        pltpu.make_async_copy(q_hbm, qbuf.at[pl.ds(0, q_dev)], csem.at[0]),
        pltpu.make_async_copy(p_hbm, lrow(x, zl), csem.at[1]),
        pltpu.make_async_copy(p_hbm, prow(y, zh), csem.at[2]),
    ]
    for copy in local:
        copy.start()
    ids[0] = jnp.broadcast_to(hid_ref[...], ids.shape[1:])
    hs[...] = jnp.zeros(hs.shape, F32)
    top[...] = jnp.full(top.shape, -jnp.inf, F32)
    run[...] = jnp.zeros(run.shape, F32)
    hit[...] = jnp.zeros(hit.shape, F32)

    barrier = pltpu.get_barrier_semaphore()
    for peer in (xp, xm, yp, ym, p1, p2, sib):
        pl.semaphore_signal(barrier, inc=1, device_id=peer, device_id_type=MESH)
    pl.semaphore_wait(barrier, 7)

    own = [p_hbm.at[pl.ds(h * half, half)] for h in range(2)]
    quarters = [(k * quarter, quarter) for k in range(4)]

    for k in range(4):
        send(f"z{k}", p_hbm.at[pl.ds(k * quarter, quarter)], lrow(x, zl, quarters[k]), p1)
    for h in range(2):
        r = 1 - h
        send(f"x+o{h}", own[h], lrow(x, zl, halves[h]), xp)
        send(f"x-o{r}", own[r], lrow(x, zl, halves[r]), xm)
        send(f"y+o{h}", own[h], prow(y, zh, halves[h]), yp)
        send(f"y-o{r}", own[r], prow(y, zh, halves[r]), ym)
    send("ids", ids.at[0], ids.at[1], sib)
    send("q", q_hbm, qbuf.at[pl.ds(q_dev, q_dev)], sib)

    def turn(k):
        @pl.loop(0, width // q_dev)
        def _(t):
            cols = rows(t * q_dev, q_dev, q_dev)
            stage[pl.ds(k * slots, q_dev), cols] = qbuf[pl.ds(k * q_dev, q_dev), cols].T

    def score(table, start, k):
        total = jnp.zeros((p_dev, q_dev), F32)
        for t in range(width // q_dev):
            cols = pl.ds(t * q_dev, q_dev)
            total += jnp.dot(
                table[rows(start, p_dev), cols], stage[rows(k * slots, q_dev, 256), cols],
                preferred_element_type=F32,
            )
        return scale * total

    def score_loop(xx, zz):
        c = xx * 2 + zz
        acc = score(lbuf, c * p_dev, 0)
        s[:, rows(c * q_dev, q_dev, q_dev)] = acc
        old = top[0:1]
        peak = jnp.maximum(old, jnp.max(acc, axis=0, keepdims=True))
        total = run[0:1] * jnp.exp(old - peak) + jnp.sum(
            jnp.exp(acc - peak), axis=0, keepdims=True
        )
        row = lax.broadcasted_iota(jnp.int32, acc.shape, 0) + c * p_dev
        top[...] = jnp.broadcast_to(peak, top.shape)
        run[...] = jnp.broadcast_to(total, run.shape)
        hit[...] += jnp.sum(jnp.where(row == pos_ref[...], acc, 0.0), axis=0, keepdims=True)

    def pool_base(yy, zz, cc):
        return (zz * 8 + yy * 2 + cc) * p_dev

    def score_pool(yy, zz):
        slot = yy * 2 + zz
        base = pool_base(yy, zz, core)

        @pl.loop(0, 2)
        def _(k):
            acc = score(pbuf, slot * p_dev, k)
            row = lax.broadcasted_iota(jnp.int32, acc.shape, 0) + base
            named = jnp.where(row == ids[k, 0:1, :], acc, 0.0)
            hs[k] += jnp.sum(named, axis=0, keepdims=True)

    oz, oh = 1 - zl, 1 - zh

    for copy in local:
        copy.wait()
    send("oo", prow(y, zh), orow(y, zh), sib)
    turn(0)

    def pass_x(name, xx, zz, part, peer):
        send(name, lrow(xx, zz, part), lrow(xx, zz, part), peer)

    def pass_y(name, yy, zz, part, peer):
        send(name, prow(yy, zz, part), prow(yy, zz, part), peer)

    def pass_z(k):
        arrived(f"z{k}", lrow(x, oz, quarters[k]))
        send(f"h{k}", lrow(x, oz, quarters[k]), prow(y, zh, quarters[k]), p2)

    pass_z(0)
    pass_z(1)
    arrived("x+o0", lrow(px[3], zl, halves[0]))
    pass_x("x+f", px[3], zl, halves[0], xp)
    arrived("x-o1", lrow(px[1], zl, halves[1]))
    pass_x("x-f", px[1], zl, halves[1], xm)
    arrived("y+o0", prow(py[3], zh, halves[0]))
    pass_y("y+f", py[3], zh, halves[0], yp)
    arrived("y-o1", prow(py[1], zh, halves[1]))
    pass_y("y-f", py[1], zh, halves[1], ym)
    pass_x("x+p0", x, oz, halves[0], xp)
    arrived("ids", ids.at[1])
    arrived("q", qbuf.at[pl.ds(q_dev, q_dev)])
    turn(1)

    pass_z(2)
    arrived("h0", prow(y, oh, quarters[0]))
    arrived("h1", prow(y, oh, quarters[1]))
    pass_y("y+p0", y, oh, halves[0], yp)
    pass_z(3)
    pass_x("x-p1", x, oz, halves[1], xm)
    pass_x("x+p1", x, oz, direct[1], xp)
    pass_x("x-p0", x, oz, direct[0], xm)
    arrived("x+o1", lrow(px[3], zl, halves[1]))
    pass_x("zx1", px[3], zl, by_z[1], p1)
    arrived("x-o0", lrow(px[1], zl, halves[0]))
    pass_x("zx0", px[1], zl, by_z[0], p1)
    arrived("y+o1", prow(py[3], zh, halves[1]))
    send("ty1", prow(py[3], zh, by_z[1]), via.at[1], p2)
    arrived("y-o0", prow(py[1], zh, halves[0]))
    send("ty0", prow(py[1], zh, by_z[0]), via.at[0], p2)
    send("o3", prow(py[3], zh), orow(py[3], zh), sib)
    send("o1", prow(py[1], zh), orow(py[1], zh), sib)
    score_loop(x, zl)
    score_loop(x, oz)
    score_loop(px[3], zl)
    score_loop(px[1], zl)
    arrived("h2", prow(y, oh, quarters[2]))
    arrived("h3", prow(y, oh, quarters[3]))
    pass_y("y-p1", y, oh, halves[1], ym)
    pass_y("y+p1", y, oh, direct[1], yp)
    pass_y("y-p0", y, oh, direct[0], ym)
    send("op", prow(y, oh), orow(y, oh), sib)
    score_pool(y, zh)
    score_pool(py[3], zh)
    score_pool(py[1], zh)
    arrived("x+f", lrow(px[2], zl, halves[0]))
    arrived("x-f", lrow(px[2], zl, halves[1]))
    score_loop(px[2], zl)
    arrived("ty1", via.at[1])
    send("tz1", via.at[1], prow(py[3], oh, by_z[1]), p1)
    score_pool(y, oh)
    arrived("y+f", prow(py[2], zh, halves[0]))
    arrived("y-f", prow(py[2], zh, halves[1]))
    send("o2", prow(py[2], zh), orow(py[2], zh), sib)
    score_pool(py[2], zh)
    arrived("x+p0", lrow(px[3], oz, halves[0]))
    pass_x("x+g", px[3], oz, halves[0], xp)
    arrived("x-p1", lrow(px[1], oz, halves[1]))
    pass_x("x-g", px[1], oz, halves[1], xm)
    arrived("y+p0", prow(py[3], oh, halves[0]))
    pass_y("y+g", py[3], oh, halves[0], yp)
    arrived("y-p1", prow(py[1], oh, halves[1]))
    pass_y("y-g", py[1], oh, halves[1], ym)
    arrived("ty0", via.at[0])
    send("tz0", via.at[0], prow(py[1], oh, by_z[0]), p1)
    arrived("x+p1", lrow(px[3], oz, direct[1]))
    arrived("zx1", lrow(px[3], oz, by_z[1]))
    score_loop(px[3], oz)
    arrived("x-p0", lrow(px[1], oz, direct[0]))
    arrived("zx0", lrow(px[1], oz, by_z[0]))
    score_loop(px[1], oz)
    arrived("y+p1", prow(py[3], oh, direct[1]))
    arrived("tz1", prow(py[3], oh, by_z[1]))
    score_pool(py[3], oh)
    arrived("y-p0", prow(py[1], oh, direct[0]))
    arrived("tz0", prow(py[1], oh, by_z[0]))
    score_pool(py[1], oh)
    arrived("y+g", prow(py[2], oh, halves[0]))
    arrived("y-g", prow(py[2], oh, halves[1]))
    score_pool(py[2], oh)
    send("hs", hs.at[1], hin, sib)
    arrived("x+g", lrow(px[2], oz, halves[0]))
    arrived("x-g", lrow(px[2], oz, halves[1]))
    score_loop(px[2], oz)

    arrived("hs", hin)
    hard = hs[0, 0:1, :] + hin[0:1, :]
    peak = jnp.maximum(top[0:1], hard)
    total = run[0:1] * jnp.exp(top[0:1] - peak) + jnp.exp(hard - peak)
    log_total = peak + jnp.log(total)
    w_hard = jnp.exp(hard - log_total).astype(BF16).astype(F32)
    w2[0] = jnp.broadcast_to(w_hard, w2.shape[1:])
    send("w", w2.at[0], w2.at[1], sib)
    lsum[...] = jnp.broadcast_to(
        jnp.sum(log_total - hit[0:1], axis=1, keepdims=True), lsum.shape
    )
    blocks = s.shape[1] // q_dev

    def weigh(xx, zz):
        c = xx * 2 + zz
        part = s[:, rows(c * q_dev, q_dev, q_dev)]
        row = lax.broadcasted_iota(jnp.int32, part.shape, 0) + c * p_dev
        one = jnp.where(row == pos_ref[...], 1.0, 0.0)
        wt[rows(c * p_dev, p_dev), :] = (jnp.exp(part - log_total) - one).astype(BF16)

    loss_peers = [
        (lax.rem(b + 2 + 4 * lax.rem(x, 2), 8), g),
        (b, zh * 8 + lax.rem(y + 1 + 2 * lax.rem(y, 2), 4) * 2 + core),
        p1,
        p2,
        sib,
        ((3 - x) * 2 + zl, g),
        (b, zh * 8 + (3 - y) * 2 + core),
    ]

    def loss_start(k):
        lsend[k] = lsum[...]
        send(f"l{k}", lsend.at[k], lrecv.at[k], loss_peers[k])

    def loss_finish(k):
        arrived(f"l{k}", lrecv.at[k])
        lsum[...] = lsend[k] + lrecv[k]

    loss_start(0)

    step = 512

    def columns(count):
        return width // 2 if count == p_dev else step

    def loop_part(start, count, store):
        n = columns(count)

        @pl.loop(0, width // n, unroll=min(4, width // n // 2))
        def _(t):
            cols = rows(t * n, n, n)
            store(cols, scale * jnp.dot(
                wt[rows(start, count), :], qbuf[pl.ds(0, q_dev), cols],
                preferred_element_type=F32,
            ))

    def pool_weights(yy, zz, at):
        base = pool_base(yy, zz, core)
        for k in range(2):
            row = lax.broadcasted_iota(jnp.int32, (p_dev, q_dev), 0) + base
            wht[at:at + p_dev, k * q_dev:(k + 1) * q_dev] = jnp.where(
                row == ids[k, 0:1, :], w2[k, 0:1, :], 0.0
            ).astype(BF16)

    def pool_part(count, store):
        n = columns(count)

        @pl.loop(0, width // n, unroll=min(4, width // n // 2))
        def _(t):
            cols = rows(t * n, n, n)
            store(cols, scale * jnp.dot(
                wht[pl.ds(0, count), :], qbuf[:, cols], preferred_element_type=F32
            ))

    z_of = {"x": (oz, zl), "y": (oh, zh)}
    axes = {"x": (xs, xrf, xrs, xp, xm), "y": (ys, yrf, yrs, yp, ym)}

    def piece(a, slot, role, part):
        start = (slot * 2 + z_of[a][role]) * p_dev + part[0]
        return axes[a][0].at[rows(start, part[1], 16)]

    def at(part):
        return pl.ds(part[0], part[1])

    def add_to(dst, *terms):
        @pl.loop(0, width // step, unroll=2)
        def _(t):
            cols = rows(t * step, step, step)
            total = dst[:, cols].astype(F32)
            for term in terms:
                total += term[:, cols].astype(F32)
            dst[:, cols] = total.astype(BF16)

    def send_far(a, role):
        _, rf, _, plus, minus = axes[a]
        send(f"{a}+s2{role}", piece(a, 2, role, halves[0]), rf.at[0, role], plus)
        send(f"{a}-s2{role}", piece(a, 2, role, halves[1]), rf.at[1, role], minus)

    def send_near(a, role):
        _, _, rs, plus, minus = axes[a]
        send(f"{a}+s1{role}", piece(a, 0, role, direct[1]), rs.at[0, role, at(direct[1])], plus)
        send(f"{a}-s1{role}", piece(a, 1, role, direct[0]), rs.at[1, role, at(direct[0])], minus)

    def send_mix_x():
        send("mx1", piece("x", 0, 0, by_z[1]), mix.at[1], p1)
        send("mx0", piece("x", 1, 0, by_z[0]), mix.at[0], p1)

    hop = [xrs.at[1, 0, at(by_z[0])], xrs.at[0, 0, at(by_z[1])]]
    end = [yrs.at[1, 0, at(by_z[0])], yrs.at[0, 0, at(by_z[1])]]

    def send_mix_y():
        send("my1", piece("y", 0, 0, by_z[1]), hop[1], p2)
        send("my0", piece("y", 1, 0, by_z[0]), hop[0], p2)

    def pass_mix_y(h):
        arrived(f"my{h}", hop[h])
        send(f"mz{h}", hop[h], end[h], p1)

    def send_mixed(a, h):
        _, _, rs, plus, minus = axes[a]
        term = mix.at[h] if a == "x" else end[h]
        arrived(f"mx{h}" if a == "x" else f"mz{h}", term)
        mine = piece(a, 1 - h, 1, by_z[h])
        add_to(mine, term)
        send(f"{a}m{h}", mine, rs.at[1 - h, 1, at(by_z[h])], plus if h else minus)

    def send_sum(a, role):
        _, rf, rs, plus, minus = axes[a]
        for d, (sign, peer) in enumerate((("+", plus), ("-", minus))):
            arrived(f"{a}{sign}s2{role}", rf.at[d, role])
            mine = piece(a, d, role, halves[d])
            add_to(mine, rf.at[d, role])
            send(f"{a}{sign}s0{role}", mine, rs.at[d, role, at(halves[d])], peer)

    def sums_arrived(a, role):
        rs = axes[a][2]
        for d, sign in enumerate("+-"):
            arrived(f"{a}{sign}s1{role}", rs.at[d, role, at(direct[1 - d])])
            if role:
                arrived(f"{a}m{1 - d}", rs.at[d, role, at(by_z[1 - d])])
            arrived(f"{a}{sign}s0{role}", rs.at[d, role, at(halves[d])])

    def store_to(ref):
        def store(cols, value):
            ref[:, cols] = value.astype(BF16)
        return store

    place = {1: 0, 3: 1, 2: 2}

    def x_part(k, role):
        zz = z_of["x"][role]
        weigh(px[k], zz)
        loop_part((px[k] * 2 + zz) * p_dev, p_dev, store_to(piece("x", place[k], role, whole)))

    def y_part(k, role):
        pool_weights(py[k], z_of["y"][role], 0)
        pool_part(p_dev, store_to(piece("y", place[k], role, whole)))

    x_part(2, 0)
    send_far("x", 0)
    loss_finish(0)
    loss_start(1)
    arrived("w", w2.at[1])
    y_part(2, 0)
    loss_finish(1)
    send_far("y", 0)
    loss_start(2)
    send("o4", prow(py[3], oh), orow(py[3], oh), sib)
    send("o5", prow(py[1], oh), orow(py[1], oh), sib)
    send("o6", prow(py[2], oh), orow(py[2], oh), sib)
    x_part(1, 0)
    x_part(3, 0)
    send_near("x", 0)
    loss_finish(2)
    loss_start(3)
    send_mix_x()
    y_part(1, 0)
    y_part(3, 0)
    send_near("y", 0)
    loss_finish(3)
    send_mix_y()
    loss_start(4)
    for k in (2, 1, 3):
        x_part(k, 1)
    weigh(x, 0)
    weigh(x, 1)
    send_sum("x", 0)
    y_part(2, 1)
    send_sum("y", 0)
    loss_finish(4)
    loss_start(5)
    send_far("x", 1)
    send_far("y", 1)
    y_part(1, 1)
    y_part(3, 1)
    send_near("x", 1)
    send_near("y", 1)

    for a in "xy":
        sent(f"{a}+s20")
        sent(f"{a}-s20")

    hand_x = xs.at[rows((4 + oz) * p_dev, p_dev)]
    hand_y = ys.at[rows((4 + oh) * p_dev, p_dev)]

    def split(first, value):
        low, high = value[:p_dev], value[p_dev:]
        return jnp.where(first, low, high), jnp.where(first, high, low)

    def store_x(cols, value):
        mine, handed = split(zl == 0, value)
        s[:, cols] = mine
        hand_x[:, cols] = handed.astype(BF16)

    def store_y(cols, value):
        mine, handed = split(zh == 0, value)
        s[:, cols] += mine
        hand_y[:, cols] = handed.astype(BF16)

    loop_part(x * 2 * p_dev, 2 * p_dev, store_x)
    pool_weights(y, 0, 0)
    pool_weights(y, 1, p_dev)
    pool_part(2 * p_dev, store_y)
    pass_mix_y(1)
    send_mixed("x", 1)
    send_mixed("x", 0)

    for c in range(blocks):
        wall[:, c * p_dev:(c + 1) * p_dev] = (
            wt[c * p_dev:(c + 1) * p_dev, :].astype(F32).T.astype(BF16)
        )
    loop_rows = blocks * p_dev

    @pl.loop(0, q_dev // 128)
    def _(n):
        part = rows(n * 128, 128, 128)
        names = jnp.broadcast_to(ids[0, 0:1, part].astype(F32), (128, 128)).T
        values = jnp.broadcast_to(w2[0, 0:1, part], (128, 128)).T
        lane = lax.broadcasted_iota(jnp.int32, (128, 128), 1)
        for k in range(2):
            cc = core if k == 0 else 1 - core
            for slot in range(8):
                base = pool_base(slot // 2, slot % 2, cc)
                at = loop_rows + (k * 8 + slot) * p_dev
                wall[part, at:at + p_dev] = jnp.where(
                    names == (lane + base).astype(F32), values, 0.0
                ).astype(BF16)

    arrived("oo", orow(y, zh))
    arrived("o3", orow(py[3], zh))
    arrived("o1", orow(py[1], zh))
    arrived("op", orow(y, oh))
    arrived("o2", orow(py[2], zh))
    arrived("o4", orow(py[3], oh))
    arrived("o5", orow(py[1], oh))
    arrived("o6", orow(py[2], oh))

    tile = dqt.shape[2]
    tiles = width // tile
    pool_rows = pbuf.shape[0]

    def tile_in(t):
        k = lax.rem(t, 2)
        return pltpu.make_async_copy(
            other_hbm.at[:, rows(t * tile, tile, tile)], otile.at[k], csem.at[k]
        )

    def tile_out(t):
        k = lax.rem(t, 2)
        return pltpu.make_async_copy(
            dqt.at[k], dq_hbm.at[:, rows(t * tile, tile, tile)], csem.at[2 + k]
        )

    tile_in(0).start()

    def query_slope(first, last):
        @pl.loop(first, last)
        def _(t):
            k = lax.rem(t, 2)

            @pl.when(t + 1 < tiles)
            def _():
                tile_in(t + 1).start()

            @pl.when(t >= 2)
            def _():
                tile_out(t - 2).wait()

            cols = rows(t * tile, tile, tile)
            tile_in(t).wait()
            acc = jnp.dot(
                wall[:, 0:loop_rows], lbuf[:, cols], preferred_element_type=F32
            )
            acc += jnp.dot(
                wall[:, loop_rows:loop_rows + pool_rows], pbuf[:, cols],
                preferred_element_type=F32,
            )
            acc += jnp.dot(
                wall[:, loop_rows + pool_rows:], otile[k], preferred_element_type=F32
            )
            dqt[k] = (scale * acc).astype(BF16)
            tile_out(t).start()

    query_slope(0, tiles // 4)
    pass_mix_y(0)
    loss_finish(5)
    loss_start(6)
    query_slope(tiles // 4, tiles * 3 // 8)

    parts = [pl.ds(0, moved), pl.ds(moved, p_dev - 2 * moved), pl.ds(p_dev - moved, moved)]
    signs = [(0,), (0, 1), (1,)]
    sums_arrived("y", 0)
    for k, part in enumerate(parts):
        add_to(hand_y.at[part], *(yrs.at[d, 0, part] for d in signs[k]))
        send(f"zh{k}", hand_y.at[part], zrh.at[part], p2)
    send_mixed("y", 1)
    query_slope(tiles * 3 // 8, tiles * 5 // 8)
    sums_arrived("x", 0)
    send_mixed("y", 0)
    send_sum("x", 1)
    send_sum("y", 1)
    for k, part in enumerate(parts):
        arrived(f"zh{k}", zrh.at[part])
        add_to(hand_x.at[part], zrh.at[part], *(xrs.at[d, 0, part] for d in signs[k]))
        send(f"zl{k}", hand_x.at[part], zrl.at[part], p1)
        query_slope(tiles * (10 + 2 * k) // 16, tiles * (12 + 2 * k) // 16)
    loss_finish(6)
    loss_ref[0] = jnp.max(lsum[...]) / (q_dev * lax.axis_size("blk") * lax.axis_size("grp"))

    sums_arrived("x", 1)
    for h, part in enumerate(parts):
        arrived(f"zl{h}", zrl.at[part])

        @pl.loop(0, width // step, unroll=2)
        def _(t):
            cols = rows(t * step, step, step)
            s[part, cols] += (
                xrs[0, 1, part, cols].astype(F32)
                + xrs[1, 1, part, cols].astype(F32)
                + zrl[part, cols].astype(F32)
            )

    sums_arrived("y", 1)
    sent("y+s21")
    sent("y-s21")
    result = ys.at[rows((4 + zh) * p_dev, p_dev)]
    outs = []
    for h, part in enumerate(parts):
        @pl.loop(0, width // step, unroll=2)
        def _(t):
            cols = rows(t * step, step, step)
            result[part, cols] = (
                s[part, cols]
                + yrs[0, 1, part, cols].astype(F32)
                + yrs[1, 1, part, cols].astype(F32)
            ).astype(BF16)

        copy = pltpu.make_async_copy(result.at[part], dp_hbm.at[part], csem.at[4 + h])
        copy.start()
        outs.append(copy)
    tile_out(tiles - 2).wait()
    tile_out(tiles - 1).wait()
    for copy in outs:
        copy.wait()
    for name in list(started):
        sent(name)


def write(loss_in, slope_in, grad_in, loss_out, slope_out, grad_out, loss, slope, grad, sem):
    pieces = 4
    n = slope.shape[0] // pieces
    moves = [
        (slope_in.at[part], slope.at[part], slope_out.at[part])
        for part in (pl.ds(k * n, n) for k in range(pieces))
    ]
    moves.insert(1, (grad_in, grad, grad_out))
    moves.append((loss_in, loss, loss_out))
    reads = [
        pltpu.make_async_copy(src, buf, sem.at[0, k]) for k, (src, buf, _) in enumerate(moves)
    ]
    writes = [
        pltpu.make_async_copy(buf, dst, sem.at[1, k]) for k, (_, buf, dst) in enumerate(moves)
    ]
    for copy in reads:
        copy.start()
    for read, copy in zip(reads, writes):
        read.wait()
        copy.start()
    for copy in writes:
        copy.wait()


def shards(queries, passages, positive_ids, hard_ids):
    q_dev, width = queries.shape
    p_dev = passages.shape[0]
    half = p_dev // 2
    moved = half * 3 // 4
    vmem = pltpu.VMEM
    hbm = pl.BlockSpec(memory_space=pl.ANY)
    block = pl.BlockSpec(memory_space=pltpu.VMEM)
    loss, slope, grad, _ = pl.pallas_call(
        kernel,
        out_shape=(
            jax.ShapeDtypeStruct((1,), F32),
            jax.ShapeDtypeStruct((q_dev, width), BF16),
            jax.ShapeDtypeStruct((p_dev, width), BF16),
            jax.ShapeDtypeStruct((8 * p_dev, width), BF16),
        ),
        in_specs=[hbm, hbm, block, block],
        out_specs=(pl.BlockSpec(memory_space=pltpu.SMEM), hbm, hbm, hbm),
        scratch_shapes=[
            vmem((8 * p_dev, width), BF16),
            vmem((8 * p_dev, width), BF16),
            vmem((2 * q_dev, width), BF16),
            vmem((p_dev, 8 * q_dev), F32),
            vmem((8 * p_dev, q_dev), BF16),
            vmem((q_dev, 24 * p_dev), BF16),
            vmem((2 * p_dev, 2 * q_dev), BF16),
            vmem((12 * p_dev, width), BF16),
            vmem((2, 2, half, width), BF16),
            vmem((2, 2, p_dev, width), BF16),
            vmem((2, 2, half, width), BF16),
            vmem((2, 2, p_dev, width), BF16),
            vmem((p_dev, width), BF16),
            vmem((p_dev, width), BF16),
            vmem((2, moved, width), BF16),
            vmem((2, moved, width), BF16),
            vmem((2, 8, q_dev), jnp.int32),
            vmem((2, 8, q_dev), F32),
            vmem((8, q_dev), F32),
            vmem((2, 8, q_dev), F32),
            vmem((8, q_dev), F32),
            vmem((8, q_dev), F32),
            vmem((8, q_dev), F32),
            vmem((8, 128), F32),
            vmem((7, 8, 128), F32),
            vmem((7, 8, 128), F32),
            vmem((2, 8 * p_dev, 256), BF16),
            vmem((2, q_dev, 256), BF16),
            pltpu.SemaphoreType.DMA((COPIES,)),
            pltpu.SemaphoreType.DMA((COPIES,)),
            pltpu.SemaphoreType.DMA((7,)),
        ],
        compiler_params=pltpu.CompilerParams(
            collective_id=0, has_side_effects=True, vmem_limit_bytes=63 * 2**20
        ),
        cost_estimate=pl.CostEstimate(
            flops=2 * q_dev * width * 9 * 8 * p_dev,
            bytes_accessed=40 * 2**20,
            transcendentals=2 * 8 * p_dev * q_dev,
        ),
    )(
        queries,
        passages,
        positive_ids.reshape(1, q_dev),
        hard_ids.reshape(1, q_dev),
    )
    loss, slope, grad = pl.pallas_call(
        write,
        out_shape=(
            jax.ShapeDtypeStruct((1,), F32),
            jax.ShapeDtypeStruct(slope.shape, BF16),
            jax.ShapeDtypeStruct(grad.shape, BF16),
        ),
        in_specs=[hbm, hbm, hbm],
        out_specs=(hbm, hbm, hbm),
        scratch_shapes=[
            pltpu.SMEM((1,), F32),
            vmem(slope.shape, BF16),
            vmem(grad.shape, BF16),
            pltpu.SemaphoreType.DMA((2, 6)),
        ],
        compiler_params=pltpu.CompilerParams(vmem_limit_bytes=63 * 2**20),
    )(loss, slope, grad)
    return loss[0], slope, grad


def solution(mesh):
    return jax.shard_map(
        shards,
        mesh=mesh,
        in_specs=(
            P(("blk", "grp"), None),
            P(("blk", "grp"), None),
            P(("blk", "grp")),
            P(("blk", "grp"), None),
        ),
        out_specs=(P(), P(("blk", "grp"), None), P(("blk", "grp"), None)),
        check_vma=False,
    )
```

```python
import functools

import jax
import jax.numpy as jnp
from jax import lax
from jax.experimental import pallas as pl
from jax.experimental.pallas import tpu as pltpu
from jax.sharding import PartitionSpec as P

logit_scaling_coefficient = 20.0
MESH = pl.DeviceIdType.MESH
BF16 = jnp.bfloat16
F32 = jnp.float32
COPIES = 112


def rows(start, size, multiple=64):
    return pl.ds(pl.multiple_of(start, multiple), size)


def kernel(
    q_hbm, p_hbm, pos_ref, hid_ref,
    loss_ref, dq_hbm, dp_hbm, other_hbm,
    lbuf, pbuf, qbuf, s, wt, wall, wht, stage, xrf, xrs, yrf, yrs, zrh, zrl, via, mix,
    ids, hs, hin, w2, top, run, hit, lsum, lsend, lrecv, otile, dqt,
    ssem, rsem, csem,
):
    q_dev, width = q_hbm.shape
    p_dev = p_hbm.shape[0]
    half = p_dev // 2
    scale = logit_scaling_coefficient
    slots = 6 * p_dev
    xs = stage.at[pl.ds(0, slots)]
    ys = stage.at[pl.ds(slots, slots)]

    b = lax.axis_index("blk")
    g = lax.axis_index("grp")
    x, zl = lax.div(b, 2), lax.rem(b, 2)
    zh, y, core = lax.div(g, 8), lax.div(lax.rem(g, 8), 2), lax.rem(g, 2)
    pb = x * 2 + 1 - zl
    px = [lax.rem(x + k, 4) for k in range(4)]
    py = [lax.rem(y + k, 4) for k in range(4)]
    xp = (px[1] * 2 + zl, g)
    xm = (px[3] * 2 + zl, g)
    yp = (b, zh * 8 + py[1] * 2 + core)
    ym = (b, zh * 8 + py[3] * 2 + core)
    p1 = (pb, g)
    p2 = (pb, lax.rem(g + 8, 16))
    sib = (b, zh * 8 + y * 2 + 1 - core)

    number = {}
    started = {}

    def describe(name, src, dst, peer):
        k = number.setdefault(name, len(number))
        return pltpu.make_async_remote_copy(
            src_ref=src, dst_ref=dst, send_sem=ssem.at[k], recv_sem=rsem.at[k],
            device_id=peer, device_id_type=MESH,
        )

    def send(name, src, dst, peer):
        copy = describe(name, src, dst, peer)
        copy.start()
        started[name] = copy

    def sent(name):
        started.pop(name).wait_send()

    def arrived(name, dst):
        describe(name, dst, dst, sib).wait_recv()

    quarter = half // 2
    moved = half * 3 // 4
    halves = [(0, half), (half, half)]
    by_z = [(0, moved), (p_dev - moved, moved)]
    direct = [(moved, half - moved), (half, half - moved)]
    whole = (0, p_dev)

    def lrow(xx, zz, part=whole):
        return lbuf.at[rows((xx * 2 + zz) * p_dev + part[0], part[1], 16)]

    def prow(yy, zz, part=whole):
        return pbuf.at[rows((yy * 2 + zz) * p_dev + part[0], part[1], 16)]

    def orow(yy, zz):
        return other_hbm.at[rows((yy * 2 + zz) * p_dev, p_dev)]

    local = [
        pltpu.make_async_copy(q_hbm, qbuf.at[pl.ds(0, q_dev)], csem.at[0]),
        pltpu.make_async_copy(p_hbm, lrow(x, zl), csem.at[1]),
        pltpu.make_async_copy(p_hbm, prow(y, zh), csem.at[2]),
    ]
    for copy in local:
        copy.start()
    ids[0] = jnp.broadcast_to(hid_ref[...], ids.shape[1:])
    hs[...] = jnp.zeros(hs.shape, F32)
    top[...] = jnp.full(top.shape, -jnp.inf, F32)
    run[...] = jnp.zeros(run.shape, F32)
    hit[...] = jnp.zeros(hit.shape, F32)

    barrier = pltpu.get_barrier_semaphore()
    for peer in (xp, xm, yp, ym, p1, p2, sib):
        pl.semaphore_signal(barrier, inc=1, device_id=peer, device_id_type=MESH)
    pl.semaphore_wait(barrier, 7)

    own = [p_hbm.at[pl.ds(h * half, half)] for h in range(2)]
    quarters = [(k * quarter, quarter) for k in range(4)]

    for k in range(4):
        send(f"z{k}", p_hbm.at[pl.ds(k * quarter, quarter)], lrow(x, zl, quarters[k]), p1)
    for h in range(2):
        r = 1 - h
        send(f"x+o{h}", own[h], lrow(x, zl, halves[h]), xp)
        send(f"x-o{r}", own[r], lrow(x, zl, halves[r]), xm)
        send(f"y+o{h}", own[h], prow(y, zh, halves[h]), yp)
        send(f"y-o{r}", own[r], prow(y, zh, halves[r]), ym)
    send("ids", ids.at[0], ids.at[1], sib)
    send("q", q_hbm, qbuf.at[pl.ds(q_dev, q_dev)], sib)

    def turn(k):
        @pl.loop(0, width // q_dev)
        def _(t):
            cols = rows(t * q_dev, q_dev, q_dev)
            stage[pl.ds(k * slots, q_dev), cols] = qbuf[pl.ds(k * q_dev, q_dev), cols].T

    def score(table, start, k):
        total = jnp.zeros((p_dev, q_dev), F32)
        for t in range(width // q_dev):
            cols = pl.ds(t * q_dev, q_dev)
            total += jnp.dot(
                table[rows(start, p_dev), cols], stage[rows(k * slots, q_dev, 256), cols],
                preferred_element_type=F32,
            )
        return scale * total

    def score_loop(xx, zz):
        c = xx * 2 + zz
        acc = score(lbuf, c * p_dev, 0)
        s[:, rows(c * q_dev, q_dev, q_dev)] = acc
        old = top[0:1]
        peak = jnp.maximum(old, jnp.max(acc, axis=0, keepdims=True))
        total = run[0:1] * jnp.exp(old - peak) + jnp.sum(
            jnp.exp(acc - peak), axis=0, keepdims=True
        )
        row = lax.broadcasted_iota(jnp.int32, acc.shape, 0) + c * p_dev
        top[...] = jnp.broadcast_to(peak, top.shape)
        run[...] = jnp.broadcast_to(total, run.shape)
        hit[...] += jnp.sum(jnp.where(row == pos_ref[...], acc, 0.0), axis=0, keepdims=True)

    def pool_base(yy, zz, cc):
        return (zz * 8 + yy * 2 + cc) * p_dev

    def score_pool(yy, zz):
        slot = yy * 2 + zz
        base = pool_base(yy, zz, core)

        @pl.loop(0, 2)
        def _(k):
            acc = score(pbuf, slot * p_dev, k)
            row = lax.broadcasted_iota(jnp.int32, acc.shape, 0) + base
            named = jnp.where(row == ids[k, 0:1, :], acc, 0.0)
            hs[k] += jnp.sum(named, axis=0, keepdims=True)

    oz, oh = 1 - zl, 1 - zh

    for copy in local:
        copy.wait()
    send("oo", prow(y, zh), orow(y, zh), sib)
    turn(0)

    def pass_x(name, xx, zz, part, peer):
        send(name, lrow(xx, zz, part), lrow(xx, zz, part), peer)

    def pass_y(name, yy, zz, part, peer):
        send(name, prow(yy, zz, part), prow(yy, zz, part), peer)

    def pass_z(k):
        arrived(f"z{k}", lrow(x, oz, quarters[k]))
        send(f"h{k}", lrow(x, oz, quarters[k]), prow(y, zh, quarters[k]), p2)

    pass_z(0)
    pass_z(1)
    arrived("x+o0", lrow(px[3], zl, halves[0]))
    pass_x("x+f", px[3], zl, halves[0], xp)
    arrived("x-o1", lrow(px[1], zl, halves[1]))
    pass_x("x-f", px[1], zl, halves[1], xm)
    arrived("y+o0", prow(py[3], zh, halves[0]))
    pass_y("y+f", py[3], zh, halves[0], yp)
    arrived("y-o1", prow(py[1], zh, halves[1]))
    pass_y("y-f", py[1], zh, halves[1], ym)
    pass_x("x+p0", x, oz, halves[0], xp)
    arrived("ids", ids.at[1])
    arrived("q", qbuf.at[pl.ds(q_dev, q_dev)])
    turn(1)

    pass_z(2)
    arrived("h0", prow(y, oh, quarters[0]))
    arrived("h1", prow(y, oh, quarters[1]))
    pass_y("y+p0", y, oh, halves[0], yp)
    pass_z(3)
    pass_x("x-p1", x, oz, halves[1], xm)
    pass_x("x+p1", x, oz, direct[1], xp)
    pass_x("x-p0", x, oz, direct[0], xm)
    arrived("x+o1", lrow(px[3], zl, halves[1]))
    pass_x("zx1", px[3], zl, by_z[1], p1)
    arrived("x-o0", lrow(px[1], zl, halves[0]))
    pass_x("zx0", px[1], zl, by_z[0], p1)
    arrived("y+o1", prow(py[3], zh, halves[1]))
    send("ty1", prow(py[3], zh, by_z[1]), via.at[1], p2)
    arrived("y-o0", prow(py[1], zh, halves[0]))
    send("ty0", prow(py[1], zh, by_z[0]), via.at[0], p2)
    send("o3", prow(py[3], zh), orow(py[3], zh), sib)
    send("o1", prow(py[1], zh), orow(py[1], zh), sib)
    score_loop(x, zl)
    score_loop(x, oz)
    score_loop(px[3], zl)
    score_loop(px[1], zl)
    arrived("h2", prow(y, oh, quarters[2]))
    arrived("h3", prow(y, oh, quarters[3]))
    pass_y("y-p1", y, oh, halves[1], ym)
    pass_y("y+p1", y, oh, direct[1], yp)
    pass_y("y-p0", y, oh, direct[0], ym)
    send("op", prow(y, oh), orow(y, oh), sib)
    score_pool(y, zh)
    score_pool(py[3], zh)
    score_pool(py[1], zh)
    arrived("x+f", lrow(px[2], zl, halves[0]))
    arrived("x-f", lrow(px[2], zl, halves[1]))
    score_loop(px[2], zl)
    arrived("ty1", via.at[1])
    send("tz1", via.at[1], prow(py[3], oh, by_z[1]), p1)
    score_pool(y, oh)
    arrived("y+f", prow(py[2], zh, halves[0]))
    arrived("y-f", prow(py[2], zh, halves[1]))
    send("o2", prow(py[2], zh), orow(py[2], zh), sib)
    score_pool(py[2], zh)
    arrived("x+p0", lrow(px[3], oz, halves[0]))
    pass_x("x+g", px[3], oz, halves[0], xp)
    arrived("x-p1", lrow(px[1], oz, halves[1]))
    pass_x("x-g", px[1], oz, halves[1], xm)
    arrived("y+p0", prow(py[3], oh, halves[0]))
    pass_y("y+g", py[3], oh, halves[0], yp)
    arrived("y-p1", prow(py[1], oh, halves[1]))
    pass_y("y-g", py[1], oh, halves[1], ym)
    arrived("ty0", via.at[0])
    send("tz0", via.at[0], prow(py[1], oh, by_z[0]), p1)
    arrived("x+p1", lrow(px[3], oz, direct[1]))
    arrived("zx1", lrow(px[3], oz, by_z[1]))
    score_loop(px[3], oz)
    arrived("x-p0", lrow(px[1], oz, direct[0]))
    arrived("zx0", lrow(px[1], oz, by_z[0]))
    score_loop(px[1], oz)
    arrived("y+p1", prow(py[3], oh, direct[1]))
    arrived("tz1", prow(py[3], oh, by_z[1]))
    score_pool(py[3], oh)
    arrived("y-p0", prow(py[1], oh, direct[0]))
    arrived("tz0", prow(py[1], oh, by_z[0]))
    score_pool(py[1], oh)
    arrived("y+g", prow(py[2], oh, halves[0]))
    arrived("y-g", prow(py[2], oh, halves[1]))
    score_pool(py[2], oh)
    send("hs", hs.at[1], hin, sib)
    arrived("x+g", lrow(px[2], oz, halves[0]))
    arrived("x-g", lrow(px[2], oz, halves[1]))
    score_loop(px[2], oz)

    arrived("hs", hin)
    hard = hs[0, 0:1, :] + hin[0:1, :]
    peak = jnp.maximum(top[0:1], hard)
    total = run[0:1] * jnp.exp(top[0:1] - peak) + jnp.exp(hard - peak)
    log_total = peak + jnp.log(total)
    w_hard = jnp.exp(hard - log_total).astype(BF16).astype(F32)
    w2[0] = jnp.broadcast_to(w_hard, w2.shape[1:])
    send("w", w2.at[0], w2.at[1], sib)
    lsum[...] = jnp.broadcast_to(
        jnp.sum(log_total - hit[0:1], axis=1, keepdims=True), lsum.shape
    )
    blocks = s.shape[1] // q_dev

    def weigh(xx, zz):
        c = xx * 2 + zz
        part = s[:, rows(c * q_dev, q_dev, q_dev)]
        row = lax.broadcasted_iota(jnp.int32, part.shape, 0) + c * p_dev
        one = jnp.where(row == pos_ref[...], 1.0, 0.0)
        wt[rows(c * p_dev, p_dev), :] = (jnp.exp(part - log_total) - one).astype(BF16)

    loss_peers = [
        (lax.rem(b + 2 + 4 * lax.rem(x, 2), 8), g),
        (b, zh * 8 + lax.rem(y + 1 + 2 * lax.rem(y, 2), 4) * 2 + core),
        p1,
        p2,
        sib,
        ((3 - x) * 2 + zl, g),
        (b, zh * 8 + (3 - y) * 2 + core),
    ]

    def loss_start(k):
        lsend[k] = lsum[...]
        send(f"l{k}", lsend.at[k], lrecv.at[k], loss_peers[k])

    def loss_finish(k):
        arrived(f"l{k}", lrecv.at[k])
        lsum[...] = lsend[k] + lrecv[k]

    loss_start(0)

    step = 512

    def columns(count):
        return width // 2 if count == p_dev else step

    def loop_part(start, count, store):
        n = columns(count)

        @pl.loop(0, width // n, unroll=min(4, width // n // 2))
        def _(t):
            cols = rows(t * n, n, n)
            store(cols, scale * jnp.dot(
                wt[rows(start, count), :], qbuf[pl.ds(0, q_dev), cols],
                preferred_element_type=F32,
            ))

    def pool_weights(yy, zz, at):
        base = pool_base(yy, zz, core)
        for k in range(2):
            row = lax.broadcasted_iota(jnp.int32, (p_dev, q_dev), 0) + base
            wht[at:at + p_dev, k * q_dev:(k + 1) * q_dev] = jnp.where(
                row == ids[k, 0:1, :], w2[k, 0:1, :], 0.0
            ).astype(BF16)

    def pool_part(count, store):
        n = columns(count)

        @pl.loop(0, width // n, unroll=min(4, width // n // 2))
        def _(t):
            cols = rows(t * n, n, n)
            store(cols, scale * jnp.dot(
                wht[pl.ds(0, count), :], qbuf[:, cols], preferred_element_type=F32
            ))

    z_of = {"x": (oz, zl), "y": (oh, zh)}
    axes = {"x": (xs, xrf, xrs, xp, xm), "y": (ys, yrf, yrs, yp, ym)}

    def piece(a, slot, role, part):
        start = (slot * 2 + z_of[a][role]) * p_dev + part[0]
        return axes[a][0].at[rows(start, part[1], 16)]

    def at(part):
        return pl.ds(part[0], part[1])

    def add_to(dst, *terms):
        @pl.loop(0, width // step, unroll=2)
        def _(t):
            cols = rows(t * step, step, step)
            total = dst[:, cols].astype(F32)
            for term in terms:
                total += term[:, cols].astype(F32)
            dst[:, cols] = total.astype(BF16)

    def send_far(a, role):
        _, rf, _, plus, minus = axes[a]
        send(f"{a}+s2{role}", piece(a, 2, role, halves[0]), rf.at[0, role], plus)
        send(f"{a}-s2{role}", piece(a, 2, role, halves[1]), rf.at[1, role], minus)

    def send_near(a, role):
        _, _, rs, plus, minus = axes[a]
        send(f"{a}+s1{role}", piece(a, 0, role, direct[1]), rs.at[0, role, at(direct[1])], plus)
        send(f"{a}-s1{role}", piece(a, 1, role, direct[0]), rs.at[1, role, at(direct[0])], minus)

    def send_mix_x():
        send("mx1", piece("x", 0, 0, by_z[1]), mix.at[1], p1)
        send("mx0", piece("x", 1, 0, by_z[0]), mix.at[0], p1)

    hop = [xrs.at[1, 0, at(by_z[0])], xrs.at[0, 0, at(by_z[1])]]
    end = [yrs.at[1, 0, at(by_z[0])], yrs.at[0, 0, at(by_z[1])]]

    def send_mix_y():
        send("my1", piece("y", 0, 0, by_z[1]), hop[1], p2)
        send("my0", piece("y", 1, 0, by_z[0]), hop[0], p2)

    def pass_mix_y(h):
        arrived(f"my{h}", hop[h])
        send(f"mz{h}", hop[h], end[h], p1)

    def send_mixed(a, h):
        _, _, rs, plus, minus = axes[a]
        term = mix.at[h] if a == "x" else end[h]
        arrived(f"mx{h}" if a == "x" else f"mz{h}", term)
        mine = piece(a, 1 - h, 1, by_z[h])
        add_to(mine, term)
        send(f"{a}m{h}", mine, rs.at[1 - h, 1, at(by_z[h])], plus if h else minus)

    def send_sum(a, role):
        _, rf, rs, plus, minus = axes[a]
        for d, (sign, peer) in enumerate((("+", plus), ("-", minus))):
            arrived(f"{a}{sign}s2{role}", rf.at[d, role])
            mine = piece(a, d, role, halves[d])
            add_to(mine, rf.at[d, role])
            send(f"{a}{sign}s0{role}", mine, rs.at[d, role, at(halves[d])], peer)

    def sums_arrived(a, role):
        rs = axes[a][2]
        for d, sign in enumerate("+-"):
            arrived(f"{a}{sign}s1{role}", rs.at[d, role, at(direct[1 - d])])
            if role:
                arrived(f"{a}m{1 - d}", rs.at[d, role, at(by_z[1 - d])])
            arrived(f"{a}{sign}s0{role}", rs.at[d, role, at(halves[d])])

    def store_to(ref):
        def store(cols, value):
            ref[:, cols] = value.astype(BF16)
        return store

    place = {1: 0, 3: 1, 2: 2}

    def x_part(k, role):
        zz = z_of["x"][role]
        weigh(px[k], zz)
        loop_part((px[k] * 2 + zz) * p_dev, p_dev, store_to(piece("x", place[k], role, whole)))

    def y_part(k, role):
        pool_weights(py[k], z_of["y"][role], 0)
        pool_part(p_dev, store_to(piece("y", place[k], role, whole)))

    x_part(2, 0)
    send_far("x", 0)
    loss_finish(0)
    loss_start(1)
    arrived("w", w2.at[1])
    y_part(2, 0)
    loss_finish(1)
    send_far("y", 0)
    loss_start(2)
    send("o4", prow(py[3], oh), orow(py[3], oh), sib)
    send("o5", prow(py[1], oh), orow(py[1], oh), sib)
    send("o6", prow(py[2], oh), orow(py[2], oh), sib)
    x_part(1, 0)
    x_part(3, 0)
    send_near("x", 0)
    loss_finish(2)
    loss_start(3)
    send_mix_x()
    y_part(1, 0)
    y_part(3, 0)
    send_near("y", 0)
    loss_finish(3)
    send_mix_y()
    loss_start(4)
    for k in (2, 1, 3):
        x_part(k, 1)
    weigh(x, 0)
    weigh(x, 1)
    send_sum("x", 0)
    y_part(2, 1)
    send_sum("y", 0)
    loss_finish(4)
    loss_start(5)
    send_far("x", 1)
    send_far("y", 1)
    y_part(1, 1)
    y_part(3, 1)
    send_near("x", 1)
    send_near("y", 1)

    for a in "xy":
        sent(f"{a}+s20")
        sent(f"{a}-s20")

    hand_x = xs.at[rows((4 + oz) * p_dev, p_dev)]
    hand_y = ys.at[rows((4 + oh) * p_dev, p_dev)]

    def split(first, value):
        low, high = value[:p_dev], value[p_dev:]
        return jnp.where(first, low, high), jnp.where(first, high, low)

    def store_x(cols, value):
        mine, handed = split(zl == 0, value)
        s[:, cols] = mine
        hand_x[:, cols] = handed.astype(BF16)

    def store_y(cols, value):
        mine, handed = split(zh == 0, value)
        s[:, cols] += mine
        hand_y[:, cols] = handed.astype(BF16)

    loop_part(x * 2 * p_dev, 2 * p_dev, store_x)
    pool_weights(y, 0, 0)
    pool_weights(y, 1, p_dev)
    pool_part(2 * p_dev, store_y)
    pass_mix_y(1)
    send_mixed("x", 1)
    send_mixed("x", 0)

    for c in range(blocks):
        wall[:, c * p_dev:(c + 1) * p_dev] = (
            wt[c * p_dev:(c + 1) * p_dev, :].astype(F32).T.astype(BF16)
        )
    loop_rows = blocks * p_dev

    @pl.loop(0, q_dev // 128)
    def _(n):
        part = rows(n * 128, 128, 128)
        names = jnp.broadcast_to(ids[0, 0:1, part].astype(F32), (128, 128)).T
        values = jnp.broadcast_to(w2[0, 0:1, part], (128, 128)).T
        lane = lax.broadcasted_iota(jnp.int32, (128, 128), 1)
        for k in range(2):
            cc = core if k == 0 else 1 - core
            for slot in range(8):
                base = pool_base(slot // 2, slot % 2, cc)
                at = loop_rows + (k * 8 + slot) * p_dev
                wall[part, at:at + p_dev] = jnp.where(
                    names == (lane + base).astype(F32), values, 0.0
                ).astype(BF16)

    arrived("oo", orow(y, zh))
    arrived("o3", orow(py[3], zh))
    arrived("o1", orow(py[1], zh))
    arrived("op", orow(y, oh))
    arrived("o2", orow(py[2], zh))
    arrived("o4", orow(py[3], oh))
    arrived("o5", orow(py[1], oh))
    arrived("o6", orow(py[2], oh))

    tile = dqt.shape[2]
    tiles = width // tile
    pool_rows = pbuf.shape[0]

    def tile_in(t):
        k = lax.rem(t, 2)
        return pltpu.make_async_copy(
            other_hbm.at[:, rows(t * tile, tile, tile)], otile.at[k], csem.at[k]
        )

    def tile_out(t):
        k = lax.rem(t, 2)
        return pltpu.make_async_copy(
            dqt.at[k], dq_hbm.at[:, rows(t * tile, tile, tile)], csem.at[2 + k]
        )

    tile_in(0).start()

    def query_slope(first, last):
        @pl.loop(first, last)
        def _(t):
            k = lax.rem(t, 2)

            @pl.when(t + 1 < tiles)
            def _():
                tile_in(t + 1).start()

            @pl.when(t >= 2)
            def _():
                tile_out(t - 2).wait()

            cols = rows(t * tile, tile, tile)
            tile_in(t).wait()
            acc = jnp.dot(
                wall[:, 0:loop_rows], lbuf[:, cols], preferred_element_type=F32
            )
            acc += jnp.dot(
                wall[:, loop_rows:loop_rows + pool_rows], pbuf[:, cols],
                preferred_element_type=F32,
            )
            acc += jnp.dot(
                wall[:, loop_rows + pool_rows:], otile[k], preferred_element_type=F32
            )
            dqt[k] = (scale * acc).astype(BF16)
            tile_out(t).start()

    query_slope(0, tiles // 4)
    pass_mix_y(0)
    loss_finish(5)
    loss_start(6)
    query_slope(tiles // 4, tiles * 3 // 8)

    parts = [pl.ds(0, moved), pl.ds(moved, p_dev - 2 * moved), pl.ds(p_dev - moved, moved)]
    signs = [(0,), (0, 1), (1,)]
    sums_arrived("y", 0)
    for k, part in enumerate(parts):
        add_to(hand_y.at[part], *(yrs.at[d, 0, part] for d in signs[k]))
        send(f"zh{k}", hand_y.at[part], zrh.at[part], p2)
    send_mixed("y", 1)
    query_slope(tiles * 3 // 8, tiles * 5 // 8)
    sums_arrived("x", 0)
    send_mixed("y", 0)
    send_sum("x", 1)
    send_sum("y", 1)
    for k, part in enumerate(parts):
        arrived(f"zh{k}", zrh.at[part])
        add_to(hand_x.at[part], zrh.at[part], *(xrs.at[d, 0, part] for d in signs[k]))
        send(f"zl{k}", hand_x.at[part], zrl.at[part], p1)
        query_slope(tiles * (10 + 2 * k) // 16, tiles * (12 + 2 * k) // 16)
    loss_finish(6)
    loss_ref[0] = jnp.max(lsum[...]) / (q_dev * lax.axis_size("blk") * lax.axis_size("grp"))

    sums_arrived("x", 1)
    for h, part in enumerate(parts):
        arrived(f"zl{h}", zrl.at[part])

        @pl.loop(0, width // step, unroll=2)
        def _(t):
            cols = rows(t * step, step, step)
            s[part, cols] += (
                xrs[0, 1, part, cols].astype(F32)
                + xrs[1, 1, part, cols].astype(F32)
                + zrl[part, cols].astype(F32)
            )

    sums_arrived("y", 1)
    sent("y+s21")
    sent("y-s21")
    result = ys.at[rows((4 + zh) * p_dev, p_dev)]
    outs = []
    for h, part in enumerate(parts):
        @pl.loop(0, width // step, unroll=2)
        def _(t):
            cols = rows(t * step, step, step)
            result[part, cols] = (
                s[part, cols]
                + yrs[0, 1, part, cols].astype(F32)
                + yrs[1, 1, part, cols].astype(F32)
            ).astype(BF16)

        copy = pltpu.make_async_copy(result.at[part], dp_hbm.at[part], csem.at[4 + h])
        copy.start()
        outs.append(copy)
    tile_out(tiles - 2).wait()
    tile_out(tiles - 1).wait()
    for copy in outs:
        copy.wait()
    for name in list(started):
        sent(name)


def write(loss_in, slope_in, grad_in, loss_out, slope_out, grad_out, loss, slope, grad, sem):
    pieces = 4
    n = slope.shape[0] // pieces
    moves = [
        (slope_in.at[part], slope.at[part], slope_out.at[part])
        for part in (pl.ds(k * n, n) for k in range(pieces))
    ]
    moves.insert(0, (grad_in, grad, grad_out))
    moves.insert(0, (loss_in, loss, loss_out))
    reads = [
        pltpu.make_async_copy(src, buf, sem.at[0, k]) for k, (src, buf, _) in enumerate(moves)
    ]
    writes = [
        pltpu.make_async_copy(buf, dst, sem.at[1, k]) for k, (_, buf, dst) in enumerate(moves)
    ]
    for copy in reads:
        copy.start()
    for k in (1, 2, 0, *range(3, len(moves))):
        reads[k].wait()
        writes[k].start()
    for copy in writes:
        copy.wait()


def shards(queries, passages, positive_ids, hard_ids):
    q_dev, width = queries.shape
    p_dev = passages.shape[0]
    half = p_dev // 2
    moved = half * 3 // 4
    vmem = pltpu.VMEM
    hbm = pl.BlockSpec(memory_space=pl.ANY)
    block = pl.BlockSpec(memory_space=pltpu.VMEM)
    loss, slope, grad, _ = pl.pallas_call(
        kernel,
        out_shape=(
            jax.ShapeDtypeStruct((1,), F32),
            jax.ShapeDtypeStruct((q_dev, width), BF16),
            jax.ShapeDtypeStruct((p_dev, width), BF16),
            jax.ShapeDtypeStruct((8 * p_dev, width), BF16),
        ),
        in_specs=[hbm, hbm, block, block],
        out_specs=(pl.BlockSpec(memory_space=pltpu.SMEM), hbm, hbm, hbm),
        scratch_shapes=[
            vmem((8 * p_dev, width), BF16),
            vmem((8 * p_dev, width), BF16),
            vmem((2 * q_dev, width), BF16),
            vmem((p_dev, 8 * q_dev), F32),
            vmem((8 * p_dev, q_dev), BF16),
            vmem((q_dev, 24 * p_dev), BF16),
            vmem((2 * p_dev, 2 * q_dev), BF16),
            vmem((12 * p_dev, width), BF16),
            vmem((2, 2, half, width), BF16),
            vmem((2, 2, p_dev, width), BF16),
            vmem((2, 2, half, width), BF16),
            vmem((2, 2, p_dev, width), BF16),
            vmem((p_dev, width), BF16),
            vmem((p_dev, width), BF16),
            vmem((2, moved, width), BF16),
            vmem((2, moved, width), BF16),
            vmem((2, 8, q_dev), jnp.int32),
            vmem((2, 8, q_dev), F32),
            vmem((8, q_dev), F32),
            vmem((2, 8, q_dev), F32),
            vmem((8, q_dev), F32),
            vmem((8, q_dev), F32),
            vmem((8, q_dev), F32),
            vmem((8, 128), F32),
            vmem((7, 8, 128), F32),
            vmem((7, 8, 128), F32),
            vmem((2, 8 * p_dev, 256), BF16),
            vmem((2, q_dev, 256), BF16),
            pltpu.SemaphoreType.DMA((COPIES,)),
            pltpu.SemaphoreType.DMA((COPIES,)),
            pltpu.SemaphoreType.DMA((7,)),
        ],
        compiler_params=pltpu.CompilerParams(
            collective_id=0, has_side_effects=True, vmem_limit_bytes=63 * 2**20
        ),
        cost_estimate=pl.CostEstimate(
            flops=2 * q_dev * width * 9 * 8 * p_dev,
            bytes_accessed=40 * 2**20,
            transcendentals=2 * 8 * p_dev * q_dev,
        ),
    )(
        queries,
        passages,
        positive_ids.reshape(1, q_dev),
        hard_ids.reshape(1, q_dev),
    )
    loss, slope, grad = pl.pallas_call(
        write,
        out_shape=(
            jax.ShapeDtypeStruct((1,), F32),
            jax.ShapeDtypeStruct(slope.shape, BF16),
            jax.ShapeDtypeStruct(grad.shape, BF16),
        ),
        in_specs=[hbm, hbm, hbm],
        out_specs=(hbm, hbm, hbm),
        scratch_shapes=[
            pltpu.SMEM((1,), F32),
            vmem(slope.shape, BF16),
            vmem(grad.shape, BF16),
            pltpu.SemaphoreType.DMA((2, 6)),
        ],
        compiler_params=pltpu.CompilerParams(vmem_limit_bytes=63 * 2**20),
    )(loss, slope, grad)
    return loss[0], slope, grad


def solution(mesh):
    return jax.shard_map(
        shards,
        mesh=mesh,
        in_specs=(
            P(("blk", "grp"), None),
            P(("blk", "grp"), None),
            P(("blk", "grp")),
            P(("blk", "grp"), None),
        ),
        out_specs=(P(), P(("blk", "grp"), None), P(("blk", "grp"), None)),
        check_vma=False,
    )
```
